32 devices in a mesh: frames: 8 (over z, x), mp: 4 (over y, core).
Axes of the slice: x: 2, y: 2, z: 4, core: 2. Of those that a mesh axis runs over, the one named last changes fastest.
Arguments:
- video_tokens: bfloat16 [8, 256, 1024], P('frames', 'mp'), may hold values from -64 to 64
- grad_output: bfloat16 [8, 256, 1024], P('frames', 'mp'), may hold values from -6 to 6
- spatial_qkv: bfloat16 [3, 1024, 1024], P(None, None, 'mp'), may hold values from -1 to 1
- spatial_out: bfloat16 [1024, 1024], P('mp'), may hold values from -0.1875 to 0.1875
- temporal_qkv: bfloat16 [3, 1024, 1024], P(None, None, 'mp'), may hold values from -1 to 1
- temporal_out: bfloat16 [1024, 1024], P('mp'), may hold values from -0.1875 to 0.1875
- clip_frames: int32 [4], replicated, may hold values from 1 to 4, 8 in all
Outputs:
- grad_tokens: bfloat16 [8, 256, 1024], P('frames', 'mp')
- grad_spatial_qkv: float32 [3, 1024, 1024], P(None, 'frames', 'mp')
- grad_spatial_out: float32 [1024, 1024], P('mp', 'frames')
- grad_temporal_qkv: float32 [3, 1024, 1024], P(None, 'frames', 'mp')
- grad_temporal_out: float32 [1024, 1024], P('mp', 'frames')
The draws below stay inside these ranges and needn't reach their ends.
Inputs may be any that keep to these rules, and one draw needn't show every extreme that they name: `clip_frames`: 4 clip lengths that sum to 8; the longest is exactly 4.
All inputs are finite; a program needn't handle non-finite values.
Results may differ from the reference program's by a relative error of at most 0.015.
Values may be sent and summed in bfloat16 or wider, within the bound.
No kernel may reach another device: no remote copies, remote signals or barrier semaphores. Data moves between devices by JAX's collectives and lax.ppermute only.
A program may use at most 128 MiB of HBM per device.

```python
import math
import jax
import jax.numpy as jnp
import numpy as np
from jax import lax

D = 1024
HEADS = 16
HD = 64
P_SIZE = 256
FRAMES = 8
CLIPS = 4
CLIP_MOST = 4


def draw_video_tokens(key, part):
    key = jax.random.fold_in(key, 7)
    k_base, k_cols, k_rows = jax.random.split(key, 3)
    full_shape = (FRAMES, P_SIZE, D)
    base_draw = jnp.clip(jax.random.normal(k_base, full_shape, jnp.float32), -4.0, 4.0)
    col_scale = 0.3 * jnp.exp(jax.random.uniform(k_cols, (D,), jnp.float32, 0.0, math.log(10.0)))
    row_scale = 0.5 * jnp.exp(jax.random.uniform(k_rows, (FRAMES, P_SIZE, 1), jnp.float32, 0.0, math.log(10.0)))
    return (base_draw * col_scale * row_scale).astype(jnp.bfloat16)


def projection_draw(key):
    k_one, k_two, k_three = jax.random.split(key, 3)
    spread = D ** (-0.5)
    queries = jnp.clip(jax.random.normal(k_one, (D, D), jnp.float32), -4.0, 4.0) * spread
    own_keys = jnp.clip(jax.random.normal(k_two, (D, D), jnp.float32), -4.0, 4.0) * spread
    values_part = jnp.clip(jax.random.normal(k_three, (D, D), jnp.float32), -4.0, 4.0) * spread
    keys_part = own_keys
    return jnp.clip(jnp.stack([queries, keys_part, values_part]), -1.0, 1.0).astype(jnp.bfloat16)


def draw_spatial_qkv(key, part):
    key = jax.random.fold_in(key, 19)
    return projection_draw(key)


def draw_temporal_qkv(key, part):
    key = jax.random.fold_in(key, 23)
    return projection_draw(key)


def strengthened(entries, rng, source, target, shards_of, factor):
    def block_of(position):
        return (jnp.arange(entries.shape[position]) // (entries.shape[position] // shards_of)).reshape((-1,) + (1,) * (entries.ndim - 1 - position))

    near = jax.random.permutation(rng, shards_of)[block_of(target)]
    other_side = (block_of(target) + shards_of // 2) % shards_of
    return jnp.where((block_of(source) == near) | (block_of(source) == other_side), factor * entries, entries)


def steps_of(key, shape, cuts, smallest, high):
    def one(axis_at, shards_of):
        heights = jax.random.uniform(jax.random.fold_in(jax.random.fold_in(key, 6), axis_at), (shards_of,), jnp.float32, smallest / len(cuts), high / len(cuts))
        return jnp.repeat(jnp.exp(heights), shape[axis_at] // shards_of).reshape((-1,) + (1,) * (len(shape) - axis_at - 1))

    factor_of = one(*cuts[0])
    for cut in cuts[1:]:
        factor_of = factor_of * one(*cut)
    return factor_of


def profile(amount, total, most, lean):
    portions = [(1 << 20) // math.isqrt(standing ** lean) + 1 for standing in range(2, amount + 1)]
    surplus, holding = total - most - (amount - 1), [1] * (amount - 1)
    while surplus > 0:
        candidates = [i for i in range(amount - 1) if holding[i] < most]
        whole, left = sum([portions[i] for i in candidates]), surplus
        for i in candidates:
            addition = min(most - holding[i], max(1, left * portions[i] // whole), surplus)
            holding[i] = holding[i] + addition
            surplus = surplus - addition
    return np.array([most] + holding)


def uneven_parts(own_key, number_of, total, most, slope):
    if number_of == 2:
        one = jax.random.randint(own_key, (), max(1, total - most), min(most, total - 1) + 1)
        return jnp.stack([one, total - one])
    tallies = jnp.asarray(profile(number_of, total, most, slope), jnp.int32)
    pairs = (number_of - 1) // 2
    source_of, taker = tallies[1:1 + 2 * pairs:2], tallies[2:2 + 2 * pairs:2]
    slack = jnp.minimum(source_of - 1, most - taker)
    moved = jax.random.randint(jax.random.fold_in(own_key, 1), (pairs,), 0, 1 << 20) % (slack + 1)
    tallies = tallies.at[1:1 + 2 * pairs:2].set(source_of - moved).at[2:2 + 2 * pairs:2].set(taker + moved)
    return tallies[jax.random.permutation(jax.random.fold_in(own_key, 2), number_of)]


def gaussian(key, dims, scale, most, cuts=(), held_as=jnp.bfloat16):
    entries = scale * jax.random.normal(key, dims, jnp.float32)
    if cuts:
        entries = entries * steps_of(key, dims, cuts, -0.22, 0.18)
    return jnp.clip(entries, -most, most).astype(held_as)


def noise_with(rng, shape, deviation, limit, shards, heavy, kind=jnp.bfloat16):
    values = deviation * jax.random.normal(rng, shape, jnp.float32)
    if shards:
        values = values * steps_of(rng, shape, shards, -0.22, 0.18)
    return jnp.clip(strengthened(values, jax.random.fold_in(rng, 3), *heavy), -limit, limit).astype(kind)


def setup_inputs(seed: int = 0) -> dict:
    keys = jax.random.split(jax.random.key(seed), 8)
    return {
        "video_tokens": draw_video_tokens(jax.random.fold_in(keys[7], 71), 0),
        "grad_output": noise_with(keys[1], (FRAMES, P_SIZE, D), 1.0, 6.0, ((0, 8), (1, 4)), (0, 2, 8, 2.0)),
        "spatial_qkv": draw_spatial_qkv(jax.random.fold_in(keys[7], 71), 0),
        "spatial_out": gaussian(keys[3], (D, D), D ** -0.5, 0.1875, ((0, 4),)),
        "temporal_qkv": draw_temporal_qkv(jax.random.fold_in(keys[7], 71), 0),
        "temporal_out": gaussian(keys[5], (D, D), D ** -0.5, 0.1875, ((0, 4),)),
        "clip_frames": uneven_parts(keys[6], CLIPS, FRAMES, CLIP_MOST, 2).astype(jnp.int32),
    }


EPS = 1e-06
NEGATIVE = -1e+30

def normed(values_in):
    inv_rms = lax.rsqrt(lax.optimization_barrier(jnp.mean(values_in * values_in, -1, keepdims=True)) + EPS)
    return ((values_in * inv_rms).astype(jnp.bfloat16), inv_rms)

def norm_back(values_in, inv_rms, upstream):
    return inv_rms * (upstream - values_in * (inv_rms * inv_rms) * lax.optimization_barrier(jnp.mean(upstream * values_in, -1, keepdims=True)))

def rounded(tensor):
    return lax.optimization_barrier(tensor.astype(jnp.bfloat16)).astype(jnp.float32)

def probs_of(queries, keys_in, mask_bias):
    scores = jnp.einsum('bld,bmd->blm', queries.astype(jnp.float32), keys_in.astype(jnp.float32))
    scores = scores * queries.shape[-1] ** (-0.5) + mask_bias
    scores = scores - lax.optimization_barrier(jnp.max(scores, -1, keepdims=True))
    expo = jnp.exp(scores)
    return expo / lax.optimization_barrier(jnp.sum(expo, -1, keepdims=True))

def attend(queries, keys_in, values_in, mask_bias):
    probs_f = probs_of(queries, keys_in, mask_bias)
    result = jnp.einsum('blm,bmd->bld', rounded(probs_f), values_in.astype(jnp.float32))
    return result.astype(jnp.bfloat16)

def attend_back(queries, keys_in, values_in, mask_bias, upstream):
    probs_f = probs_of(queries, keys_in, mask_bias)
    up_float = upstream.astype(jnp.float32)
    d_values = jnp.einsum('blm,bld->bmd', rounded(probs_f), up_float)
    d_probs = jnp.einsum('bld,bmd->blm', up_float, values_in.astype(jnp.float32))
    row_delta = lax.optimization_barrier(jnp.sum(probs_f * d_probs, -1, keepdims=True))
    d_scores = rounded(probs_f * (d_probs - row_delta) * queries.shape[-1] ** (-0.5))
    d_queries = jnp.einsum('blm,bmd->bld', d_scores, keys_in.astype(jnp.float32))
    d_keys = jnp.einsum('blm,bld->bmd', d_scores, queries.astype(jnp.float32))
    return (d_queries.astype(jnp.bfloat16), d_keys.astype(jnp.bfloat16), d_values.astype(jnp.bfloat16))

def reference(video_tokens, grad_output, spatial_qkv, spatial_out, temporal_qkv, temporal_out, clip_frames):
    frame_total, patch_total, model_width = video_tokens.shape
    token_total = frame_total * patch_total

    def spatial_heads(flat):
        return flat.reshape(frame_total, patch_total, HEADS, HD).transpose(2, 0, 1, 3)

    def spatial_merge(stacked):
        return stacked.transpose(1, 2, 0, 3).reshape(token_total, model_width)

    def temporal_heads(flat):
        return flat.reshape(frame_total, patch_total, HEADS, HD).transpose(2, 1, 0, 3)

    def temporal_merge(stacked):
        return stacked.transpose(2, 1, 0, 3).reshape(token_total, model_width)

    def project(flat, weights):
        return jnp.stack([jnp.dot(flat, weights[which], preferred_element_type=jnp.float32) for which in range(3)]).astype(jnp.bfloat16)

    def back_project(grads, weights):
        joined = grads.transpose(1, 0, 2).reshape(token_total, 3 * model_width)
        stacked_w = weights.transpose(0, 2, 1).reshape(3 * model_width, model_width)
        return jnp.dot(joined, stacked_w, preferred_element_type=jnp.float32)

    def weight_grads(flat, grads):
        return jnp.stack([jnp.dot(flat.T, grads[which], preferred_element_type=jnp.float32) for which in range(3)])
    no_mask = jnp.zeros((patch_total, patch_total), jnp.float32)
    clip_ends = jnp.cumsum(clip_frames).astype(jnp.int32)
    frame_ids = jnp.arange(frame_total, dtype=jnp.int32)
    clip_ids = lax.optimization_barrier(jnp.sum((frame_ids[:, None] >= clip_ends[None, :]).astype(jnp.int32), axis=1))
    clip_mask = jnp.where(clip_ids[:, None] == clip_ids[None, :], 0.0, NEGATIVE).astype(jnp.float32)
    x_float = video_tokens.astype(jnp.float32)
    normed_x, inv_x = normed(x_float)
    normed_x_flat = normed_x.reshape(token_total, model_width)
    qkv_s = project(normed_x_flat, spatial_qkv)
    heads_s = (spatial_heads(qkv_s[0]), spatial_heads(qkv_s[1]), spatial_heads(qkv_s[2]))
    attn_s = spatial_merge(lax.map(lambda trio: attend(trio[0], trio[1], trio[2], no_mask), heads_s))
    hidden = x_float + jnp.dot(attn_s, spatial_out, preferred_element_type=jnp.float32).reshape(video_tokens.shape)
    normed_h, inv_h = normed(hidden)
    normed_h_flat = normed_h.reshape(token_total, model_width)
    qkv_t = project(normed_h_flat, temporal_qkv)
    heads_t = (temporal_heads(qkv_t[0]), temporal_heads(qkv_t[1]), temporal_heads(qkv_t[2]))
    attn_t = temporal_merge(lax.map(lambda trio: attend(trio[0], trio[1], trio[2], clip_mask), heads_t))
    dy_flat = grad_output.reshape(token_total, model_width)
    grad_temporal_out = jnp.dot(attn_t.T, dy_flat, preferred_element_type=jnp.float32)
    d_attn_t = jnp.dot(dy_flat, temporal_out.T, preferred_element_type=jnp.float32).astype(jnp.bfloat16)
    back_t = lax.map(lambda quad: attend_back(quad[0], quad[1], quad[2], clip_mask, quad[3]), heads_t + (temporal_heads(d_attn_t),))
    d_qkv_t = jnp.stack([temporal_merge(piece) for piece in back_t])
    grad_temporal_qkv = weight_grads(normed_h_flat, d_qkv_t)
    d_normed_h = back_project(d_qkv_t, temporal_qkv).reshape(video_tokens.shape)
    d_hidden = grad_output.astype(jnp.float32) + norm_back(hidden, inv_h, d_normed_h)
    d_hidden_b = d_hidden.astype(jnp.bfloat16).reshape(token_total, model_width)
    grad_spatial_out = jnp.dot(attn_s.T, d_hidden_b, preferred_element_type=jnp.float32)
    d_attn_s = jnp.dot(d_hidden_b, spatial_out.T, preferred_element_type=jnp.float32).astype(jnp.bfloat16)
    back_s = lax.map(lambda quad: attend_back(quad[0], quad[1], quad[2], no_mask, quad[3]), heads_s + (spatial_heads(d_attn_s),))
    d_qkv_s = jnp.stack([spatial_merge(piece) for piece in back_s])
    grad_spatial_qkv = weight_grads(normed_x_flat, d_qkv_s)
    d_normed_x = back_project(d_qkv_s, spatial_qkv).reshape(video_tokens.shape)
    grad_tokens = (d_hidden + norm_back(x_float, inv_x, d_normed_x)).astype(jnp.bfloat16)
    return (grad_tokens, grad_spatial_qkv, grad_spatial_out, grad_temporal_qkv, grad_temporal_out)
```

```python
import jax
import jax.numpy as jnp
from jax import lax
from jax.experimental import pallas as pl
from jax.experimental.pallas import tpu as pltpu
from jax.sharding import PartitionSpec as P

HD = 64
EPS = 1e-06
NEGATIVE = -1e30
BF = jnp.bfloat16
F32 = jnp.float32
VMEM_LIMIT = 20 * 1024 * 1024


def mm(a, b, ca, cb):
    return lax.dot_general(a, b, (((ca,), (cb,)), ((), ())), preferred_element_type=F32)


def shape(dims, dtype=BF):
    return jax.ShapeDtypeStruct(dims, dtype)


def flipped(index, by, bits):
    total = index
    for b in range(bits):
        if (by >> b) & 1:
            total = total + (1 << b) * (1 - 2 * ((index // (1 << b)) % 2))
    return total


def swap(value, axis, by):
    size = lax.axis_size(axis)
    return lax.ppermute(value, axis, [(i, i ^ by) for i in range(size)])


class Kernel:
    def __init__(self, get, outs, put, smem, scratch, sems, early):
        self.get, self.outs, self.put = get, outs, put
        self.smem, self.scratch, self.sems, self.early = smem, scratch, sems, early

    def copy(self, src, dst):
        made = pltpu.make_async_copy(src, dst, self.sems.pop(0))
        made.start()
        return made


def run(
    body, ins, where, outs, out_where, smem=(), scratch=(), copies=0, early=None, flops=1000
):
    n, k, s = len(ins), len(outs), len(smem)
    staged_in = [i for i in range(n) if where[i] in "ha"]
    staged_out = [i for i in range(k) if out_where[i] in "ha"]

    def wrapped(*refs):
        refs = list(refs)

        def take(count):
            part = refs[:count]
            del refs[:count]
            return part

        scalars, src, dst = take(s), take(n), take(k)
        in_bufs, out_bufs = take(len(staged_in)), take(len(staged_out))
        in_sem, out_sem, own_sem = take(3)
        loads, stores = {}, {}
        results = list(dst)
        for at, i in enumerate(staged_out):
            results[i] = out_bufs[at]
        held = {i: in_bufs[at] for at, i in enumerate(staged_in)}
        waited = set()

        def get(i):
            if i not in held:
                return src[i]
            if i not in waited:
                loads[i].wait()
                waited.add(i)
            return held[i]

        def put(i):
            if i in staged_out and i not in stores:
                at = staged_out.index(i)
                stores[i] = pltpu.make_async_copy(out_bufs[at], dst[i], out_sem.at[at])
                stores[i].start()

        sems = [own_sem.at[i] for i in range(copies)]
        tools = Kernel(get, results, put, scalars, refs, sems, None)
        if early is not None:
            tools.early = early(tools)
        for at, i in enumerate(staged_in):
            loads[i] = pltpu.make_async_copy(src[i], in_bufs[at], in_sem.at[at])
            loads[i].start()
        body(tools)
        for i in staged_in:
            get(i)
        for i in range(k):
            put(i)
        for copy in stores.values():
            copy.wait()

    specs = {"v": pltpu.VMEM, "h": pltpu.HBM, "a": pl.ANY, "n": pl.ANY, "x": pltpu.HBM}
    specs = {key: pl.BlockSpec(memory_space=space) for key, space in specs.items()}
    buffers = [pltpu.VMEM(ins[i].shape, ins[i].dtype) for i in staged_in]
    buffers += [pltpu.VMEM(outs[i].shape, outs[i].dtype) for i in staged_out]
    ins = [
        pltpu.with_memory_space_constraint(a, pltpu.HBM) if w in "hx" else a
        for a, w in zip(ins, where)
    ]
    return pl.pallas_call(
        wrapped,
        out_shape=tuple(
            pltpu.HBM(o.shape, o.dtype) if w in "hx" else o for o, w in zip(outs, out_where)
        ),
        in_specs=[pl.BlockSpec(memory_space=pltpu.SMEM)] * s
        + [specs[w] for w in where],
        out_specs=tuple(specs[w] for w in out_where),
        scratch_shapes=buffers
        + [pltpu.SemaphoreType.DMA((max(1, c),)) for c in (len(staged_in), len(staged_out), copies)]
        + list(scratch),
        compiler_params=pltpu.CompilerParams(vmem_limit_bytes=VMEM_LIMIT),
        cost_estimate=pl.CostEstimate(flops=flops, bytes_accessed=1000, transcendentals=0),
    )(*smem, *ins)


def inv_rms(v):
    return lax.rsqrt(jnp.mean(v * v, -1, keepdims=True) + EPS)


SCALE = HD ** (-0.5)
assert SCALE == 0.125


def head_mask(width, head, scale=1.0):
    lane = lax.broadcasted_iota(jnp.int32, (1, width), 1)
    mask = ((lane >= head * HD) & (lane < (head + 1) * HD)).astype(F32)
    return (mask * scale).astype(BF)


def probs_of(q, k, head, allowed):
    scores = mm(q * head_mask(q.shape[1], head, SCALE), k, 1, 1)
    if allowed is not None:
        scores = jnp.where(allowed, scores, NEGATIVE)
    expo = jnp.exp(scores - jnp.max(scores, -1, keepdims=True))
    return expo * (1.0 / jnp.sum(expo, -1, keepdims=True))


def attend(q, k, v, heads):
    total = jnp.zeros(q.shape, F32)
    for h in range(heads):
        mask = head_mask(q.shape[1], h)
        probs = probs_of(q, k, h, None)
        total += mm(probs.astype(BF), v * mask, 1, 0)
    return total.astype(BF)


def attend_back(q, k, v, up, heads, probs_at, with_out):
    zero = jnp.zeros(q.shape, F32)
    out, dq, dk, dv = zero, zero, zero, zero
    v_scaled = v * jnp.full((1, 1), SCALE, BF)
    for h in range(heads):
        mask = head_mask(q.shape[1], h)
        up_head = up * mask
        probs = probs_at(h)
        probs_b = probs.astype(BF)
        if with_out:
            out += mm(probs_b, v * mask, 1, 0)
        dv += mm(probs_b, up_head, 0, 0)
        dp = mm(up_head, v_scaled, 1, 1)
        delta = jnp.sum(probs * dp, -1, keepdims=True)
        ds = (probs * (dp - delta)).astype(BF)
        dq += mm(ds, k * mask, 1, 0)
        dk += mm(ds, q * mask, 0, 0)
    return dq.astype(BF), dk.astype(BF), dv.astype(BF), out.astype(BF)


def row_order(rows, outer, middle, inner):
    to = lax.broadcasted_iota(jnp.int32, (rows, 1), 0)
    at = lax.broadcasted_iota(jnp.int32, (1, rows), 1)
    o, m, i = to // (middle * inner), (to // inner) % middle, to % inner
    return (at == (m * outer + o) * inner + i).astype(F32).astype(BF)


def own_block(r, rows):
    start = flipped(lax.axis_index("mp"), r, 2) * rows
    return pl.ds(pl.multiple_of(start, rows), rows)


def joined(x, grad):
    rows, dim = x.shape

    def body(t):
        for i in range(2):
            t.outs[0][:, i * dim : (i + 1) * dim] = t.get(i)[...]

    return run(body, (x, grad), "hh", (shape((rows, 2 * dim)),), "v")[0]


def spatial_forward(parts, weights, heads, groups):
    own_rows, dim = parts[0].shape
    mp, width = len(parts), weights.shape[2]
    rows = mp * own_rows

    def body(t):
        for r in (*range(1, mp), 0):
            xf = t.get(r)[...].astype(F32)
            t.outs[0][own_block(r, own_rows), :] = (xf * inv_rms(xf)).astype(BF)
        nx = t.outs[0][...]
        t.put(0)
        w = t.get(mp)
        q, k, v = [mm(nx, w[j], 1, 0).astype(BF) for j in range(3)]
        for j, part in enumerate((q, k, v)):
            t.outs[1][j] = part
        t.put(1)
        attn = attend(q, k, v, heads)
        order = row_order(rows, groups, mp, rows // (groups * mp))
        t.outs[2][...] = mm(order, attn, 1, 0).astype(BF)

    outs = (shape((rows, dim)), shape((3, rows, width)), shape((rows, width)))
    return run(
        body, (*parts, weights), "h" + "v" * (mp - 1) + "h", outs, "hhv"
    )


def owner_rows(xg, w_to):
    own_rows, mp = xg[0].shape[0], len(xg)
    rows, (width, dim) = mp * own_rows, w_to.shape

    def body(t):
        for r in range(mp):
            at = own_block(r, own_rows)
            t.outs[0][at, :] = t.get(r)[:, :dim]
            t.outs[1][at, :] = t.get(r)[:, dim:]
        t.outs[2][...] = mm(t.outs[1][...], t.get(mp)[...], 1, 1).astype(BF)

    whole = shape((rows, dim))
    return run(
        body, (*xg, w_to), "v" * mp + "h", (whole, whole, shape((rows, width))), "vvv"
    )


SENT = ((1, 3, 5, 7), (2, 3, 6, 7))
KEPT = ((0, 2, 4, 6), (0, 1, 4, 5))
OUT_SENT, OUT_KEPT = (1, 5, 3, 7), (0, 4, 2, 6)


def chunk_of(flat, right, r, groups):
    chunk = right.shape[1] // groups
    start = pl.multiple_of(flipped(lax.axis_index("frames"), r, 3) * chunk, chunk)
    return mm(flat, right[:, pl.ds(start, chunk)], 1, 0).astype(BF)


def chunk_grads(t, first, chosen, grads, normed, other, groups):
    flat = [grad.T for grad in grads]
    right = (normed, normed, normed, other)
    for pair, relative in enumerate(chosen):
        for i, r in enumerate(relative):
            for j in range(2):
                at = 2 * pair + j
                t.outs[first + pair][i, j] = chunk_of(flat[at], right[at], r, groups)


def half_shape(width, dim, groups):
    return shape((groups // 2, 2, width, dim // groups))


def temporal_stage(attn, x_all, g_all, up, w_so, w_qkv, clips, heads, frames, per):
    mp, (rows, width) = len(attn), attn[0].shape
    own_rows = rows // mp
    dim = x_all.shape[1]
    halves = frames == 8

    def rows_of(r):
        return own_block(r, own_rows)

    def body(t):
        (clip_ref,) = t.smem
        back, inv_buf = t.scratch
        total = t.get(mp)[...].astype(F32)
        order = row_order(rows, mp, frames, per)
        for r in range(mp):
            part = mm(order, t.get(r)[...], 1, 0).astype(BF)
            total += mm(part, t.get(mp + 2 + r)[...], 1, 0)
        inv = inv_rms(total)
        nh = (total * inv).astype(BF)
        t.outs[2][...] = nh
        inv_buf[...] = jnp.broadcast_to(inv, inv_buf.shape)
        t.outs[3][...] = t.outs[2][rows_of(0), :]
        t.outs[4][...] = inv_buf[rows_of(0), :]

        def key_of(axis):
            dims = (rows, 1) if axis == 0 else (1, rows)
            token = lax.broadcasted_iota(jnp.int32, dims, axis)
            block = token // per
            frame = block % frames
            patch = (block // frames) * per + token % per
            end = jnp.int32(0)
            clip = jnp.zeros(dims, jnp.int32)
            for c in range(clips.shape[0]):
                end = end + clip_ref[c]
                clip += (frame >= end).astype(jnp.int32)
            return clip * rows + patch

        allowed = key_of(0) == key_of(1)
        w = t.get(2 * mp + 2)
        q, k, v = [mm(nh, w[j], 1, 0).astype(BF) for j in range(3)]
        grads = attend_back(
            q, k, v, t.get(mp + 1)[...], heads, lambda h: probs_of(q, k, h, allowed), True
        )
        for j in range(4):
            t.outs[5][j] = grads[j]
        d_normed = jnp.zeros((rows, dim), F32)
        for j in range(3):
            d_normed += mm(grads[j], w[j], 1, 1)
        back[...] = d_normed.astype(BF)
        for r in range(mp):
            t.outs[1 - r % 2][r // 2] = back[rows_of(r), :]
        if halves:
            chunk_grads(t, 6, SENT, grads, t.outs[2], t.get(2 * mp + 3), frames)

    half = shape((mp // 2, own_rows, dim))
    outs = (
        half,
        half,
        shape((rows, dim)),
        shape((own_rows, dim)),
        shape((own_rows, 128), F32),
        shape((4, rows, width)),
    )
    if halves:
        outs += (half_shape(width, dim, frames),) * 2
    ins = (*attn, x_all, up, *w_so, w_qkv, g_all)
    return run(
        body, ins, "v" * len(ins), outs, "v" * len(outs), smem=(clips,),
        scratch=(pltpu.VMEM((rows, dim), BF), pltpu.VMEM((rows, 128), F32)),
    )


def head_sums(send, keep):
    def body(t):
        t.outs[0][...] = (t.get(0)[1].astype(F32) + t.get(1)[1].astype(F32)).astype(BF)

    came = swap(send, "mp", 1)
    (pair,) = run(body, (keep, came), "vv", (shape(keep.shape[1:]),), "v")
    return keep, came, swap(pair, "mp", 2)


def summed(t):
    return t.get(0)[0].astype(F32) + t.get(1)[0].astype(F32) + t.get(2)[...].astype(F32)


def hidden_back(parts, unit, inv, grad):
    dim = unit.shape[1]

    def body(t):
        total, nh = summed(t), t.get(3)[...].astype(F32)
        rest = total - nh * jnp.mean(total * nh, -1, keepdims=True)
        g = t.get(5)[:, dim:].astype(F32)
        t.outs[0][...] = (g + t.get(4)[:, :1] * rest).astype(BF)

    return run(body, (*parts, unit, inv, grad), "vvvvvv", (shape(unit.shape),), "v")[0]


def tokens_back(parts, x, grad):
    def body(t):
        total, xf = summed(t), t.get(3)[...].astype(F32)
        inv = inv_rms(xf)
        nx = xf * inv
        rest = total - nx * jnp.mean(total * nx, -1, keepdims=True)
        t.outs[0][...] = (t.get(4)[...].astype(F32) + inv * rest).astype(BF)

    return run(body, (*parts, x, grad), "vvvvv", (shape(x.shape),), "v")[0]


def weight_grads_half(grads, normed, other, groups, flops=1000):
    def body(t):
        left = [t.get(0)[j] for j in range(4)]
        chunk_grads(t, 0, KEPT, left, t.get(1), t.get(2), groups)

    half = half_shape(grads.shape[2], normed.shape[1], groups)
    return run(body, (grads, normed, other), "vvv", (half, half), "vv", flops=flops)


def weight_grads_whole(grads, normed, other):
    def body(t):
        for j in range(4):
            right = t.get(2) if j == 3 else t.get(1)
            t.outs[0][j] = mm(t.get(0)[j], right[...], 0, 0)

    whole = shape((4, grads.shape[2], normed.shape[1]), F32)
    return run(body, (grads, normed, other), "vhh", (whole,), "h")[0]


def spatial_probs(qkv, attn_moved, heads, groups, mp):
    rows, width = attn_moved.shape

    def body(t):
        q, k = t.get(0)[0], t.get(0)[1]
        for h in range(heads):
            t.outs[0][h] = probs_of(q, k, h, None)
        order = row_order(rows, mp, groups, rows // (groups * mp))
        t.outs[1][...] = mm(order, t.get(1)[...], 1, 0).astype(BF)

    outs = (shape((heads, rows, rows), F32), shape((rows, width)))
    return run(body, (qkv, attn_moved), "vv", outs, "vv")


def out_chunks(parts, attn, groups):
    own_rows, dim = parts[0].shape
    mp, width = len(parts), attn.shape[1]

    def body(t):
        dh = t.outs[0]
        for r in range(mp):
            dh[own_block(r, own_rows), :] = t.get(r)[...]
        if groups == 8:
            flat = t.get(mp)[...].T
            for at, relative in ((1, OUT_SENT), (2, OUT_KEPT)):
                for i, r in enumerate(relative):
                    t.outs[at][i] = chunk_of(flat, dh, r, groups)

    outs = (shape((mp * own_rows, dim)),)
    if groups == 8:
        outs += (shape((groups // 2, width, dim // groups)),) * 2
    return run(body, (*parts, attn), "v" * (mp + 1), outs, "v" * len(outs))


def qkv_parts(grads):
    flat = jnp.concatenate([grad.T for grad in grads], 0)
    first = 7 * flat.shape[0] // 12
    return flat[:first], flat[first:]


def qkv_chunks(t, first, chosen, grads, normed, groups):
    for at, (flat, relative) in enumerate(zip(qkv_parts(grads), chosen)):
        for i, r in enumerate(relative):
            t.outs[first + at][i] = chunk_of(flat, normed, r, groups)


def qkv_part_shapes(width, dim, groups):
    first = 7 * 3 * width // 12
    return tuple(
        shape((groups // 2, rows, dim // groups)) for rows in (first, 3 * width - first)
    )


def spatial_back(dh, w_so, qkv, probs, normed, heads, groups):
    rows, dim = dh.shape
    width = w_so.shape[0]

    def body(t):
        up = mm(t.get(0)[...], t.get(1)[...], 1, 1).astype(BF)
        qkv_ref = t.get(2)
        grads = attend_back(
            qkv_ref[0], qkv_ref[1], qkv_ref[2], up, heads, lambda h: t.get(3)[h], False
        )[:3]
        for j in range(3):
            t.outs[0][j] = grads[j]
        if groups == 8:
            qkv_chunks(t, 1, SENT, grads, t.get(4), groups)

    outs = (shape((3, rows, width)),)
    if groups == 8:
        outs += qkv_part_shapes(width, dim, groups)
    return run(body, (dh, w_so, qkv, probs, normed), "vvvvh", outs, "v" * len(outs))


def qkv_keeps(grads, normed, groups, flops):
    def body(t):
        qkv_chunks(t, 0, KEPT, [t.get(0)[j] for j in range(3)], t.get(1), groups)

    outs = qkv_part_shapes(grads.shape[2], normed.shape[1], groups)
    return run(body, (grads, normed), "vv", outs, "vv", flops=flops)


def normed_back(grads, w_qkv, mp):
    rows, dim = grads.shape[1], w_qkv.shape[1]
    own_rows = rows // mp

    def body(t):
        (back,) = t.scratch
        total = jnp.zeros((rows, dim), F32)
        for j in range(3):
            total += mm(t.get(0)[j], t.get(1)[j], 1, 1)
        back[...] = total.astype(BF)
        for r in range(mp):
            t.outs[1 - r % 2][r // 2] = back[own_block(r, own_rows), :]

    half = shape((mp // 2, own_rows, dim))
    return run(
        body, (grads, w_qkv), "vv", (half, half), "vv", scratch=(pltpu.VMEM((rows, dim), BF),)
    )


def halve(keeps, cames, keep_in="v", out="v", merged=False):
    n, depth = len(keeps), keeps[0].shape[0]

    def body(t):
        for i in range(depth - 1, -1, -1):
            for at in range(n):
                total = t.get(at)[i].astype(F32) + t.get(n + at)[i].astype(F32)
                kept = 1 - i % 2
                if merged:
                    t.outs[kept][at] = total.astype(BF)
                else:
                    t.outs[n * kept + at][i // 2] = total.astype(BF)

    if merged:
        outs = (shape((n, *keeps[0].shape[1:])),) * 2
    else:
        outs = tuple(shape((depth // 2, *keep.shape[1:])) for keep in keeps) * 2
    where = keep_in * n + "v" * n
    return run(body, (*keeps, *cames), where, outs, out * len(outs))


def last_sums(pairs):
    chunk, size = pairs[0][0].shape[-1], HD
    blocks = [tuple(part.reshape(-1, size, chunk) for part in pair) for pair in pairs]
    width = sum(pair[0].shape[0] for pair in blocks) * size // 4
    per = width // size

    def body(t):
        b = 0
        for at, (keep, _) in enumerate(blocks):
            for i in range(keep.shape[0]):
                total = t.get(2 * at)[i].astype(F32) + t.get(2 * at + 1)[i].astype(F32)
                side = slice((b % per) * size, (b % per + 1) * size)
                if b < 3 * per:
                    t.outs[0][b // per, :, side] = total.T
                else:
                    t.outs[1][side, :] = total
                b += 1

    ins = [part for pair in blocks for part in pair]
    outs = (shape((3, chunk, width), F32), shape((width, chunk), F32))
    return run(body, ins, "v" * len(ins), outs, "hh")


def reduce_whole(flat, normed, other):
    whole = weight_grads_whole(flat, normed, other)
    mine = lax.psum_scatter(whole, "frames", scatter_dimension=2, tiled=True)
    return jnp.swapaxes(mine[:3], 1, 2), mine[3]


def shards(
    video_tokens, grad_output, spatial_qkv, spatial_out, temporal_qkv, temporal_out, clip_frames
):
    frames_dev, rows_mp, dim = video_tokens.shape
    width = spatial_out.shape[0]
    heads = width // HD
    groups = lax.axis_size("frames")
    mp = lax.axis_size("mp")
    patches = rows_mp * mp
    per = rows_mp // groups
    assert frames_dev == 1 and rows_mp % groups == 0 and mp == 4

    halves = groups == 8
    x_own, g_own = video_tokens[0], grad_output[0]
    x_one, x_two = swap(x_own, "mp", 1), swap(x_own, "mp", 2)
    xg, x_one, x_two, so_own = lax.optimization_barrier(
        (joined(x_own, g_own), x_one, x_two, spatial_out)
    )
    x_three = swap(x_two, "mp", 1)
    xg = lax.all_to_all(xg.reshape(groups, per, 2 * dim), "frames", 0, 0, tiled=True)
    xg = xg.reshape(rows_mp, 2 * dim)
    so_two = swap(so_own, "mp", 2)

    normed_x, qkv_s, attn_send = spatial_forward(
        (x_own, x_one, x_two, x_three), spatial_qkv, heads, groups
    )
    attn_send, xg = lax.optimization_barrier((attn_send, xg))
    xg_two = swap(xg, "mp", 2)
    moved = lax.all_to_all(
        attn_send.reshape(groups, mp * per, width), "frames", 0, 0, tiled=True
    ).reshape(patches, width)
    so_two, moved = lax.optimization_barrier((so_two, moved))
    moved_two = swap(moved, "mp", 2)
    w_so = spatial_out, swap(spatial_out, "mp", 1), so_two, swap(so_two, "mp", 1)
    xg_all = xg, swap(xg, "mp", 1), xg_two, swap(xg_two, "mp", 1)
    moved_two, rows_own = lax.optimization_barrier((moved_two, owner_rows(xg_all, temporal_out)))
    x_rows, g_rows, d_attn_t = rows_own
    attn_owned = moved, swap(moved, "mp", 1), moved_two, swap(moved_two, "mp", 1)

    send_h, keep_h, normed_h, unit_own, inv_own, t_grads, *t_sent = temporal_stage(
        attn_owned, x_rows, g_rows, d_attn_t, w_so, temporal_qkv, clip_frames, heads, groups, per
    )
    parts = head_sums(send_h, keep_h)
    if halves:
        t_kept = weight_grads_half(t_grads, normed_h, g_rows, groups)
        parts, t_kept = lax.optimization_barrier((parts, t_kept))
        came = [swap(t_sent[0], "frames", 1), swap(t_sent[1], "frames", 2)]
        t_sums = halve(t_kept, came, out="h")
    d_hidden = hidden_back(parts, unit_own, inv_own, xg)
    d_hidden = lax.all_to_all(
        d_hidden.reshape(groups, per, dim), "frames", 0, 0, tiled=True
    ).reshape(rows_mp, dim)
    if halves:
        d_hidden, t_sums = lax.optimization_barrier((d_hidden, t_sums))
        t_second = [swap(t_sums[0], "frames", 2), swap(t_sums[1], "frames", 1)]
    dh_one, dh_two = swap(d_hidden, "mp", 1), swap(d_hidden, "mp", 2)
    d_hidden, qkv_s, attn_send = lax.optimization_barrier((d_hidden, qkv_s, attn_send))
    probs_s, attn_s = spatial_probs(qkv_s, attn_send, heads, groups, mp)
    dh_two, probs_s, attn_s = lax.optimization_barrier((dh_two, probs_s, attn_s))
    dh_three = swap(dh_two, "mp", 1)
    d_hidden_all, *o_chunks = out_chunks((d_hidden, dh_one, dh_two, dh_three), attn_s, groups)
    dh_ready = d_hidden_all
    if halves:
        dh_ready, t_second = lax.optimization_barrier((dh_ready, t_second))
        t_send, t_keep = halve(t_sums[2:], t_second, keep_in="h", merged=True)
        dh_ready, t_send, t_keep = lax.optimization_barrier((dh_ready, t_send, t_keep))
        t_came = swap(t_send, "frames", 4)
    else:
        t_qkv, t_out = reduce_whole(t_grads, normed_h, g_rows)
    s_grads, *s_sent = spatial_back(
        dh_ready, spatial_out, qkv_s, probs_s, normed_x, heads, groups
    )
    if halves:
        after = lax.optimization_barrier
        o_send, o_keep = halve([o_chunks[1]], [swap(o_chunks[0], "frames", 1)])
        send_x, keep_x = normed_back(s_grads, spatial_qkv, mp)
        s_grads, t_came, o_send, o_keep = after((s_grads, t_came, o_send, o_keep))
        t_qkv, t_out = last_sums([(t_keep, t_came)])
        s_kept = qkv_keeps(s_grads, normed_x, groups, 50_000_000_000)
        a_came, b_came = swap(s_sent[0], "frames", 1), swap(s_sent[1], "frames", 2)
        o_came = swap(o_send, "frames", 4)
        a_sums = halve([s_kept[0]], [a_came])
        a_sums, b_came = after((a_sums, b_came))
        b_sums = halve([s_kept[1]], [b_came])
        b_sums, o_came = after((b_sums, o_came))
        o_sums = halve([o_keep], [o_came])
        a_came, b_came = swap(a_sums[0], "frames", 2), swap(b_sums[0], "frames", 1)
        o_sums, a_came = after((o_sums, a_came))
        a_sums = halve([a_sums[1]], [a_came])
        a_sums, b_came = after((a_sums, b_came))
        b_sums = halve([b_sums[1]], [b_came])
        s_qkv, s_out = last_sums([
            (a_sums[1], swap(a_sums[0], "frames", 4)),
            (b_sums[1], swap(b_sums[0], "frames", 4)),
            (o_sums[1], swap(o_sums[0], "frames", 2)),
        ])
    else:
        send_x, keep_x = normed_back(s_grads, spatial_qkv, mp)
        all_grads = jnp.concatenate([s_grads, attn_s[None]], 0)
        s_qkv, s_out = reduce_whole(all_grads, normed_x, d_hidden_all)
    grad_tokens = tokens_back(head_sums(send_x, keep_x), x_own, d_hidden)
    return grad_tokens[None], s_qkv, s_out, t_qkv, t_out


def solution(mesh):
    placed = (
        P("frames", "mp", None),
        P("frames", "mp", None),
        P(None, None, "mp"),
        P("mp", None),
        P(None, None, "mp"),
        P("mp", None),
        P(),
    )
    return jax.shard_map(
        shards,
        mesh=mesh,
        in_specs=placed,
        out_specs=(
            P("frames", "mp", None),
            P(None, "frames", "mp"),
            P("mp", "frames"),
            P(None, "frames", "mp"),
            P("mp", "frames"),
        ),
        check_vma=False,
    )
```

```python
import jax
import jax.numpy as jnp
from jax import lax
from jax.experimental import pallas as pl
from jax.experimental.pallas import tpu as pltpu
from jax.sharding import PartitionSpec as P

HD = 64
EPS = 1e-06
NEGATIVE = -1e30
BF = jnp.bfloat16
F32 = jnp.float32
VMEM_LIMIT = 20 * 1024 * 1024


def mm(a, b, ca, cb):
    return lax.dot_general(a, b, (((ca,), (cb,)), ((), ())), preferred_element_type=F32)


def shape(dims, dtype=BF):
    return jax.ShapeDtypeStruct(dims, dtype)


def flipped(index, by, bits):
    total = index
    for b in range(bits):
        if (by >> b) & 1:
            total = total + (1 << b) * (1 - 2 * ((index // (1 << b)) % 2))
    return total


def swap(value, axis, by):
    size = lax.axis_size(axis)
    return lax.ppermute(value, axis, [(i, i ^ by) for i in range(size)])


class Kernel:
    def __init__(self, get, outs, put, smem, scratch, sems, early):
        self.get, self.outs, self.put = get, outs, put
        self.smem, self.scratch, self.sems, self.early = smem, scratch, sems, early

    def copy(self, src, dst):
        made = pltpu.make_async_copy(src, dst, self.sems.pop(0))
        made.start()
        return made


def run(
    body, ins, where, outs, out_where, smem=(), scratch=(), copies=0, early=None, flops=1000
):
    n, k, s = len(ins), len(outs), len(smem)
    staged_in = [i for i in range(n) if where[i] in "ha"]
    staged_out = [i for i in range(k) if out_where[i] in "ha"]

    def wrapped(*refs):
        refs = list(refs)

        def take(count):
            part = refs[:count]
            del refs[:count]
            return part

        scalars, src, dst = take(s), take(n), take(k)
        in_bufs, out_bufs = take(len(staged_in)), take(len(staged_out))
        in_sem, out_sem, own_sem = take(3)
        loads, stores = {}, {}
        results = list(dst)
        for at, i in enumerate(staged_out):
            results[i] = out_bufs[at]
        held = {i: in_bufs[at] for at, i in enumerate(staged_in)}
        waited = set()

        def get(i):
            if i not in held:
                return src[i]
            if i not in waited:
                loads[i].wait()
                waited.add(i)
            return held[i]

        def put(i):
            if i in staged_out and i not in stores:
                at = staged_out.index(i)
                stores[i] = pltpu.make_async_copy(out_bufs[at], dst[i], out_sem.at[at])
                stores[i].start()

        sems = [own_sem.at[i] for i in range(copies)]
        tools = Kernel(get, results, put, scalars, refs, sems, None)
        if early is not None:
            tools.early = early(tools)
        for at, i in enumerate(staged_in):
            loads[i] = pltpu.make_async_copy(src[i], in_bufs[at], in_sem.at[at])
            loads[i].start()
        body(tools)
        for i in staged_in:
            get(i)
        for i in range(k):
            put(i)
        for copy in stores.values():
            copy.wait()

    specs = {"v": pltpu.VMEM, "h": pltpu.HBM, "a": pl.ANY, "n": pl.ANY, "x": pltpu.HBM}
    specs = {key: pl.BlockSpec(memory_space=space) for key, space in specs.items()}
    buffers = [pltpu.VMEM(ins[i].shape, ins[i].dtype) for i in staged_in]
    buffers += [pltpu.VMEM(outs[i].shape, outs[i].dtype) for i in staged_out]
    ins = [
        pltpu.with_memory_space_constraint(a, pltpu.HBM) if w in "hx" else a
        for a, w in zip(ins, where)
    ]
    return pl.pallas_call(
        wrapped,
        out_shape=tuple(
            pltpu.HBM(o.shape, o.dtype) if w in "hx" else o for o, w in zip(outs, out_where)
        ),
        in_specs=[pl.BlockSpec(memory_space=pltpu.SMEM)] * s
        + [specs[w] for w in where],
        out_specs=tuple(specs[w] for w in out_where),
        scratch_shapes=buffers
        + [pltpu.SemaphoreType.DMA((max(1, c),)) for c in (len(staged_in), len(staged_out), copies)]
        + list(scratch),
        compiler_params=pltpu.CompilerParams(vmem_limit_bytes=VMEM_LIMIT),
        cost_estimate=pl.CostEstimate(flops=flops, bytes_accessed=1000, transcendentals=0),
    )(*smem, *ins)


def inv_rms(v):
    return lax.rsqrt(jnp.mean(v * v, -1, keepdims=True) + EPS)


SCALE = HD ** (-0.5)
assert SCALE == 0.125


def head_mask(width, head, scale=1.0):
    lane = lax.broadcasted_iota(jnp.int32, (1, width), 1)
    mask = ((lane >= head * HD) & (lane < (head + 1) * HD)).astype(F32)
    return (mask * scale).astype(BF)


def probs_of(q, k, head, allowed):
    scores = mm(q * head_mask(q.shape[1], head, SCALE), k, 1, 1)
    if allowed is not None:
        scores = jnp.where(allowed, scores, NEGATIVE)
    expo = jnp.exp(scores - jnp.max(scores, -1, keepdims=True))
    return expo * (1.0 / jnp.sum(expo, -1, keepdims=True))


def attend(q, k, v, heads):
    total = jnp.zeros(q.shape, F32)
    for h in range(heads):
        mask = head_mask(q.shape[1], h)
        probs = probs_of(q, k, h, None)
        total += mm(probs.astype(BF), v * mask, 1, 0)
    return total.astype(BF)


def attend_back(q, k, v, up, heads, probs_at, with_out):
    zero = jnp.zeros(q.shape, F32)
    out, dq, dk, dv = zero, zero, zero, zero
    v_scaled = v * jnp.full((1, 1), SCALE, BF)
    for h in range(heads):
        mask = head_mask(q.shape[1], h)
        up_head = up * mask
        probs = probs_at(h)
        probs_b = probs.astype(BF)
        if with_out:
            out += mm(probs_b, v * mask, 1, 0)
        dv += mm(probs_b, up_head, 0, 0)
        dp = mm(up_head, v_scaled, 1, 1)
        delta = jnp.sum(probs * dp, -1, keepdims=True)
        ds = (probs * (dp - delta)).astype(BF)
        dq += mm(ds, k * mask, 1, 0)
        dk += mm(ds, q * mask, 0, 0)
    return dq.astype(BF), dk.astype(BF), dv.astype(BF), out.astype(BF)


def row_order(rows, outer, middle, inner):
    to = lax.broadcasted_iota(jnp.int32, (rows, 1), 0)
    at = lax.broadcasted_iota(jnp.int32, (1, rows), 1)
    o, m, i = to // (middle * inner), (to // inner) % middle, to % inner
    return (at == (m * outer + o) * inner + i).astype(F32).astype(BF)


def own_block(r, rows):
    start = flipped(lax.axis_index("mp"), r, 2) * rows
    return pl.ds(pl.multiple_of(start, rows), rows)


def joined(x, grad):
    rows, dim = x.shape

    def body(t):
        for i in range(2):
            t.outs[0][:, i * dim : (i + 1) * dim] = t.get(i)[...]

    return run(body, (x, grad), "hh", (shape((rows, 2 * dim)),), "v")[0]


def spatial_forward(parts, weights, heads, groups):
    own_rows, dim = parts[0].shape
    mp, width = len(parts), weights.shape[2]
    rows = mp * own_rows

    def body(t):
        for r in (*range(1, mp), 0):
            xf = t.get(r)[...].astype(F32)
            t.outs[0][own_block(r, own_rows), :] = (xf * inv_rms(xf)).astype(BF)
        nx = t.outs[0][...]
        t.put(0)
        w = t.get(mp)
        q, k, v = [mm(nx, w[j], 1, 0).astype(BF) for j in range(3)]
        for j, part in enumerate((q, k, v)):
            t.outs[1][j] = part
        t.put(1)
        attn = attend(q, k, v, heads)
        order = row_order(rows, groups, mp, rows // (groups * mp))
        t.outs[2][...] = mm(order, attn, 1, 0).astype(BF)

    outs = (shape((rows, dim)), shape((3, rows, width)), shape((rows, width)))
    return run(
        body, (*parts, weights), "h" + "v" * (mp - 1) + "h", outs, "hhv"
    )


def owner_rows(xg, w_to, attn, w_so, frames, per):
    own_rows, mp = xg[0].shape[0], len(xg)
    rows, (width, dim) = mp * own_rows, w_to.shape

    def body(t):
        x_buf = t.scratch[0]
        for r in range(mp):
            at = own_block(r, own_rows)
            x_buf[at, :] = t.get(r)[:, :dim]
            t.outs[1][at, :] = t.get(r)[:, dim:]
        total = x_buf[...].astype(F32)
        order = row_order(rows, mp, frames, per)
        for i in range(len(attn)):
            part = mm(order, t.get(mp + 1 + i)[...], 1, 0).astype(BF)
            total += mm(part, t.get(mp + 1 + len(attn) + i)[...], 1, 0)
        t.outs[0][...] = total
        t.outs[2][...] = mm(t.outs[1][...], t.get(mp)[...], 1, 1).astype(BF)

    outs = (shape((rows, dim), F32), shape((rows, dim)), shape((rows, width)))
    ins = (*xg, w_to, *attn, *w_so)
    where = "v" * mp + "h" + "v" * len(attn) + "h" + "v" * (len(w_so) - 1)
    return run(body, ins, where, outs, "vvv", scratch=(pltpu.VMEM((rows, dim), BF),))


SENT = ((1, 3, 5, 7), (2, 3, 6, 7))
KEPT = ((0, 2, 4, 6), (0, 1, 4, 5))
OUT_SENT, OUT_KEPT = (1, 5, 3, 7), (0, 4, 2, 6)


def chunk_of(flat, right, r, groups):
    chunk = right.shape[1] // groups
    start = pl.multiple_of(flipped(lax.axis_index("frames"), r, 3) * chunk, chunk)
    return mm(flat, right[:, pl.ds(start, chunk)], 1, 0).astype(BF)


def chunk_grads(t, first, chosen, grads, normed, other, groups):
    flat = [grad.T for grad in grads]
    right = (normed, normed, normed, other)
    for pair, relative in enumerate(chosen):
        for i, r in enumerate(relative):
            for j in range(2):
                at = 2 * pair + j
                side = slice(j * flat[at].shape[0], (j + 1) * flat[at].shape[0])
                t.outs[first + pair][i, side] = chunk_of(flat[at], right[at], r, groups)


def half_shape(width, dim, groups):
    return shape((groups // 2, 2 * width, dim // groups))


def temporal_stage(attn, so_far, g_all, up, w_so, w_qkv, clips, heads, frames, per, mp):
    n, (rows, width) = len(attn), attn[0].shape
    own_rows = rows // mp
    dim = so_far.shape[1]
    halves = frames == 8

    def rows_of(r):
        return own_block(r, own_rows)

    def body(t):
        (clip_ref,) = t.smem
        back, inv_buf = t.scratch
        total = t.get(n)[...]
        order = row_order(rows, mp, frames, per)
        for r in range(n):
            part = mm(order, t.get(r)[...], 1, 0).astype(BF)
            total += mm(part, t.get(n + 2 + r)[...], 1, 0)
        inv = inv_rms(total)
        nh = (total * inv).astype(BF)
        t.outs[2][...] = nh
        inv_buf[...] = jnp.broadcast_to(inv, inv_buf.shape)
        t.outs[3][...] = t.outs[2][rows_of(0), :]
        t.outs[4][...] = inv_buf[rows_of(0), :]

        def key_of(axis):
            dims = (rows, 1) if axis == 0 else (1, rows)
            token = lax.broadcasted_iota(jnp.int32, dims, axis)
            block = token // per
            frame = block % frames
            patch = (block // frames) * per + token % per
            end = jnp.int32(0)
            clip = jnp.zeros(dims, jnp.int32)
            for c in range(clips.shape[0]):
                end = end + clip_ref[c]
                clip += (frame >= end).astype(jnp.int32)
            return clip * rows + patch

        allowed = key_of(0) == key_of(1)
        w = t.get(2 * n + 2)
        q, k, v = [mm(nh, w[j], 1, 0).astype(BF) for j in range(3)]
        grads = attend_back(
            q, k, v, t.get(n + 1)[...], heads, lambda h: probs_of(q, k, h, allowed), True
        )
        for j in range(4):
            t.outs[5][j] = grads[j]
        d_normed = jnp.zeros((rows, dim), F32)
        for j in range(3):
            d_normed += mm(grads[j], w[j], 1, 1)
        back[...] = d_normed.astype(BF)
        for r in range(mp):
            t.outs[1 - r % 2][r // 2] = back[rows_of(r), :]
        if halves:
            chunk_grads(t, 6, SENT, grads, t.outs[2], t.get(2 * n + 3), frames)

    half = shape((mp // 2, own_rows, dim))
    outs = (
        half,
        half,
        shape((rows, dim)),
        shape((own_rows, dim)),
        shape((own_rows, 128), F32),
        shape((4, rows, width)),
    )
    if halves:
        outs += (half_shape(width, dim, frames),) * 2
    ins = (*attn, so_far, up, *w_so, w_qkv, g_all)
    return run(
        body, ins, "v" * len(ins), outs, "v" * len(outs), smem=(clips,),
        scratch=(pltpu.VMEM((rows, dim), BF), pltpu.VMEM((rows, 128), F32)),
    )


def head_sums(send, keep):
    def body(t):
        t.outs[0][...] = (t.get(0)[1].astype(F32) + t.get(1)[1].astype(F32)).astype(BF)

    came = swap(send, "mp", 1)
    (pair,) = run(body, (keep, came), "vv", (shape(keep.shape[1:]),), "v")
    return keep, came, swap(pair, "mp", 2)


def summed(t):
    return t.get(0)[0].astype(F32) + t.get(1)[0].astype(F32) + t.get(2)[...].astype(F32)


def hidden_back(parts, unit, inv, grad):
    dim = unit.shape[1]

    def body(t):
        total, nh = summed(t), t.get(3)[...].astype(F32)
        rest = total - nh * jnp.mean(total * nh, -1, keepdims=True)
        g = t.get(5)[:, dim:].astype(F32)
        t.outs[0][...] = (g + t.get(4)[:, :1] * rest).astype(BF)

    return run(body, (*parts, unit, inv, grad), "vvvvvv", (shape(unit.shape),), "v")[0]


def tokens_back(parts, x, grad):
    def body(t):
        total, xf = summed(t), t.get(3)[...].astype(F32)
        inv = inv_rms(xf)
        nx = xf * inv
        rest = total - nx * jnp.mean(total * nx, -1, keepdims=True)
        t.outs[0][...] = (t.get(4)[...].astype(F32) + inv * rest).astype(BF)

    return run(body, (*parts, x, grad), "vvvvv", (shape(x.shape),), "v")[0]


def weight_grads_half(grads, normed, other, groups, flops=1000):
    def body(t):
        left = [t.get(0)[j] for j in range(4)]
        chunk_grads(t, 0, KEPT, left, t.get(1), t.get(2), groups)

    half = half_shape(grads.shape[2], normed.shape[1], groups)
    return run(body, (grads, normed, other), "vvv", (half, half), "vv", flops=flops)


def weight_grads_whole(grads, normed, other):
    def body(t):
        for j in range(4):
            right = t.get(2) if j == 3 else t.get(1)
            t.outs[0][j] = mm(t.get(0)[j], right[...], 0, 0)

    whole = shape((4, grads.shape[2], normed.shape[1]), F32)
    return run(body, (grads, normed, other), "vhh", (whole,), "h")[0]


def spatial_probs(qkv, attn_moved, heads, groups, mp):
    rows, width = attn_moved.shape

    def body(t):
        q, k = t.get(0)[0], t.get(0)[1]
        for h in range(heads):
            t.outs[0][h] = probs_of(q, k, h, None)
        order = row_order(rows, mp, groups, rows // (groups * mp))
        t.outs[1][...] = mm(order, t.get(1)[...], 1, 0).astype(BF)

    outs = (shape((heads, rows, rows), F32), shape((rows, width)))
    return run(body, (qkv, attn_moved), "vv", outs, "vv")


def out_chunks(parts, attn, groups):
    own_rows, dim = parts[0].shape
    mp, width = len(parts), attn.shape[1]

    def body(t):
        dh = t.outs[0]
        for r in range(mp):
            dh[own_block(r, own_rows), :] = t.get(r)[...]
        if groups == 8:
            flat = t.get(mp)[...].T
            for at, relative in ((1, OUT_SENT), (2, OUT_KEPT)):
                for i, r in enumerate(relative):
                    t.outs[at][i] = chunk_of(flat, dh, r, groups)

    outs = (shape((mp * own_rows, dim)),)
    if groups == 8:
        outs += (shape((groups // 2, width, dim // groups)),) * 2
    return run(body, (*parts, attn), "v" * (mp + 1), outs, "v" * len(outs))


def qkv_parts(grads):
    flat = jnp.concatenate([grad.T for grad in grads], 0)
    first = 7 * flat.shape[0] // 12
    return flat[:first], flat[first:]


def qkv_chunks(t, first, chosen, grads, normed, groups):
    for at, (flat, relative) in enumerate(zip(qkv_parts(grads), chosen)):
        for i, r in enumerate(relative):
            t.outs[first + at][i] = chunk_of(flat, normed, r, groups)


def qkv_part_shapes(width, dim, groups):
    first = 7 * 3 * width // 12
    return tuple(
        shape((groups // 2, rows, dim // groups)) for rows in (first, 3 * width - first)
    )


def spatial_back(dh, w_so, qkv, probs, normed, heads, groups):
    rows, dim = dh.shape
    width = w_so.shape[0]

    def body(t):
        up = mm(t.get(0)[...], t.get(1)[...], 1, 1).astype(BF)
        qkv_ref = t.get(2)
        grads = attend_back(
            qkv_ref[0], qkv_ref[1], qkv_ref[2], up, heads, lambda h: t.get(3)[h], False
        )[:3]
        for j in range(3):
            t.outs[0][j] = grads[j]
        if groups == 8:
            qkv_chunks(t, 1, SENT, grads, t.get(4), groups)

    outs = (shape((3, rows, width)),)
    if groups == 8:
        outs += qkv_part_shapes(width, dim, groups)
    return run(body, (dh, w_so, qkv, probs, normed), "vvvvh", outs, "v" * len(outs))


def qkv_keeps(grads, normed, groups, flops):
    def body(t):
        qkv_chunks(t, 0, KEPT, [t.get(0)[j] for j in range(3)], t.get(1), groups)

    outs = qkv_part_shapes(grads.shape[2], normed.shape[1], groups)
    return run(body, (grads, normed), "vv", outs, "vv", flops=flops)


def normed_back(grads, w_qkv, mp):
    rows, dim = grads.shape[1], w_qkv.shape[1]
    own_rows = rows // mp

    def body(t):
        (back,) = t.scratch
        total = jnp.zeros((rows, dim), F32)
        for j in range(3):
            total += mm(t.get(0)[j], t.get(1)[j], 1, 1)
        back[...] = total.astype(BF)
        for r in range(mp):
            t.outs[1 - r % 2][r // 2] = back[own_block(r, own_rows), :]

    half = shape((mp // 2, own_rows, dim))
    return run(
        body, (grads, w_qkv), "vv", (half, half), "vv", scratch=(pltpu.VMEM((rows, dim), BF),)
    )


def halve(keeps, cames, keep_in="v", out="v", merged=False):
    n, depth = len(keeps), keeps[0].shape[0]
    rows = [keep.shape[1] for keep in keeps]
    chunk = keeps[0].shape[2]

    def body(t):
        for i in range(depth - 1, -1, -1):
            for at in range(n):
                total = t.get(at)[i].astype(F32) + t.get(n + at)[i].astype(F32)
                kept, first = 1 - i % 2, sum(rows[:at])
                if merged:
                    t.outs[kept][first : first + rows[at]] = total.astype(BF)
                else:
                    t.outs[n * kept + at][i // 2] = total.astype(BF)

    if merged:
        outs = (shape((sum(rows), chunk)),) * 2
    else:
        outs = tuple(shape((depth // 2, r, chunk)) for r in rows) * 2
    where = keep_in * n + "v" * n
    return run(body, (*keeps, *cames), where, outs, out * len(outs))


def last_sums(pairs):
    chunk = pairs[0][0].shape[-1]
    pairs = [tuple(part.reshape(-1, chunk) for part in pair) for pair in pairs]
    width = sum(pair[0].shape[0] for pair in pairs) // 4

    def body(t):
        row = 0
        for at, (keep, _) in enumerate(pairs):
            start = 0
            while start < keep.shape[0]:
                size = min(width - row % width, keep.shape[0] - start)
                here = slice(start, start + size)
                total = t.get(2 * at)[here].astype(F32) + t.get(2 * at + 1)[here].astype(F32)
                side = slice(row % width, row % width + size)
                if row < 3 * width:
                    t.outs[0][row // width, :, side] = total.T
                else:
                    t.outs[1][side, :] = total
                start, row = start + size, row + size

    ins = [part for pair in pairs for part in pair]
    outs = (shape((3, chunk, width), F32), shape((width, chunk), F32))
    return run(body, ins, "v" * len(ins), outs, "hh")


def reduce_whole(flat, normed, other):
    whole = weight_grads_whole(flat, normed, other)
    mine = lax.psum_scatter(whole, "frames", scatter_dimension=2, tiled=True)
    return jnp.swapaxes(mine[:3], 1, 2), mine[3]


def shards(
    video_tokens, grad_output, spatial_qkv, spatial_out, temporal_qkv, temporal_out, clip_frames
):
    frames_dev, rows_mp, dim = video_tokens.shape
    width = spatial_out.shape[0]
    heads = width // HD
    groups = lax.axis_size("frames")
    mp = lax.axis_size("mp")
    patches = rows_mp * mp
    per = rows_mp // groups
    assert frames_dev == 1 and rows_mp % groups == 0 and mp == 4

    halves = groups == 8
    x_own, g_own = video_tokens[0], grad_output[0]
    x_one, x_two = swap(x_own, "mp", 1), swap(x_own, "mp", 2)
    xg, x_one, x_two, so_own = lax.optimization_barrier(
        (joined(x_own, g_own), x_one, x_two, spatial_out)
    )
    x_three = swap(x_two, "mp", 1)
    xg = lax.all_to_all(xg.reshape(groups, per, 2 * dim), "frames", 0, 0, tiled=True)
    xg = xg.reshape(rows_mp, 2 * dim)
    so_two = swap(so_own, "mp", 2)

    normed_x, qkv_s, attn_send = spatial_forward(
        (x_own, x_one, x_two, x_three), spatial_qkv, heads, groups
    )
    attn_send, xg = lax.optimization_barrier((attn_send, xg))
    xg_two = swap(xg, "mp", 2)
    moved = lax.all_to_all(
        attn_send.reshape(groups, mp * per, width), "frames", 0, 0, tiled=True
    ).reshape(patches, width)
    so_two, moved = lax.optimization_barrier((so_two, moved))
    moved_one, moved_two = swap(moved, "mp", 1), swap(moved, "mp", 2)
    so_one = swap(spatial_out, "mp", 1)
    xg_all = xg, swap(xg, "mp", 1), xg_two, swap(xg_two, "mp", 1)
    rows_own = owner_rows(
        xg_all, temporal_out, (moved, moved_one), (spatial_out, so_one), groups, per
    )
    moved_two, rows_own = lax.optimization_barrier((moved_two, rows_own))
    so_far, g_rows, d_attn_t = rows_own

    send_h, keep_h, normed_h, unit_own, inv_own, t_grads, *t_sent = temporal_stage(
        (moved_two, swap(moved_two, "mp", 1)), so_far, g_rows, d_attn_t,
        (so_two, swap(so_two, "mp", 1)), temporal_qkv, clip_frames, heads, groups, per, mp,
    )
    parts = head_sums(send_h, keep_h)
    if halves:
        t_kept = weight_grads_half(t_grads, normed_h, g_rows, groups)
        parts, t_kept = lax.optimization_barrier((parts, t_kept))
        came = [swap(t_sent[0], "frames", 1), swap(t_sent[1], "frames", 2)]
        t_sums = halve(t_kept, came, out="h")
    d_hidden = hidden_back(parts, unit_own, inv_own, xg)
    d_hidden = lax.all_to_all(
        d_hidden.reshape(groups, per, dim), "frames", 0, 0, tiled=True
    ).reshape(rows_mp, dim)
    if halves:
        d_hidden, t_sums = lax.optimization_barrier((d_hidden, t_sums))
        t_second = [swap(t_sums[0], "frames", 2), swap(t_sums[1], "frames", 1)]
    dh_one, dh_two = swap(d_hidden, "mp", 1), swap(d_hidden, "mp", 2)
    d_hidden, qkv_s, attn_send = lax.optimization_barrier((d_hidden, qkv_s, attn_send))
    probs_s, attn_s = spatial_probs(qkv_s, attn_send, heads, groups, mp)
    dh_two, probs_s, attn_s = lax.optimization_barrier((dh_two, probs_s, attn_s))
    dh_three = swap(dh_two, "mp", 1)
    d_hidden_all, *o_chunks = out_chunks((d_hidden, dh_one, dh_two, dh_three), attn_s, groups)
    dh_ready = d_hidden_all
    if halves:
        dh_ready, t_second = lax.optimization_barrier((dh_ready, t_second))
        t_send, t_keep = halve(t_sums[2:], t_second, keep_in="h", merged=True)
        dh_ready, t_send, t_keep = lax.optimization_barrier((dh_ready, t_send, t_keep))
        t_came = swap(t_send, "frames", 4)
    else:
        t_qkv, t_out = reduce_whole(t_grads, normed_h, g_rows)
    s_grads, *s_sent = spatial_back(
        dh_ready, spatial_out, qkv_s, probs_s, normed_x, heads, groups
    )
    if halves:
        after = lax.optimization_barrier
        send_x, keep_x = normed_back(s_grads, spatial_qkv, mp)
        s_grads, t_came = after((s_grads, t_came))
        t_qkv, t_out = last_sums([(t_keep, t_came)])
        s_kept = qkv_keeps(s_grads, normed_x, groups, 50_000_000_000)
        came = [swap(s_sent[0], "frames", 1), swap(s_sent[1], "frames", 2)]
        came.append(swap(o_chunks[0], "frames", 1))
        *sends, keep_a, keep_b, o_keep = halve([*s_kept, o_chunks[1]], came)
        came = [swap(send, "frames", by) for send, by in zip(sends, (2, 1, 4))]
        s_send, s_keep = halve([keep_a, keep_b], came[:2], merged=True)
        o_send, o_keep = halve([o_keep], came[2:])
        s_qkv, s_out = last_sums([
            (s_keep, swap(s_send, "frames", 4)), (o_keep, swap(o_send, "frames", 2))
        ])
    else:
        send_x, keep_x = normed_back(s_grads, spatial_qkv, mp)
        all_grads = jnp.concatenate([s_grads, attn_s[None]], 0)
        s_qkv, s_out = reduce_whole(all_grads, normed_x, d_hidden_all)
    grad_tokens = tokens_back(head_sums(send_x, keep_x), x_own, d_hidden)
    return grad_tokens[None], s_qkv, s_out, t_qkv, t_out


def solution(mesh):
    placed = (
        P("frames", "mp", None),
        P("frames", "mp", None),
        P(None, None, "mp"),
        P("mp", None),
        P(None, None, "mp"),
        P("mp", None),
        P(),
    )
    return jax.shard_map(
        shards,
        mesh=mesh,
        in_specs=placed,
        out_specs=(
            P("frames", "mp", None),
            P(None, "frames", "mp"),
            P("mp", "frames"),
            P(None, "frames", "mp"),
            P("mp", "frames"),
        ),
        check_vma=False,
    )
```

```python
import jax
import jax.numpy as jnp
from jax import lax
from jax.experimental import pallas as pl
from jax.experimental.pallas import tpu as pltpu
from jax.sharding import PartitionSpec as P

HD = 64
EPS = 1e-06
NEGATIVE = -1e30
BF = jnp.bfloat16
F32 = jnp.float32
VMEM_LIMIT = 20 * 1024 * 1024


def mm(a, b, ca, cb):
    return lax.dot_general(a, b, (((ca,), (cb,)), ((), ())), preferred_element_type=F32)


def shape(dims, dtype=BF):
    return jax.ShapeDtypeStruct(dims, dtype)


def flipped(index, by, bits):
    total = index
    for b in range(bits):
        if (by >> b) & 1:
            total = total + (1 << b) * (1 - 2 * ((index // (1 << b)) % 2))
    return total


def swap(value, axis, by):
    size = lax.axis_size(axis)
    return lax.ppermute(value, axis, [(i, i ^ by) for i in range(size)])


class Kernel:
    def __init__(self, get, outs, put, smem, scratch, sems, early):
        self.get, self.outs, self.put = get, outs, put
        self.smem, self.scratch, self.sems, self.early = smem, scratch, sems, early

    def copy(self, src, dst):
        made = pltpu.make_async_copy(src, dst, self.sems.pop(0))
        made.start()
        return made


def run(
    body, ins, where, outs, out_where, smem=(), scratch=(), copies=0, early=None, flops=1000
):
    n, k, s = len(ins), len(outs), len(smem)
    staged_in = [i for i in range(n) if where[i] in "ha"]
    staged_out = [i for i in range(k) if out_where[i] in "ha"]

    def wrapped(*refs):
        refs = list(refs)

        def take(count):
            part = refs[:count]
            del refs[:count]
            return part

        scalars, src, dst = take(s), take(n), take(k)
        in_bufs, out_bufs = take(len(staged_in)), take(len(staged_out))
        in_sem, out_sem, own_sem = take(3)
        loads, stores = {}, {}
        results = list(dst)
        for at, i in enumerate(staged_out):
            results[i] = out_bufs[at]
        held = {i: in_bufs[at] for at, i in enumerate(staged_in)}
        waited = set()

        def get(i):
            if i not in held:
                return src[i]
            if i not in waited:
                loads[i].wait()
                waited.add(i)
            return held[i]

        def put(i):
            if i in staged_out and i not in stores:
                at = staged_out.index(i)
                stores[i] = pltpu.make_async_copy(out_bufs[at], dst[i], out_sem.at[at])
                stores[i].start()

        sems = [own_sem.at[i] for i in range(copies)]
        tools = Kernel(get, results, put, scalars, refs, sems, None)
        if early is not None:
            tools.early = early(tools)
        for at, i in enumerate(staged_in):
            loads[i] = pltpu.make_async_copy(src[i], in_bufs[at], in_sem.at[at])
            loads[i].start()
        body(tools)
        for i in staged_in:
            get(i)
        for i in range(k):
            put(i)
        for copy in stores.values():
            copy.wait()

    specs = {"v": pltpu.VMEM, "h": pltpu.HBM, "a": pl.ANY, "n": pl.ANY, "x": pltpu.HBM}
    specs = {key: pl.BlockSpec(memory_space=space) for key, space in specs.items()}
    buffers = [pltpu.VMEM(ins[i].shape, ins[i].dtype) for i in staged_in]
    buffers += [pltpu.VMEM(outs[i].shape, outs[i].dtype) for i in staged_out]
    ins = [
        pltpu.with_memory_space_constraint(a, pltpu.HBM) if w in "hx" else a
        for a, w in zip(ins, where)
    ]
    return pl.pallas_call(
        wrapped,
        out_shape=tuple(
            pltpu.HBM(o.shape, o.dtype) if w in "hx" else o for o, w in zip(outs, out_where)
        ),
        in_specs=[pl.BlockSpec(memory_space=pltpu.SMEM)] * s
        + [specs[w] for w in where],
        out_specs=tuple(specs[w] for w in out_where),
        scratch_shapes=buffers
        + [pltpu.SemaphoreType.DMA((max(1, c),)) for c in (len(staged_in), len(staged_out), copies)]
        + list(scratch),
        compiler_params=pltpu.CompilerParams(vmem_limit_bytes=VMEM_LIMIT),
        cost_estimate=pl.CostEstimate(flops=flops, bytes_accessed=1000, transcendentals=0),
    )(*smem, *ins)


def inv_rms(v):
    return lax.rsqrt(jnp.mean(v * v, -1, keepdims=True) + EPS)


SCALE = HD ** (-0.5)
assert SCALE == 0.125


def head_mask(width, head, scale=1.0):
    lane = lax.broadcasted_iota(jnp.int32, (1, width), 1)
    mask = ((lane >= head * HD) & (lane < (head + 1) * HD)).astype(F32)
    return (mask * scale).astype(BF)


def probs_of(q, k, head, allowed):
    scores = mm(q * head_mask(q.shape[1], head, SCALE), k, 1, 1)
    if allowed is not None:
        scores = jnp.where(allowed, scores, NEGATIVE)
    expo = jnp.exp(scores - jnp.max(scores, -1, keepdims=True))
    return expo * (1.0 / jnp.sum(expo, -1, keepdims=True))


def attend(q, k, v, heads):
    total = jnp.zeros(q.shape, F32)
    for h in range(heads):
        mask = head_mask(q.shape[1], h)
        probs = probs_of(q, k, h, None)
        total += mm(probs.astype(BF), v * mask, 1, 0)
    return total.astype(BF)


def attend_back(q, k, v, up, heads, probs_at, with_out):
    zero = jnp.zeros(q.shape, F32)
    out, dq, dk, dv = zero, zero, zero, zero
    v_scaled = v * jnp.full((1, 1), SCALE, BF)
    for h in range(heads):
        mask = head_mask(q.shape[1], h)
        up_head = up * mask
        probs = probs_at(h)
        probs_b = probs.astype(BF)
        if with_out:
            out += mm(probs_b, v * mask, 1, 0)
        dv += mm(probs_b, up_head, 0, 0)
        dp = mm(up_head, v_scaled, 1, 1)
        delta = jnp.sum(probs * dp, -1, keepdims=True)
        ds = (probs * (dp - delta)).astype(BF)
        dq += mm(ds, k * mask, 1, 0)
        dk += mm(ds, q * mask, 0, 0)
    return dq.astype(BF), dk.astype(BF), dv.astype(BF), out.astype(BF)


def row_order(rows, outer, middle, inner):
    to = lax.broadcasted_iota(jnp.int32, (rows, 1), 0)
    at = lax.broadcasted_iota(jnp.int32, (1, rows), 1)
    o, m, i = to // (middle * inner), (to // inner) % middle, to % inner
    return (at == (m * outer + o) * inner + i).astype(F32).astype(BF)


def own_block(r, rows):
    start = flipped(lax.axis_index("mp"), r, 2) * rows
    return pl.ds(pl.multiple_of(start, rows), rows)


def joined(x, grad, weights):
    rows, dim = x.shape

    def body(t):
        brought = t.copy(t.get(2), t.outs[1])
        for i in range(2):
            t.outs[0][:, i * dim : (i + 1) * dim] = t.get(i)[...]
        brought.wait()

    outs = (shape((rows, 2 * dim)), shape(weights.shape))
    return run(body, (x, grad, weights), "hhx", outs, "vv", copies=1)


def spatial_forward(parts, weights, heads, groups):
    own_rows, dim = parts[0].shape
    mp, width = len(parts), weights.shape[2]
    rows = mp * own_rows

    def body(t):
        for r in (*range(1, mp), 0):
            xf = t.get(r)[...].astype(F32)
            t.outs[0][own_block(r, own_rows), :] = (xf * inv_rms(xf)).astype(BF)
        nx = t.outs[0][...]
        t.put(0)
        w = t.get(mp)
        q, k, v = [mm(nx, w[j], 1, 0).astype(BF) for j in range(3)]
        for j, part in enumerate((q, k, v)):
            t.outs[1][j] = part
        t.put(1)
        attn = attend(q, k, v, heads)
        order = row_order(rows, groups, mp, rows // (groups * mp))
        t.outs[2][...] = mm(order, attn, 1, 0).astype(BF)

    outs = (shape((rows, dim)), shape((3, rows, width)), shape((rows, width)))
    return run(
        body, (*parts, weights), "h" + "v" * mp, outs, "hhv"
    )


def owner_rows(xg, w_to, attn, w_so, frames, per):
    own_rows, mp = xg[0].shape[0], len(xg)
    rows, (width, dim) = mp * own_rows, w_to.shape

    def body(t):
        x_buf = t.scratch[0]
        for r in range(mp):
            at = own_block(r, own_rows)
            x_buf[at, :] = t.get(r)[:, :dim]
            t.outs[1][at, :] = t.get(r)[:, dim:]
        total = x_buf[...].astype(F32)
        order = row_order(rows, mp, frames, per)
        for i in range(len(attn)):
            part = mm(order, t.get(mp + 1 + i)[...], 1, 0).astype(BF)
            total += mm(part, t.get(mp + 1 + len(attn) + i)[...], 1, 0)
        t.outs[0][...] = total
        t.outs[2][...] = mm(t.outs[1][...], t.get(mp)[...], 1, 1).astype(BF)

    outs = (shape((rows, dim), F32), shape((rows, dim)), shape((rows, width)))
    ins = (*xg, w_to, *attn, *w_so)
    where = "v" * mp + "h" + "v" * len(attn) + "h" + "v" * (len(w_so) - 1)
    return run(body, ins, where, outs, "vvv", scratch=(pltpu.VMEM((rows, dim), BF),))


SENT = ((1, 3, 5, 7), (2, 3, 6, 7))
KEPT = ((0, 2, 4, 6), (0, 1, 4, 5))
OUT_SENT, OUT_KEPT = (1, 5, 3, 7), (0, 4, 2, 6)


def chunk_of(flat, right, r, groups):
    chunk = right.shape[1] // groups
    start = pl.multiple_of(flipped(lax.axis_index("frames"), r, 3) * chunk, chunk)
    return mm(flat, right[:, pl.ds(start, chunk)], 1, 0).astype(BF)


def chunk_grads(t, first, chosen, grads, normed, other, groups):
    flat = [grad.T for grad in grads]
    right = (normed, normed, normed, other)
    for pair, relative in enumerate(chosen):
        for i, r in enumerate(relative):
            for j in range(2):
                at = 2 * pair + j
                side = slice(j * flat[at].shape[0], (j + 1) * flat[at].shape[0])
                t.outs[first + pair][i, side] = chunk_of(flat[at], right[at], r, groups)


def half_shape(width, dim, groups):
    return shape((groups // 2, 2 * width, dim // groups))


def temporal_stage(attn, so_far, g_all, up, w_so, w_qkv, clips, heads, frames, per, mp):
    n, (rows, width) = len(attn), attn[0].shape
    own_rows = rows // mp
    dim = so_far.shape[1]
    halves = frames == 8

    def rows_of(r):
        return own_block(r, own_rows)

    def body(t):
        (clip_ref,) = t.smem
        back, inv_buf = t.scratch
        total = t.get(n)[...]
        order = row_order(rows, mp, frames, per)
        for r in range(n):
            part = mm(order, t.get(r)[...], 1, 0).astype(BF)
            total += mm(part, t.get(n + 2 + r)[...], 1, 0)
        inv = inv_rms(total)
        nh = (total * inv).astype(BF)
        t.outs[2][...] = nh
        inv_buf[...] = jnp.broadcast_to(inv, inv_buf.shape)
        t.outs[3][...] = t.outs[2][rows_of(0), :]
        t.outs[4][...] = inv_buf[rows_of(0), :]

        def key_of(axis):
            dims = (rows, 1) if axis == 0 else (1, rows)
            token = lax.broadcasted_iota(jnp.int32, dims, axis)
            block = token // per
            frame = block % frames
            patch = (block // frames) * per + token % per
            end = jnp.int32(0)
            clip = jnp.zeros(dims, jnp.int32)
            for c in range(clips.shape[0]):
                end = end + clip_ref[c]
                clip += (frame >= end).astype(jnp.int32)
            return clip * rows + patch

        allowed = key_of(0) == key_of(1)
        w = t.get(2 * n + 2)
        q, k, v = [mm(nh, w[j], 1, 0).astype(BF) for j in range(3)]
        grads = attend_back(
            q, k, v, t.get(n + 1)[...], heads, lambda h: probs_of(q, k, h, allowed), True
        )
        for j in range(4):
            t.outs[5][j] = grads[j]
        d_normed = jnp.zeros((rows, dim), F32)
        for j in range(3):
            d_normed += mm(grads[j], w[j], 1, 1)
        back[...] = d_normed.astype(BF)
        for r in range(mp):
            t.outs[1 - r % 2][r // 2] = back[rows_of(r), :]
        if halves:
            chunk_grads(t, 6, SENT, grads, t.outs[2], t.get(2 * n + 3), frames)

    half = shape((mp // 2, own_rows, dim))
    outs = (
        half,
        half,
        shape((rows, dim)),
        shape((own_rows, dim)),
        shape((own_rows, 128), F32),
        shape((4, rows, width)),
    )
    if halves:
        outs += (half_shape(width, dim, frames),) * 2
    ins = (*attn, so_far, up, *w_so, w_qkv, g_all)
    return run(
        body, ins, "v" * len(ins), outs, "v" * len(outs), smem=(clips,),
        scratch=(pltpu.VMEM((rows, dim), BF), pltpu.VMEM((rows, 128), F32)),
    )


def head_sums(send, keep, later=()):
    def body(t):
        t.outs[0][...] = (t.get(0)[1].astype(F32) + t.get(1)[1].astype(F32)).astype(BF)

    came = swap(send, "mp", 1)
    (pair,) = run(body, (keep, came), "vv", (shape(keep.shape[1:]),), "v")
    if later:
        pair, later = lax.optimization_barrier((pair, later))
    return (keep, came, swap(pair, "mp", 2)), later


def summed(t):
    return t.get(0)[0].astype(F32) + t.get(1)[0].astype(F32) + t.get(2)[...].astype(F32)


def hidden_back(parts, unit, inv, grad):
    dim = unit.shape[1]

    def body(t):
        total, nh = summed(t), t.get(3)[...].astype(F32)
        rest = total - nh * jnp.mean(total * nh, -1, keepdims=True)
        g = t.get(5)[:, dim:].astype(F32)
        t.outs[0][...] = (g + t.get(4)[:, :1] * rest).astype(BF)

    return run(body, (*parts, unit, inv, grad), "vvvvvv", (shape(unit.shape),), "v")[0]


def tokens_back(parts, x, grad):
    def body(t):
        total, xf = summed(t), t.get(3)[...].astype(F32)
        inv = inv_rms(xf)
        nx = xf * inv
        rest = total - nx * jnp.mean(total * nx, -1, keepdims=True)
        t.outs[0][...] = (t.get(4)[...].astype(F32) + inv * rest).astype(BF)

    return run(body, (*parts, x, grad), "vvvvv", (shape(x.shape),), "v")[0]


def weight_grads_half(grads, normed, other, groups, flops=1000):
    def body(t):
        left = [t.get(0)[j] for j in range(4)]
        chunk_grads(t, 0, KEPT, left, t.get(1), t.get(2), groups)

    half = half_shape(grads.shape[2], normed.shape[1], groups)
    return run(body, (grads, normed, other), "vvv", (half, half), "vv", flops=flops)


def weight_grads_whole(grads, normed, other):
    def body(t):
        for j in range(4):
            right = t.get(2) if j == 3 else t.get(1)
            t.outs[0][j] = mm(t.get(0)[j], right[...], 0, 0)

    whole = shape((4, grads.shape[2], normed.shape[1]), F32)
    return run(body, (grads, normed, other), "vhh", (whole,), "h")[0]


def spatial_probs(qkv, attn_moved, heads, groups, mp):
    rows, width = attn_moved.shape

    def body(t):
        q, k = t.get(0)[0], t.get(0)[1]
        for h in range(heads):
            t.outs[0][h] = probs_of(q, k, h, None)
        order = row_order(rows, mp, groups, rows // (groups * mp))
        t.outs[1][...] = mm(order, t.get(1)[...], 1, 0).astype(BF)

    outs = (shape((heads, rows, rows), F32), shape((rows, width)))
    return run(body, (qkv, attn_moved), "vv", outs, "vv")


def out_chunks(parts, attn, groups):
    own_rows, dim = parts[0].shape
    mp, width = len(parts), attn.shape[1]

    def body(t):
        dh = t.outs[0]
        for r in range(mp):
            dh[own_block(r, own_rows), :] = t.get(r)[...]
        if groups == 8:
            flat = t.get(mp)[...].T
            for at, relative in ((1, OUT_SENT), (2, OUT_KEPT)):
                for i, r in enumerate(relative):
                    t.outs[at][i] = chunk_of(flat, dh, r, groups)

    outs = (shape((mp * own_rows, dim)),)
    if groups == 8:
        outs += (shape((groups // 2, width, dim // groups)),) * 2
    return run(body, (*parts, attn), "v" * (mp + 1), outs, "v" * len(outs))


def qkv_parts(grads):
    flat = jnp.concatenate([grad.T for grad in grads], 0)
    first = 7 * flat.shape[0] // 12
    return flat[:first], flat[first:]


def qkv_chunks(t, first, chosen, grads, normed, groups):
    for at, (flat, relative) in enumerate(zip(qkv_parts(grads), chosen)):
        for i, r in enumerate(relative):
            t.outs[first + at][i] = chunk_of(flat, normed, r, groups)


def qkv_part_shapes(width, dim, groups):
    first = 7 * 3 * width // 12
    return tuple(
        shape((groups // 2, rows, dim // groups)) for rows in (first, 3 * width - first)
    )


def spatial_back(dh, w_so, qkv, probs, normed, heads, groups):
    rows, dim = dh.shape
    width = w_so.shape[0]

    def body(t):
        up = mm(t.get(0)[...], t.get(1)[...], 1, 1).astype(BF)
        qkv_ref = t.get(2)
        grads = attend_back(
            qkv_ref[0], qkv_ref[1], qkv_ref[2], up, heads, lambda h: t.get(3)[h], False
        )[:3]
        for j in range(3):
            t.outs[0][j] = grads[j]
        if groups == 8:
            qkv_chunks(t, 1, SENT, grads, t.get(4), groups)

    outs = (shape((3, rows, width)),)
    if groups == 8:
        outs += qkv_part_shapes(width, dim, groups)
    return run(body, (dh, w_so, qkv, probs, normed), "vvvvh", outs, "v" * len(outs))


def qkv_keeps(grads, normed, groups, flops):
    def body(t):
        qkv_chunks(t, 0, KEPT, [t.get(0)[j] for j in range(3)], t.get(1), groups)

    outs = qkv_part_shapes(grads.shape[2], normed.shape[1], groups)
    return run(body, (grads, normed), "vv", outs, "vv", flops=flops)


def normed_back(grads, w_qkv, mp):
    rows, dim = grads.shape[1], w_qkv.shape[1]
    own_rows = rows // mp

    def body(t):
        (back,) = t.scratch
        total = jnp.zeros((rows, dim), F32)
        for j in range(3):
            total += mm(t.get(0)[j], t.get(1)[j], 1, 1)
        back[...] = total.astype(BF)
        for r in range(mp):
            t.outs[1 - r % 2][r // 2] = back[own_block(r, own_rows), :]

    half = shape((mp // 2, own_rows, dim))
    return run(
        body, (grads, w_qkv), "vv", (half, half), "vv", scratch=(pltpu.VMEM((rows, dim), BF),)
    )


def halve(keeps, cames, keep_in="v", out="v", merged=False):
    n, depth = len(keeps), keeps[0].shape[0]
    rows = [keep.shape[1] for keep in keeps]
    chunk = keeps[0].shape[2]

    def body(t):
        for i in range(depth - 1, -1, -1):
            for at in range(n):
                total = t.get(at)[i].astype(F32) + t.get(n + at)[i].astype(F32)
                kept, first = 1 - i % 2, sum(rows[:at])
                if merged:
                    t.outs[kept][first : first + rows[at]] = total.astype(BF)
                else:
                    t.outs[n * kept + at][i // 2] = total.astype(BF)

    if merged:
        outs = (shape((sum(rows), chunk)),) * 2
    else:
        outs = tuple(shape((depth // 2, r, chunk)) for r in rows) * 2
    where = keep_in * n + "v" * n
    return run(body, (*keeps, *cames), where, outs, out * len(outs))


def last_sums(pairs):
    chunk = pairs[0][0].shape[-1]
    pairs = [tuple(part.reshape(-1, chunk) for part in pair) for pair in pairs]
    width = sum(pair[0].shape[0] for pair in pairs) // 4

    def body(t):
        row = 0
        for at, (keep, _) in enumerate(pairs):
            start = 0
            while start < keep.shape[0]:
                size = min(width - row % width, keep.shape[0] - start)
                here = slice(start, start + size)
                total = t.get(2 * at)[here].astype(F32) + t.get(2 * at + 1)[here].astype(F32)
                side = slice(row % width, row % width + size)
                if row < 3 * width:
                    t.outs[0][row // width, :, side] = total.T
                else:
                    t.outs[1][side, :] = total
                start, row = start + size, row + size

    ins = [part for pair in pairs for part in pair]
    outs = (shape((3, chunk, width), F32), shape((width, chunk), F32))
    return run(body, ins, "v" * len(ins), outs, "hh")


def reduce_whole(flat, normed, other):
    whole = weight_grads_whole(flat, normed, other)
    mine = lax.psum_scatter(whole, "frames", scatter_dimension=2, tiled=True)
    return jnp.swapaxes(mine[:3], 1, 2), mine[3]


def shards(
    video_tokens, grad_output, spatial_qkv, spatial_out, temporal_qkv, temporal_out, clip_frames
):
    frames_dev, rows_mp, dim = video_tokens.shape
    width = spatial_out.shape[0]
    heads = width // HD
    groups = lax.axis_size("frames")
    mp = lax.axis_size("mp")
    patches = rows_mp * mp
    per = rows_mp // groups
    assert frames_dev == 1 and rows_mp % groups == 0 and mp == 4

    halves = groups == 8
    x_own, g_own = video_tokens[0], grad_output[0]
    x_one, x_two = swap(x_own, "mp", 1), swap(x_own, "mp", 2)
    xg, w_spatial = joined(x_own, g_own, spatial_qkv)
    xg, x_one, x_two, so_own = lax.optimization_barrier((xg, x_one, x_two, spatial_out))
    x_three = swap(x_two, "mp", 1)
    xg = lax.all_to_all(xg.reshape(groups, per, 2 * dim), "frames", 0, 0, tiled=True)
    xg = xg.reshape(rows_mp, 2 * dim)
    so_two = swap(so_own, "mp", 2)

    normed_x, qkv_s, attn_send = spatial_forward(
        (x_own, x_one, x_two, x_three), w_spatial, heads, groups
    )
    attn_send, xg = lax.optimization_barrier((attn_send, xg))
    xg_two = swap(xg, "mp", 2)
    moved = lax.all_to_all(
        attn_send.reshape(groups, mp * per, width), "frames", 0, 0, tiled=True
    ).reshape(patches, width)
    so_two, moved = lax.optimization_barrier((so_two, moved))
    moved_one, moved_two = swap(moved, "mp", 1), swap(moved, "mp", 2)
    so_one = swap(spatial_out, "mp", 1)
    xg_all = xg, swap(xg, "mp", 1), xg_two, swap(xg_two, "mp", 1)
    rows_own = owner_rows(
        xg_all, temporal_out, (moved, moved_one), (spatial_out, so_one), groups, per
    )
    moved_two, rows_own = lax.optimization_barrier((moved_two, rows_own))
    so_far, g_rows, d_attn_t = rows_own

    send_h, keep_h, normed_h, unit_own, inv_own, t_grads, *t_sent = temporal_stage(
        (moved_two, swap(moved_two, "mp", 1)), so_far, g_rows, d_attn_t,
        (so_two, swap(so_two, "mp", 1)), temporal_qkv, clip_frames, heads, groups, per, mp,
    )
    parts, t_sent = head_sums(send_h, keep_h, t_sent)
    if halves:
        t_kept = weight_grads_half(t_grads, normed_h, g_rows, groups, 50_000_000_000)
        parts, t_kept = lax.optimization_barrier((parts, t_kept))
        came = [swap(t_sent[0], "frames", 1), swap(t_sent[1], "frames", 2)]
        t_sums = halve(t_kept, came, out="h")
    d_hidden = hidden_back(parts, unit_own, inv_own, xg)
    d_hidden = lax.all_to_all(
        d_hidden.reshape(groups, per, dim), "frames", 0, 0, tiled=True
    ).reshape(rows_mp, dim)
    if halves:
        d_hidden, t_sums = lax.optimization_barrier((d_hidden, t_sums))
        t_second = [swap(t_sums[0], "frames", 2), swap(t_sums[1], "frames", 1)]
    dh_one, dh_two = swap(d_hidden, "mp", 1), swap(d_hidden, "mp", 2)
    d_hidden, qkv_s, attn_send = lax.optimization_barrier((d_hidden, qkv_s, attn_send))
    probs_s, attn_s = spatial_probs(qkv_s, attn_send, heads, groups, mp)
    dh_two, probs_s, attn_s = lax.optimization_barrier((dh_two, probs_s, attn_s))
    dh_three = swap(dh_two, "mp", 1)
    d_hidden_all, *o_chunks = out_chunks((d_hidden, dh_one, dh_two, dh_three), attn_s, groups)
    dh_ready = d_hidden_all
    if halves:
        dh_ready, t_second = lax.optimization_barrier((dh_ready, t_second))
        t_send, t_keep = halve(t_sums[2:], t_second, keep_in="h", merged=True)
        dh_ready, t_send, t_keep = lax.optimization_barrier((dh_ready, t_send, t_keep))
        t_came = swap(t_send, "frames", 4)
    else:
        t_qkv, t_out = reduce_whole(t_grads, normed_h, g_rows)
    s_grads, *s_sent = spatial_back(
        dh_ready, spatial_out, qkv_s, probs_s, normed_x, heads, groups
    )
    if halves:
        after = lax.optimization_barrier
        send_x, keep_x = normed_back(s_grads, spatial_qkv, mp)
        s_grads, send_x, keep_x, t_came = after((s_grads, send_x, keep_x, t_came))
        t_qkv, t_out = last_sums([(t_keep, t_came)])
        s_kept = qkv_keeps(s_grads, normed_x, groups, 50_000_000_000)
        came = [swap(s_sent[0], "frames", 1), swap(s_sent[1], "frames", 2)]
        came.append(swap(o_chunks[0], "frames", 1))
        *sends, keep_a, keep_b, o_keep = halve([*s_kept, o_chunks[1]], came)
        came = [swap(send, "frames", by) for send, by in zip(sends, (2, 1, 4))]
        s_send, s_keep = halve([keep_a, keep_b], came[:2], merged=True)
        o_send, o_keep = halve([o_keep], came[2:])
        s_qkv, s_out = last_sums([
            (s_keep, swap(s_send, "frames", 4)), (o_keep, swap(o_send, "frames", 2))
        ])
    else:
        send_x, keep_x = normed_back(s_grads, spatial_qkv, mp)
        all_grads = jnp.concatenate([s_grads, attn_s[None]], 0)
        s_qkv, s_out = reduce_whole(all_grads, normed_x, d_hidden_all)
    grad_tokens = tokens_back(head_sums(send_x, keep_x)[0], x_own, d_hidden)
    return grad_tokens[None], s_qkv, s_out, t_qkv, t_out


def solution(mesh):
    placed = (
        P("frames", "mp", None),
        P("frames", "mp", None),
        P(None, None, "mp"),
        P("mp", None),
        P(None, None, "mp"),
        P("mp", None),
        P(),
    )
    return jax.shard_map(
        shards,
        mesh=mesh,
        in_specs=placed,
        out_specs=(
            P("frames", "mp", None),
            P(None, "frames", "mp"),
            P("mp", "frames"),
            P(None, "frames", "mp"),
            P("mp", "frames"),
        ),
        check_vma=False,
    )
```

```python
import jax
import jax.numpy as jnp
from jax import lax
from jax.experimental import pallas as pl
from jax.experimental.pallas import tpu as pltpu
from jax.sharding import PartitionSpec as P

HD = 64
EPS = 1e-06
NEGATIVE = -1e30
BF = jnp.bfloat16
F32 = jnp.float32
VMEM_LIMIT = 20 * 1024 * 1024


def mm(a, b, ca, cb):
    return lax.dot_general(a, b, (((ca,), (cb,)), ((), ())), preferred_element_type=F32)


def shape(dims, dtype=BF):
    return jax.ShapeDtypeStruct(dims, dtype)


def flipped(index, by, bits):
    total = index
    for b in range(bits):
        if (by >> b) & 1:
            total = total + (1 << b) * (1 - 2 * ((index // (1 << b)) % 2))
    return total


def swap(value, axis, by):
    size = lax.axis_size(axis)
    return lax.ppermute(value, axis, [(i, i ^ by) for i in range(size)])


class Kernel:
    def __init__(self, get, outs, put, smem, scratch, sems, early):
        self.get, self.outs, self.put = get, outs, put
        self.smem, self.scratch, self.sems, self.early = smem, scratch, sems, early

    def copy(self, src, dst):
        made = pltpu.make_async_copy(src, dst, self.sems.pop(0))
        made.start()
        return made


def run(
    body, ins, where, outs, out_where, smem=(), scratch=(), copies=0, early=None, flops=1000
):
    n, k, s = len(ins), len(outs), len(smem)
    staged_in = [i for i in range(n) if where[i] in "ha"]
    staged_out = [i for i in range(k) if out_where[i] in "ha"]

    def wrapped(*refs):
        refs = list(refs)

        def take(count):
            part = refs[:count]
            del refs[:count]
            return part

        scalars, src, dst = take(s), take(n), take(k)
        in_bufs, out_bufs = take(len(staged_in)), take(len(staged_out))
        in_sem, out_sem, own_sem = take(3)
        loads, stores = {}, {}
        results = list(dst)
        for at, i in enumerate(staged_out):
            results[i] = out_bufs[at]
        held = {i: in_bufs[at] for at, i in enumerate(staged_in)}
        waited = set()

        def get(i):
            if i not in held:
                return src[i]
            if i not in waited:
                loads[i].wait()
                waited.add(i)
            return held[i]

        def put(i):
            if i in staged_out and i not in stores:
                at = staged_out.index(i)
                stores[i] = pltpu.make_async_copy(out_bufs[at], dst[i], out_sem.at[at])
                stores[i].start()

        sems = [own_sem.at[i] for i in range(copies)]
        tools = Kernel(get, results, put, scalars, refs, sems, None)
        if early is not None:
            tools.early = early(tools)
        for at, i in enumerate(staged_in):
            loads[i] = pltpu.make_async_copy(src[i], in_bufs[at], in_sem.at[at])
            loads[i].start()
        body(tools)
        for i in staged_in:
            get(i)
        for i in range(k):
            put(i)
        for copy in stores.values():
            copy.wait()

    specs = {"v": pltpu.VMEM, "h": pltpu.HBM, "a": pl.ANY, "n": pl.ANY, "x": pltpu.HBM}
    specs = {key: pl.BlockSpec(memory_space=space) for key, space in specs.items()}
    buffers = [pltpu.VMEM(ins[i].shape, ins[i].dtype) for i in staged_in]
    buffers += [pltpu.VMEM(outs[i].shape, outs[i].dtype) for i in staged_out]
    ins = [
        pltpu.with_memory_space_constraint(a, pltpu.HBM) if w in "hx" else a
        for a, w in zip(ins, where)
    ]
    return pl.pallas_call(
        wrapped,
        out_shape=tuple(
            pltpu.HBM(o.shape, o.dtype) if w in "hx" else o for o, w in zip(outs, out_where)
        ),
        in_specs=[pl.BlockSpec(memory_space=pltpu.SMEM)] * s
        + [specs[w] for w in where],
        out_specs=tuple(specs[w] for w in out_where),
        scratch_shapes=buffers
        + [pltpu.SemaphoreType.DMA((max(1, c),)) for c in (len(staged_in), len(staged_out), copies)]
        + list(scratch),
        compiler_params=pltpu.CompilerParams(vmem_limit_bytes=VMEM_LIMIT),
        cost_estimate=pl.CostEstimate(flops=flops, bytes_accessed=1000, transcendentals=0),
    )(*smem, *ins)


def inv_rms(v):
    return lax.rsqrt(jnp.mean(v * v, -1, keepdims=True) + EPS)


SCALE = HD ** (-0.5)
assert SCALE == 0.125


def head_mask(width, head, scale=1.0):
    lane = lax.broadcasted_iota(jnp.int32, (1, width), 1)
    mask = ((lane >= head * HD) & (lane < (head + 1) * HD)).astype(F32)
    return (mask * scale).astype(BF)


def probs_of(q, k, head, allowed):
    scores = mm(q * head_mask(q.shape[1], head, SCALE), k, 1, 1)
    if allowed is not None:
        scores = jnp.where(allowed, scores, NEGATIVE)
    expo = jnp.exp(scores - jnp.max(scores, -1, keepdims=True))
    return expo * (1.0 / jnp.sum(expo, -1, keepdims=True))


def attend(q, k, v, heads):
    total = jnp.zeros(q.shape, F32)
    for h in range(heads):
        mask = head_mask(q.shape[1], h)
        probs = probs_of(q, k, h, None)
        total += mm(probs.astype(BF), v * mask, 1, 0)
    return total.astype(BF)


def attend_back(q, k, v, up, heads, probs_at, with_out):
    zero = jnp.zeros(q.shape, F32)
    out, dq, dk, dv = zero, zero, zero, zero
    v_scaled = v * jnp.full((1, 1), SCALE, BF)
    for h in range(heads):
        mask = head_mask(q.shape[1], h)
        up_head = up * mask
        probs = probs_at(h)
        probs_b = probs.astype(BF)
        if with_out:
            out += mm(probs_b, v * mask, 1, 0)
        dv += mm(probs_b, up_head, 0, 0)
        dp = mm(up_head, v_scaled, 1, 1)
        delta = jnp.sum(probs * dp, -1, keepdims=True)
        ds = (probs * (dp - delta)).astype(BF)
        dq += mm(ds, k * mask, 1, 0)
        dk += mm(ds, q * mask, 0, 0)
    return dq.astype(BF), dk.astype(BF), dv.astype(BF), out.astype(BF)


def row_order(rows, outer, middle, inner):
    to = lax.broadcasted_iota(jnp.int32, (rows, 1), 0)
    at = lax.broadcasted_iota(jnp.int32, (1, rows), 1)
    o, m, i = to // (middle * inner), (to // inner) % middle, to % inner
    return (at == (m * outer + o) * inner + i).astype(F32).astype(BF)


def own_block(r, rows):
    start = flipped(lax.axis_index("mp"), r, 2) * rows
    return pl.ds(pl.multiple_of(start, rows), rows)


def joined(x, grad):
    rows, dim = x.shape

    def body(t):
        for i in range(2):
            t.outs[0][:, i * dim : (i + 1) * dim] = t.get(i)[...]

    return run(body, (x, grad), "hh", (shape((rows, 2 * dim)),), "v")[0]


def spatial_forward(parts, weights, heads, groups):
    own_rows, dim = parts[0].shape
    mp, width = len(parts), weights.shape[2]
    rows = mp * own_rows

    def body(t):
        for r in (*range(1, mp), 0):
            xf = t.get(r)[...].astype(F32)
            t.outs[0][own_block(r, own_rows), :] = (xf * inv_rms(xf)).astype(BF)
        nx = t.outs[0][...]
        t.put(0)
        w = t.get(mp)
        q, k, v = [mm(nx, w[j], 1, 0).astype(BF) for j in range(3)]
        for j, part in enumerate((q, k, v)):
            t.outs[1][j] = part
        t.put(1)
        attn = attend(q, k, v, heads)
        order = row_order(rows, groups, mp, rows // (groups * mp))
        t.outs[2][...] = mm(order, attn, 1, 0).astype(BF)

    outs = (shape((rows, dim)), shape((3, rows, width)), shape((rows, width)))
    return run(
        body, (*parts, weights), "h" + "v" * (mp - 1) + "h", outs, "hhv"
    )


def owner_rows(xg, w_to, attn, w_so, frames, per):
    own_rows, mp = xg[0].shape[0], len(xg)
    rows, (width, dim) = mp * own_rows, w_to.shape

    def body(t):
        x_buf = t.scratch[0]
        for r in range(mp):
            at = own_block(r, own_rows)
            x_buf[at, :] = t.get(r)[:, :dim]
            t.outs[1][at, :] = t.get(r)[:, dim:]
        total = x_buf[...].astype(F32)
        order = row_order(rows, mp, frames, per)
        for i in range(len(attn)):
            part = mm(order, t.get(mp + 1 + i)[...], 1, 0).astype(BF)
            total += mm(part, t.get(mp + 1 + len(attn) + i)[...], 1, 0)
        t.outs[0][...] = total
        t.outs[2][...] = mm(t.outs[1][...], t.get(mp)[...], 1, 1).astype(BF)

    outs = (shape((rows, dim), F32), shape((rows, dim)), shape((rows, width)))
    ins = (*xg, w_to, *attn, *w_so)
    where = "v" * mp + "h" + "v" * len(attn) + "h" + "v" * (len(w_so) - 1)
    return run(body, ins, where, outs, "vvv", scratch=(pltpu.VMEM((rows, dim), BF),))


SENT = ((1, 3, 5, 7), (2, 3, 6, 7))
KEPT = ((0, 2, 4, 6), (0, 1, 4, 5))
OUT_SENT, OUT_KEPT = (1, 5, 3, 7), (0, 4, 2, 6)


def chunk_of(flat, right, r, groups):
    chunk = right.shape[1] // groups
    start = pl.multiple_of(flipped(lax.axis_index("frames"), r, 3) * chunk, chunk)
    return mm(flat, right[:, pl.ds(start, chunk)], 1, 0).astype(BF)


def chunk_grads(t, first, chosen, grads, normed, other, groups):
    flat = [grad.T for grad in grads]
    right = (normed, normed, normed, other)
    for pair, relative in enumerate(chosen):
        for i, r in enumerate(relative):
            for j in range(2):
                at = 2 * pair + j
                side = slice(j * flat[at].shape[0], (j + 1) * flat[at].shape[0])
                t.outs[first + pair][i, side] = chunk_of(flat[at], right[at], r, groups)


def half_shape(width, dim, groups):
    return shape((groups // 2, 2 * width, dim // groups))


def temporal_stage(attn, so_far, g_all, up, w_so, w_qkv, clips, heads, frames, per, mp):
    n, (rows, width) = len(attn), attn[0].shape
    own_rows = rows // mp
    dim = so_far.shape[1]
    halves = frames == 8

    def rows_of(r):
        return own_block(r, own_rows)

    def body(t):
        (clip_ref,) = t.smem
        back, inv_buf = t.scratch
        total = t.get(n)[...]
        order = row_order(rows, mp, frames, per)
        for r in range(n):
            part = mm(order, t.get(r)[...], 1, 0).astype(BF)
            total += mm(part, t.get(n + 2 + r)[...], 1, 0)
        inv = inv_rms(total)
        nh = (total * inv).astype(BF)
        t.outs[2][...] = nh
        inv_buf[...] = jnp.broadcast_to(inv, inv_buf.shape)
        t.outs[3][...] = t.outs[2][rows_of(0), :]
        t.outs[4][...] = inv_buf[rows_of(0), :]

        def key_of(axis):
            dims = (rows, 1) if axis == 0 else (1, rows)
            token = lax.broadcasted_iota(jnp.int32, dims, axis)
            block = token // per
            frame = block % frames
            patch = (block // frames) * per + token % per
            end = jnp.int32(0)
            clip = jnp.zeros(dims, jnp.int32)
            for c in range(clips.shape[0]):
                end = end + clip_ref[c]
                clip += (frame >= end).astype(jnp.int32)
            return clip * rows + patch

        allowed = key_of(0) == key_of(1)
        w = t.get(2 * n + 2)
        q, k, v = [mm(nh, w[j], 1, 0).astype(BF) for j in range(3)]
        grads = attend_back(
            q, k, v, t.get(n + 1)[...], heads, lambda h: probs_of(q, k, h, allowed), True
        )
        for j in range(4):
            t.outs[5][j] = grads[j]
        d_normed = jnp.zeros((rows, dim), F32)
        for j in range(3):
            d_normed += mm(grads[j], w[j], 1, 1)
        back[...] = d_normed.astype(BF)
        for r in range(mp):
            t.outs[1 - r % 2][r // 2] = back[rows_of(r), :]
        if halves:
            chunk_grads(t, 6, SENT, grads, t.outs[2], t.get(2 * n + 3), frames)

    half = shape((mp // 2, own_rows, dim))
    outs = (
        half,
        half,
        shape((rows, dim)),
        shape((own_rows, dim)),
        shape((own_rows, 128), F32),
        shape((4, rows, width)),
    )
    if halves:
        outs += (half_shape(width, dim, frames),) * 2
    ins = (*attn, so_far, up, *w_so, w_qkv, g_all)
    return run(
        body, ins, "v" * len(ins), outs, "v" * len(outs), smem=(clips,),
        scratch=(pltpu.VMEM((rows, dim), BF), pltpu.VMEM((rows, 128), F32)),
    )


def head_sums(send, keep):
    def body(t):
        t.outs[0][...] = (t.get(0)[1].astype(F32) + t.get(1)[1].astype(F32)).astype(BF)

    came = swap(send, "mp", 1)
    (pair,) = run(body, (keep, came), "vv", (shape(keep.shape[1:]),), "v")
    return keep, came, swap(pair, "mp", 2)


def summed(t):
    return t.get(0)[0].astype(F32) + t.get(1)[0].astype(F32) + t.get(2)[...].astype(F32)


def hidden_back(parts, unit, inv, grad):
    dim = unit.shape[1]

    def body(t):
        total, nh = summed(t), t.get(3)[...].astype(F32)
        rest = total - nh * jnp.mean(total * nh, -1, keepdims=True)
        g = t.get(5)[:, dim:].astype(F32)
        t.outs[0][...] = (g + t.get(4)[:, :1] * rest).astype(BF)

    return run(body, (*parts, unit, inv, grad), "vvvvvv", (shape(unit.shape),), "v")[0]


def tokens_back(parts, x, grad):
    def body(t):
        total, xf = summed(t), t.get(3)[...].astype(F32)
        inv = inv_rms(xf)
        nx = xf * inv
        rest = total - nx * jnp.mean(total * nx, -1, keepdims=True)
        t.outs[0][...] = (t.get(4)[...].astype(F32) + inv * rest).astype(BF)

    return run(body, (*parts, x, grad), "vvvvv", (shape(x.shape),), "v")[0]


def weight_grads_half(grads, normed, other, groups, flops=1000):
    def body(t):
        left = [t.get(0)[j] for j in range(4)]
        chunk_grads(t, 0, KEPT, left, t.get(1), t.get(2), groups)

    half = half_shape(grads.shape[2], normed.shape[1], groups)
    return run(body, (grads, normed, other), "vvv", (half, half), "vv", flops=flops)


def weight_grads_whole(grads, normed, other):
    def body(t):
        for j in range(4):
            right = t.get(2) if j == 3 else t.get(1)
            t.outs[0][j] = mm(t.get(0)[j], right[...], 0, 0)

    whole = shape((4, grads.shape[2], normed.shape[1]), F32)
    return run(body, (grads, normed, other), "vhh", (whole,), "h")[0]


def spatial_probs(qkv, attn_moved, heads, groups, mp):
    rows, width = attn_moved.shape

    def body(t):
        q, k = t.get(0)[0], t.get(0)[1]
        for h in range(heads):
            t.outs[0][h] = probs_of(q, k, h, None)
        order = row_order(rows, mp, groups, rows // (groups * mp))
        t.outs[1][...] = mm(order, t.get(1)[...], 1, 0).astype(BF)

    outs = (shape((heads, rows, rows), F32), shape((rows, width)))
    return run(body, (qkv, attn_moved), "vv", outs, "vv")


def out_chunks(parts, attn, groups):
    own_rows, dim = parts[0].shape
    mp, width = len(parts), attn.shape[1]

    def body(t):
        dh = t.outs[0]
        for r in range(mp):
            dh[own_block(r, own_rows), :] = t.get(r)[...]
        if groups == 8:
            flat = t.get(mp)[...].T
            for at, relative in ((1, OUT_SENT), (2, OUT_KEPT)):
                for i, r in enumerate(relative):
                    t.outs[at][i] = chunk_of(flat, dh, r, groups)

    outs = (shape((mp * own_rows, dim)),)
    if groups == 8:
        outs += (shape((groups // 2, width, dim // groups)),) * 2
    return run(body, (*parts, attn), "v" * (mp + 1), outs, "v" * len(outs))


def qkv_parts(grads):
    flat = jnp.concatenate([grad.T for grad in grads], 0)
    first = 13 * flat.shape[0] // 24
    return flat[:first], flat[first:]


def qkv_chunks(t, first, chosen, grads, normed, groups):
    for at, (flat, relative) in enumerate(zip(qkv_parts(grads), chosen)):
        for i, r in enumerate(relative):
            t.outs[first + at][i] = chunk_of(flat, normed, r, groups)


def qkv_part_shapes(width, dim, groups):
    first = 13 * 3 * width // 24
    return tuple(
        shape((groups // 2, rows, dim // groups)) for rows in (first, 3 * width - first)
    )


def spatial_back(dh, w_so, qkv, probs, normed, heads, groups):
    rows, dim = dh.shape
    width = w_so.shape[0]

    def body(t):
        up = mm(t.get(0)[...], t.get(1)[...], 1, 1).astype(BF)
        qkv_ref = t.get(2)
        grads = attend_back(
            qkv_ref[0], qkv_ref[1], qkv_ref[2], up, heads, lambda h: t.get(3)[h], False
        )[:3]
        for j in range(3):
            t.outs[0][j] = grads[j]
        if groups == 8:
            qkv_chunks(t, 1, SENT, grads, t.get(4), groups)

    outs = (shape((3, rows, width)),)
    if groups == 8:
        outs += qkv_part_shapes(width, dim, groups)
    return run(body, (dh, w_so, qkv, probs, normed), "vvvvh", outs, "v" * len(outs))


def qkv_keeps(grads, normed, groups, flops):
    def body(t):
        qkv_chunks(t, 0, KEPT, [t.get(0)[j] for j in range(3)], t.get(1), groups)

    outs = qkv_part_shapes(grads.shape[2], normed.shape[1], groups)
    return run(body, (grads, normed), "vv", outs, "vv", flops=flops)


def normed_back(grads, w_qkv, mp):
    rows, dim = grads.shape[1], w_qkv.shape[1]
    own_rows = rows // mp

    def body(t):
        (back,) = t.scratch
        total = jnp.zeros((rows, dim), F32)
        for j in range(3):
            total += mm(t.get(0)[j], t.get(1)[j], 1, 1)
        back[...] = total.astype(BF)
        for r in range(mp):
            t.outs[1 - r % 2][r // 2] = back[own_block(r, own_rows), :]

    half = shape((mp // 2, own_rows, dim))
    return run(
        body, (grads, w_qkv), "vv", (half, half), "vv", scratch=(pltpu.VMEM((rows, dim), BF),)
    )


def halve(keeps, cames, keep_in="v", out="v", merged=False):
    n, depth = len(keeps), keeps[0].shape[0]
    rows = [keep.shape[1] for keep in keeps]
    chunk = keeps[0].shape[2]

    def body(t):
        for i in range(depth - 1, -1, -1):
            for at in range(n):
                total = t.get(at)[i].astype(F32) + t.get(n + at)[i].astype(F32)
                kept, first = 1 - i % 2, sum(rows[:at])
                if merged:
                    t.outs[kept][first : first + rows[at]] = total.astype(BF)
                else:
                    t.outs[n * kept + at][i // 2] = total.astype(BF)

    if merged:
        outs = (shape((sum(rows), chunk)),) * 2
    else:
        outs = tuple(shape((depth // 2, r, chunk)) for r in rows) * 2
    where = keep_in * n + "v" * n
    return run(body, (*keeps, *cames), where, outs, out * len(outs))


def last_sums(pairs):
    chunk = pairs[0][0].shape[-1]
    pairs = [tuple(part.reshape(-1, chunk) for part in pair) for pair in pairs]
    width = sum(pair[0].shape[0] for pair in pairs) // 4

    def body(t):
        row = 0
        for at, (keep, _) in enumerate(pairs):
            start = 0
            while start < keep.shape[0]:
                size = min(width - row % width, keep.shape[0] - start)
                here = slice(start, start + size)
                total = t.get(2 * at)[here].astype(F32) + t.get(2 * at + 1)[here].astype(F32)
                side = slice(row % width, row % width + size)
                if row < 3 * width:
                    t.outs[0][row // width, :, side] = total.T
                else:
                    t.outs[1][side, :] = total
                start, row = start + size, row + size

    ins = [part for pair in pairs for part in pair]
    outs = (shape((3, chunk, width), F32), shape((width, chunk), F32))
    return run(body, ins, "v" * len(ins), outs, "hh")


def reduce_whole(flat, normed, other):
    whole = weight_grads_whole(flat, normed, other)
    mine = lax.psum_scatter(whole, "frames", scatter_dimension=2, tiled=True)
    return jnp.swapaxes(mine[:3], 1, 2), mine[3]


def shards(
    video_tokens, grad_output, spatial_qkv, spatial_out, temporal_qkv, temporal_out, clip_frames
):
    frames_dev, rows_mp, dim = video_tokens.shape
    width = spatial_out.shape[0]
    heads = width // HD
    groups = lax.axis_size("frames")
    mp = lax.axis_size("mp")
    patches = rows_mp * mp
    per = rows_mp // groups
    assert frames_dev == 1 and rows_mp % groups == 0 and mp == 4

    halves = groups == 8
    x_own, g_own = video_tokens[0], grad_output[0]
    x_one, x_two = swap(x_own, "mp", 1), swap(x_own, "mp", 2)
    xg, x_one, x_two, so_own = lax.optimization_barrier(
        (joined(x_own, g_own), x_one, x_two, spatial_out)
    )
    x_three = swap(x_two, "mp", 1)
    xg = lax.all_to_all(xg.reshape(groups, per, 2 * dim), "frames", 0, 0, tiled=True)
    xg = xg.reshape(rows_mp, 2 * dim)
    so_two = swap(so_own, "mp", 2)

    normed_x, qkv_s, attn_send = spatial_forward(
        (x_own, x_one, x_two, x_three), spatial_qkv, heads, groups
    )
    attn_send, xg = lax.optimization_barrier((attn_send, xg))
    xg_two = swap(xg, "mp", 2)
    moved = lax.all_to_all(
        attn_send.reshape(groups, mp * per, width), "frames", 0, 0, tiled=True
    ).reshape(patches, width)
    so_two, moved = lax.optimization_barrier((so_two, moved))
    moved_one, moved_two = swap(moved, "mp", 1), swap(moved, "mp", 2)
    so_one = swap(spatial_out, "mp", 1)
    xg_all = xg, swap(xg, "mp", 1), xg_two, swap(xg_two, "mp", 1)
    rows_own = owner_rows(
        xg_all, temporal_out, (moved, moved_one), (spatial_out, so_one), groups, per
    )
    moved_two, rows_own = lax.optimization_barrier((moved_two, rows_own))
    so_far, g_rows, d_attn_t = rows_own

    send_h, keep_h, normed_h, unit_own, inv_own, t_grads, *t_sent = temporal_stage(
        (moved_two, swap(moved_two, "mp", 1)), so_far, g_rows, d_attn_t,
        (so_two, swap(so_two, "mp", 1)), temporal_qkv, clip_frames, heads, groups, per, mp,
    )
    parts = head_sums(send_h, keep_h)
    if halves:
        t_kept = weight_grads_half(t_grads, normed_h, g_rows, groups)
        parts, t_kept = lax.optimization_barrier((parts, t_kept))
        came = [swap(t_sent[0], "frames", 1), swap(t_sent[1], "frames", 2)]
        t_sums = halve(t_kept, came, out="h")
    d_hidden = hidden_back(parts, unit_own, inv_own, xg)
    d_hidden = lax.all_to_all(
        d_hidden.reshape(groups, per, dim), "frames", 0, 0, tiled=True
    ).reshape(rows_mp, dim)
    if halves:
        d_hidden, t_sums = lax.optimization_barrier((d_hidden, t_sums))
        t_second = [swap(t_sums[0], "frames", 2), swap(t_sums[1], "frames", 1)]
    dh_one, dh_two = swap(d_hidden, "mp", 1), swap(d_hidden, "mp", 2)
    d_hidden, qkv_s, attn_send = lax.optimization_barrier((d_hidden, qkv_s, attn_send))
    probs_s, attn_s = spatial_probs(qkv_s, attn_send, heads, groups, mp)
    dh_two, probs_s, attn_s = lax.optimization_barrier((dh_two, probs_s, attn_s))
    dh_three = swap(dh_two, "mp", 1)
    d_hidden_all, *o_chunks = out_chunks((d_hidden, dh_one, dh_two, dh_three), attn_s, groups)
    dh_ready = d_hidden_all
    if halves:
        dh_ready, t_second = lax.optimization_barrier((dh_ready, t_second))
        t_send, t_keep = halve(t_sums[2:], t_second, keep_in="h", merged=True)
        dh_ready, t_send, t_keep = lax.optimization_barrier((dh_ready, t_send, t_keep))
        t_came = swap(t_send, "frames", 4)
    else:
        t_qkv, t_out = reduce_whole(t_grads, normed_h, g_rows)
    s_grads, *s_sent = spatial_back(
        dh_ready, spatial_out, qkv_s, probs_s, normed_x, heads, groups
    )
    if halves:
        after = lax.optimization_barrier
        send_x, keep_x = normed_back(s_grads, spatial_qkv, mp)
        o_send, o_keep = halve([o_chunks[1]], [swap(o_chunks[0], "frames", 1)])
        s_grads, send_x, keep_x, t_came, o_send, o_keep = after(
            (s_grads, send_x, keep_x, t_came, o_send, o_keep)
        )
        o_came = swap(o_send, "frames", 4)
        t_qkv, t_out = last_sums([(t_keep, t_came)])
        s_kept = qkv_keeps(s_grads, normed_x, groups, 50_000_000_000)
        came = [swap(s_sent[0], "frames", 1), swap(s_sent[1], "frames", 2)]
        send_a, send_b, keep_a, keep_b = halve(s_kept, came)
        came = [swap(send_a, "frames", 2), swap(send_b, "frames", 1)]
        s_send, s_keep = halve([keep_a, keep_b], came, merged=True)
        o_send, o_keep = halve([o_keep], [o_came])
        s_qkv, s_out = last_sums([
            (s_keep, swap(s_send, "frames", 4)), (o_keep, swap(o_send, "frames", 2))
        ])
    else:
        send_x, keep_x = normed_back(s_grads, spatial_qkv, mp)
        all_grads = jnp.concatenate([s_grads, attn_s[None]], 0)
        s_qkv, s_out = reduce_whole(all_grads, normed_x, d_hidden_all)
    grad_tokens = tokens_back(head_sums(send_x, keep_x), x_own, d_hidden)
    return grad_tokens[None], s_qkv, s_out, t_qkv, t_out


def solution(mesh):
    placed = (
        P("frames", "mp", None),
        P("frames", "mp", None),
        P(None, None, "mp"),
        P("mp", None),
        P(None, None, "mp"),
        P("mp", None),
        P(),
    )
    return jax.shard_map(
        shards,
        mesh=mesh,
        in_specs=placed,
        out_specs=(
            P("frames", "mp", None),
            P(None, "frames", "mp"),
            P("mp", "frames"),
            P(None, "frames", "mp"),
            P("mp", "frames"),
        ),
        check_vma=False,
    )
```

```python
import jax
import jax.numpy as jnp
from jax import lax
from jax.experimental import pallas as pl
from jax.experimental.pallas import tpu as pltpu
from jax.sharding import PartitionSpec as P

HD = 64
EPS = 1e-06
NEGATIVE = -1e30
BF = jnp.bfloat16
F32 = jnp.float32
VMEM_LIMIT = 20 * 1024 * 1024


def mm(a, b, ca, cb):
    return lax.dot_general(a, b, (((ca,), (cb,)), ((), ())), preferred_element_type=F32)


def shape(dims, dtype=BF):
    return jax.ShapeDtypeStruct(dims, dtype)


def flipped(index, by, bits):
    total = index
    for b in range(bits):
        if (by >> b) & 1:
            total = total + (1 << b) * (1 - 2 * ((index // (1 << b)) % 2))
    return total


def swap(value, axis, by):
    size = lax.axis_size(axis)
    return lax.ppermute(value, axis, [(i, i ^ by) for i in range(size)])


class Kernel:
    def __init__(self, get, outs, put, smem, scratch, sems, early):
        self.get, self.outs, self.put = get, outs, put
        self.smem, self.scratch, self.sems, self.early = smem, scratch, sems, early

    def copy(self, src, dst):
        made = pltpu.make_async_copy(src, dst, self.sems.pop(0))
        made.start()
        return made


def run(
    body, ins, where, outs, out_where, smem=(), scratch=(), copies=0, early=None, flops=1000
):
    n, k, s = len(ins), len(outs), len(smem)
    staged_in = [i for i in range(n) if where[i] in "ha"]
    staged_out = [i for i in range(k) if out_where[i] in "ha"]

    def wrapped(*refs):
        refs = list(refs)

        def take(count):
            part = refs[:count]
            del refs[:count]
            return part

        scalars, src, dst = take(s), take(n), take(k)
        in_bufs, out_bufs = take(len(staged_in)), take(len(staged_out))
        in_sem, out_sem, own_sem = take(3)
        loads, stores = {}, {}
        results = list(dst)
        for at, i in enumerate(staged_out):
            results[i] = out_bufs[at]
        held = {i: in_bufs[at] for at, i in enumerate(staged_in)}
        waited = set()

        def get(i):
            if i not in held:
                return src[i]
            if i not in waited:
                loads[i].wait()
                waited.add(i)
            return held[i]

        def put(i):
            if i in staged_out and i not in stores:
                at = staged_out.index(i)
                stores[i] = pltpu.make_async_copy(out_bufs[at], dst[i], out_sem.at[at])
                stores[i].start()

        sems = [own_sem.at[i] for i in range(copies)]
        tools = Kernel(get, results, put, scalars, refs, sems, None)
        if early is not None:
            tools.early = early(tools)
        for at, i in enumerate(staged_in):
            loads[i] = pltpu.make_async_copy(src[i], in_bufs[at], in_sem.at[at])
            loads[i].start()
        body(tools)
        for i in staged_in:
            get(i)
        for i in range(k):
            put(i)
        for copy in stores.values():
            copy.wait()

    specs = {"v": pltpu.VMEM, "h": pltpu.HBM, "a": pl.ANY, "n": pl.ANY, "x": pltpu.HBM}
    specs = {key: pl.BlockSpec(memory_space=space) for key, space in specs.items()}
    buffers = [pltpu.VMEM(ins[i].shape, ins[i].dtype) for i in staged_in]
    buffers += [pltpu.VMEM(outs[i].shape, outs[i].dtype) for i in staged_out]
    ins = [
        pltpu.with_memory_space_constraint(a, pltpu.HBM) if w in "hx" else a
        for a, w in zip(ins, where)
    ]
    return pl.pallas_call(
        wrapped,
        out_shape=tuple(
            pltpu.HBM(o.shape, o.dtype) if w in "hx" else o for o, w in zip(outs, out_where)
        ),
        in_specs=[pl.BlockSpec(memory_space=pltpu.SMEM)] * s
        + [specs[w] for w in where],
        out_specs=tuple(specs[w] for w in out_where),
        scratch_shapes=buffers
        + [pltpu.SemaphoreType.DMA((max(1, c),)) for c in (len(staged_in), len(staged_out), copies)]
        + list(scratch),
        compiler_params=pltpu.CompilerParams(vmem_limit_bytes=VMEM_LIMIT),
        cost_estimate=pl.CostEstimate(flops=flops, bytes_accessed=1000, transcendentals=0),
    )(*smem, *ins)


def inv_rms(v):
    return lax.rsqrt(jnp.mean(v * v, -1, keepdims=True) + EPS)


SCALE = HD ** (-0.5)
assert SCALE == 0.125


def head_mask(width, head, scale=1.0):
    lane = lax.broadcasted_iota(jnp.int32, (1, width), 1)
    mask = ((lane >= head * HD) & (lane < (head + 1) * HD)).astype(F32)
    return (mask * scale).astype(BF)


def probs_of(q, k, head, allowed):
    scores = mm(q * head_mask(q.shape[1], head, SCALE), k, 1, 1)
    if allowed is not None:
        scores = jnp.where(allowed, scores, NEGATIVE)
    expo = jnp.exp(scores - jnp.max(scores, -1, keepdims=True))
    return expo * (1.0 / jnp.sum(expo, -1, keepdims=True))


def attend(q, k, v, heads):
    total = jnp.zeros(q.shape, F32)
    for h in range(heads):
        mask = head_mask(q.shape[1], h)
        probs = probs_of(q, k, h, None)
        total += mm(probs.astype(BF), v * mask, 1, 0)
    return total.astype(BF)


def attend_back(q, k, v, up, heads, probs_at, with_out):
    zero = jnp.zeros(q.shape, F32)
    out, dq, dk, dv = zero, zero, zero, zero
    v_scaled = v * jnp.full((1, 1), SCALE, BF)
    for h in range(heads):
        mask = head_mask(q.shape[1], h)
        up_head = up * mask
        probs = probs_at(h)
        probs_b = probs.astype(BF)
        if with_out:
            out += mm(probs_b, v * mask, 1, 0)
        dv += mm(probs_b, up_head, 0, 0)
        dp = mm(up_head, v_scaled, 1, 1)
        delta = jnp.sum(probs * dp, -1, keepdims=True)
        ds = (probs * (dp - delta)).astype(BF)
        dq += mm(ds, k * mask, 1, 0)
        dk += mm(ds, q * mask, 0, 0)
    return dq.astype(BF), dk.astype(BF), dv.astype(BF), out.astype(BF)


def row_order(rows, outer, middle, inner):
    to = lax.broadcasted_iota(jnp.int32, (rows, 1), 0)
    at = lax.broadcasted_iota(jnp.int32, (1, rows), 1)
    o, m, i = to // (middle * inner), (to // inner) % middle, to % inner
    return (at == (m * outer + o) * inner + i).astype(F32).astype(BF)


def own_block(r, rows):
    start = flipped(lax.axis_index("mp"), r, 2) * rows
    return pl.ds(pl.multiple_of(start, rows), rows)


def joined(x, grad):
    rows, dim = x.shape

    def body(t):
        for i in range(2):
            t.outs[0][:, i * dim : (i + 1) * dim] = t.get(i)[...]

    return run(body, (x, grad), "hh", (shape((rows, 2 * dim)),), "v")[0]


def spatial_forward(parts, weights, heads, groups):
    own_rows, dim = parts[0].shape
    mp, width = len(parts), weights.shape[2]
    rows = mp * own_rows

    def body(t):
        for r in (*range(1, mp), 0):
            xf = t.get(r)[...].astype(F32)
            t.outs[0][own_block(r, own_rows), :] = (xf * inv_rms(xf)).astype(BF)
        nx = t.outs[0][...]
        t.put(0)
        w = t.get(mp)
        q, k, v = [mm(nx, w[j], 1, 0).astype(BF) for j in range(3)]
        for j, part in enumerate((q, k, v)):
            t.outs[1][j] = part
        t.put(1)
        attn = attend(q, k, v, heads)
        order = row_order(rows, groups, mp, rows // (groups * mp))
        t.outs[2][...] = mm(order, attn, 1, 0).astype(BF)

    outs = (shape((rows, dim)), shape((3, rows, width)), shape((rows, width)))
    return run(
        body, (*parts, weights), "h" + "v" * (mp - 1) + "h", outs, "hhv"
    )


def owner_rows(xg, w_to, attn, w_so, frames, per):
    own_rows, mp = xg[0].shape[0], len(xg)
    rows, (width, dim) = mp * own_rows, w_to.shape

    def body(t):
        x_buf = t.scratch[0]
        for r in range(mp):
            at = own_block(r, own_rows)
            x_buf[at, :] = t.get(r)[:, :dim]
            t.outs[1][at, :] = t.get(r)[:, dim:]
        total = x_buf[...].astype(F32)
        order = row_order(rows, mp, frames, per)
        for i in range(len(attn)):
            part = mm(order, t.get(mp + 1 + i)[...], 1, 0).astype(BF)
            total += mm(part, t.get(mp + 1 + len(attn) + i)[...], 1, 0)
        t.outs[0][...] = total
        t.outs[2][...] = mm(t.outs[1][...], t.get(mp)[...], 1, 1).astype(BF)

    outs = (shape((rows, dim), F32), shape((rows, dim)), shape((rows, width)))
    ins = (*xg, w_to, *attn, *w_so)
    where = "v" * mp + "h" + "v" * len(attn) + "h" + "v" * (len(w_so) - 1)
    return run(body, ins, where, outs, "vvv", scratch=(pltpu.VMEM((rows, dim), BF),))


SENT = ((1, 3, 5, 7), (2, 3, 6, 7))
KEPT = ((0, 2, 4, 6), (0, 1, 4, 5))
OUT_SENT, OUT_KEPT = (1, 5, 3, 7), (0, 4, 2, 6)


def chunk_of(flat, right, r, groups):
    chunk = right.shape[1] // groups
    start = pl.multiple_of(flipped(lax.axis_index("frames"), r, 3) * chunk, chunk)
    return mm(flat, right[:, pl.ds(start, chunk)], 1, 0).astype(BF)


def chunk_grads(t, first, chosen, grads, normed, other, groups):
    flat = [grad.T for grad in grads]
    right = (normed, normed, normed, other)
    for pair, relative in enumerate(chosen):
        for i, r in enumerate(relative):
            for j in range(2):
                at = 2 * pair + j
                side = slice(j * flat[at].shape[0], (j + 1) * flat[at].shape[0])
                t.outs[first + pair][i, side] = chunk_of(flat[at], right[at], r, groups)


def half_shape(width, dim, groups):
    return shape((groups // 2, 2 * width, dim // groups))


def temporal_stage(attn, so_far, g_all, up, w_so, w_qkv, clips, heads, frames, per, mp):
    n, (rows, width) = len(attn), attn[0].shape
    own_rows = rows // mp
    dim = so_far.shape[1]
    halves = frames == 8

    def rows_of(r):
        return own_block(r, own_rows)

    def body(t):
        (clip_ref,) = t.smem
        back, inv_buf = t.scratch
        total = t.get(n)[...]
        order = row_order(rows, mp, frames, per)
        for r in range(n):
            part = mm(order, t.get(r)[...], 1, 0).astype(BF)
            total += mm(part, t.get(n + 2 + r)[...], 1, 0)
        inv = inv_rms(total)
        nh = (total * inv).astype(BF)
        t.outs[2][...] = nh
        inv_buf[...] = jnp.broadcast_to(inv, inv_buf.shape)
        t.outs[3][...] = t.outs[2][rows_of(0), :]
        t.outs[4][...] = inv_buf[rows_of(0), :]

        def key_of(axis):
            dims = (rows, 1) if axis == 0 else (1, rows)
            token = lax.broadcasted_iota(jnp.int32, dims, axis)
            block = token // per
            frame = block % frames
            patch = (block // frames) * per + token % per
            end = jnp.int32(0)
            clip = jnp.zeros(dims, jnp.int32)
            for c in range(clips.shape[0]):
                end = end + clip_ref[c]
                clip += (frame >= end).astype(jnp.int32)
            return clip * rows + patch

        allowed = key_of(0) == key_of(1)
        w = t.get(2 * n + 2)
        q, k, v = [mm(nh, w[j], 1, 0).astype(BF) for j in range(3)]
        grads = attend_back(
            q, k, v, t.get(n + 1)[...], heads, lambda h: probs_of(q, k, h, allowed), True
        )
        for j in range(4):
            t.outs[5][j] = grads[j]
        d_normed = jnp.zeros((rows, dim), F32)
        for j in range(3):
            d_normed += mm(grads[j], w[j], 1, 1)
        back[...] = d_normed.astype(BF)
        for r in range(mp):
            t.outs[1 - r % 2][r // 2] = back[rows_of(r), :]
        if halves:
            chunk_grads(t, 6, SENT, grads, t.outs[2], t.get(2 * n + 3), frames)

    half = shape((mp // 2, own_rows, dim))
    outs = (
        half,
        half,
        shape((rows, dim)),
        shape((own_rows, dim)),
        shape((own_rows, 128), F32),
        shape((4, rows, width)),
    )
    if halves:
        outs += (half_shape(width, dim, frames),) * 2
    ins = (*attn, so_far, up, *w_so, w_qkv, g_all)
    return run(
        body, ins, "v" * len(ins), outs, "v" * len(outs), smem=(clips,),
        scratch=(pltpu.VMEM((rows, dim), BF), pltpu.VMEM((rows, 128), F32)),
    )


def head_sums(send, keep):
    def body(t):
        t.outs[0][...] = (t.get(0)[1].astype(F32) + t.get(1)[1].astype(F32)).astype(BF)

    came = swap(send, "mp", 1)
    (pair,) = run(body, (keep, came), "vv", (shape(keep.shape[1:]),), "v")
    return keep, came, swap(pair, "mp", 2)


def summed(t):
    return t.get(0)[0].astype(F32) + t.get(1)[0].astype(F32) + t.get(2)[...].astype(F32)


def hidden_back(parts, unit, inv, grad):
    dim = unit.shape[1]

    def body(t):
        total, nh = summed(t), t.get(3)[...].astype(F32)
        rest = total - nh * jnp.mean(total * nh, -1, keepdims=True)
        g = t.get(5)[:, dim:].astype(F32)
        t.outs[0][...] = (g + t.get(4)[:, :1] * rest).astype(BF)

    return run(body, (*parts, unit, inv, grad), "vvvvvv", (shape(unit.shape),), "v")[0]


def tokens_back(parts, x, grad):
    def body(t):
        total, xf = summed(t), t.get(3)[...].astype(F32)
        inv = inv_rms(xf)
        nx = xf * inv
        rest = total - nx * jnp.mean(total * nx, -1, keepdims=True)
        t.outs[0][...] = (t.get(4)[...].astype(F32) + inv * rest).astype(BF)

    return run(body, (*parts, x, grad), "vvvvv", (shape(x.shape),), "v")[0]


def weight_grads_half(grads, normed, other, groups, flops=1000):
    def body(t):
        left = [t.get(0)[j] for j in range(4)]
        chunk_grads(t, 0, KEPT, left, t.get(1), t.get(2), groups)

    half = half_shape(grads.shape[2], normed.shape[1], groups)
    return run(body, (grads, normed, other), "vvv", (half, half), "vv", flops=flops)


def weight_grads_whole(grads, normed, other):
    def body(t):
        for j in range(4):
            right = t.get(2) if j == 3 else t.get(1)
            t.outs[0][j] = mm(t.get(0)[j], right[...], 0, 0)

    whole = shape((4, grads.shape[2], normed.shape[1]), F32)
    return run(body, (grads, normed, other), "vhh", (whole,), "h")[0]


def spatial_probs(qkv, attn_moved, heads, groups, mp):
    rows, width = attn_moved.shape

    def body(t):
        q, k = t.get(0)[0], t.get(0)[1]
        for h in range(heads):
            t.outs[0][h] = probs_of(q, k, h, None)
        order = row_order(rows, mp, groups, rows // (groups * mp))
        t.outs[1][...] = mm(order, t.get(1)[...], 1, 0).astype(BF)

    outs = (shape((heads, rows, rows), F32), shape((rows, width)))
    return run(body, (qkv, attn_moved), "vv", outs, "vv")


def out_chunks(parts, attn, groups):
    own_rows, dim = parts[0].shape
    mp, width = len(parts), attn.shape[1]

    def body(t):
        dh = t.outs[0]
        for r in range(mp):
            dh[own_block(r, own_rows), :] = t.get(r)[...]
        if groups == 8:
            flat = t.get(mp)[...].T
            for at, relative in ((1, OUT_SENT), (2, OUT_KEPT)):
                for i, r in enumerate(relative):
                    t.outs[at][i] = chunk_of(flat, dh, r, groups)

    outs = (shape((mp * own_rows, dim)),)
    if groups == 8:
        outs += (shape((groups // 2, width, dim // groups)),) * 2
    return run(body, (*parts, attn), "v" * (mp + 1), outs, "v" * len(outs))


def qkv_parts(grads):
    flat = jnp.concatenate([grad.T for grad in grads], 0)
    first = 13 * flat.shape[0] // 24
    return flat[:first], flat[first:]


def qkv_chunks(t, first, chosen, grads, normed, groups):
    for at, (flat, relative) in enumerate(zip(qkv_parts(grads), chosen)):
        for i, r in enumerate(relative):
            t.outs[first + at][i] = chunk_of(flat, normed, r, groups)


def qkv_part_shapes(width, dim, groups):
    first = 13 * 3 * width // 24
    return tuple(
        shape((groups // 2, rows, dim // groups)) for rows in (first, 3 * width - first)
    )


def spatial_back(dh, w_so, qkv, probs, normed, heads, groups):
    rows, dim = dh.shape
    width = w_so.shape[0]

    def body(t):
        up = mm(t.get(0)[...], t.get(1)[...], 1, 1).astype(BF)
        qkv_ref = t.get(2)
        grads = attend_back(
            qkv_ref[0], qkv_ref[1], qkv_ref[2], up, heads, lambda h: t.get(3)[h], False
        )[:3]
        for j in range(3):
            t.outs[0][j] = grads[j]
        if groups == 8:
            qkv_chunks(t, 1, SENT, grads, t.get(4), groups)

    outs = (shape((3, rows, width)),)
    if groups == 8:
        outs += qkv_part_shapes(width, dim, groups)
    return run(body, (dh, w_so, qkv, probs, normed), "vvvvh", outs, "v" * len(outs))


def qkv_keeps(grads, normed, groups, flops):
    def body(t):
        qkv_chunks(t, 0, KEPT, [t.get(0)[j] for j in range(3)], t.get(1), groups)

    outs = qkv_part_shapes(grads.shape[2], normed.shape[1], groups)
    return run(body, (grads, normed), "vv", outs, "vv", flops=flops)


def normed_back(grads, w_qkv, mp):
    rows, dim = grads.shape[1], w_qkv.shape[1]
    own_rows = rows // mp

    def body(t):
        (back,) = t.scratch
        total = jnp.zeros((rows, dim), F32)
        for j in range(3):
            total += mm(t.get(0)[j], t.get(1)[j], 1, 1)
        back[...] = total.astype(BF)
        for r in range(mp):
            t.outs[1 - r % 2][r // 2] = back[own_block(r, own_rows), :]

    half = shape((mp // 2, own_rows, dim))
    return run(
        body, (grads, w_qkv), "vv", (half, half), "vv", scratch=(pltpu.VMEM((rows, dim), BF),)
    )


def halve(keeps, cames, keep_in="v", out="v", merged=False, flops=1000):
    n, depth = len(keeps), keeps[0].shape[0]
    rows = [keep.shape[1] for keep in keeps]
    chunk = keeps[0].shape[2]

    def body(t):
        for i in range(depth - 1, -1, -1):
            for at in range(n):
                total = t.get(at)[i].astype(F32) + t.get(n + at)[i].astype(F32)
                kept, first = 1 - i % 2, sum(rows[:at])
                if merged:
                    t.outs[kept][first : first + rows[at]] = total.astype(BF)
                else:
                    t.outs[n * kept + at][i // 2] = total.astype(BF)

    if merged:
        outs = (shape((sum(rows), chunk)),) * 2
    else:
        outs = tuple(shape((depth // 2, r, chunk)) for r in rows) * 2
    where = keep_in * n + "v" * n
    return run(body, (*keeps, *cames), where, outs, out * len(outs), flops=flops)


def last_sums(pairs, flops=1000):
    chunk = pairs[0][0].shape[-1]
    pairs = [tuple(part.reshape(-1, chunk) for part in pair) for pair in pairs]
    width = sum(pair[0].shape[0] for pair in pairs) // 4

    def body(t):
        row = 0
        for at, (keep, _) in enumerate(pairs):
            start = 0
            while start < keep.shape[0]:
                size = min(width - row % width, keep.shape[0] - start)
                here = slice(start, start + size)
                total = t.get(2 * at)[here].astype(F32) + t.get(2 * at + 1)[here].astype(F32)
                side = slice(row % width, row % width + size)
                if row < 3 * width:
                    t.outs[0][row // width, :, side] = total.T
                else:
                    t.outs[1][side, :] = total
                start, row = start + size, row + size

    ins = [part for pair in pairs for part in pair]
    outs = (shape((3, chunk, width), F32), shape((width, chunk), F32))
    return run(body, ins, "v" * len(ins), outs, "hh", flops=flops)


def reduce_whole(flat, normed, other):
    whole = weight_grads_whole(flat, normed, other)
    mine = lax.psum_scatter(whole, "frames", scatter_dimension=2, tiled=True)
    return jnp.swapaxes(mine[:3], 1, 2), mine[3]


def shards(
    video_tokens, grad_output, spatial_qkv, spatial_out, temporal_qkv, temporal_out, clip_frames
):
    frames_dev, rows_mp, dim = video_tokens.shape
    width = spatial_out.shape[0]
    heads = width // HD
    groups = lax.axis_size("frames")
    mp = lax.axis_size("mp")
    patches = rows_mp * mp
    per = rows_mp // groups
    assert frames_dev == 1 and rows_mp % groups == 0 and mp == 4

    halves = groups == 8
    x_own, g_own = video_tokens[0], grad_output[0]
    x_one, x_two = swap(x_own, "mp", 1), swap(x_own, "mp", 2)
    xg, x_one, x_two, so_own = lax.optimization_barrier(
        (joined(x_own, g_own), x_one, x_two, spatial_out)
    )
    x_three = swap(x_two, "mp", 1)
    xg = lax.all_to_all(xg.reshape(groups, per, 2 * dim), "frames", 0, 0, tiled=True)
    xg = xg.reshape(rows_mp, 2 * dim)
    so_two = swap(so_own, "mp", 2)

    normed_x, qkv_s, attn_send = spatial_forward(
        (x_own, x_one, x_two, x_three), spatial_qkv, heads, groups
    )
    attn_send, xg = lax.optimization_barrier((attn_send, xg))
    xg_two = swap(xg, "mp", 2)
    moved = lax.all_to_all(
        attn_send.reshape(groups, mp * per, width), "frames", 0, 0, tiled=True
    ).reshape(patches, width)
    so_two, moved = lax.optimization_barrier((so_two, moved))
    moved_one, moved_two = swap(moved, "mp", 1), swap(moved, "mp", 2)
    so_one = swap(spatial_out, "mp", 1)
    xg_all = xg, swap(xg, "mp", 1), xg_two, swap(xg_two, "mp", 1)
    rows_own = owner_rows(
        xg_all, temporal_out, (moved, moved_one), (spatial_out, so_one), groups, per
    )
    moved_two, rows_own = lax.optimization_barrier((moved_two, rows_own))
    so_far, g_rows, d_attn_t = rows_own

    send_h, keep_h, normed_h, unit_own, inv_own, t_grads, *t_sent = temporal_stage(
        (moved_two, swap(moved_two, "mp", 1)), so_far, g_rows, d_attn_t,
        (so_two, swap(so_two, "mp", 1)), temporal_qkv, clip_frames, heads, groups, per, mp,
    )
    parts = head_sums(send_h, keep_h)
    if halves:
        t_kept = weight_grads_half(t_grads, normed_h, g_rows, groups)
        parts, t_kept = lax.optimization_barrier((parts, t_kept))
        came = [swap(t_sent[0], "frames", 1), swap(t_sent[1], "frames", 2)]
        t_sums = halve(t_kept, came, out="h")
    d_hidden = hidden_back(parts, unit_own, inv_own, xg)
    d_hidden = lax.all_to_all(
        d_hidden.reshape(groups, per, dim), "frames", 0, 0, tiled=True
    ).reshape(rows_mp, dim)
    if halves:
        d_hidden, t_sums = lax.optimization_barrier((d_hidden, t_sums))
        t_second = [swap(t_sums[0], "frames", 2), swap(t_sums[1], "frames", 1)]
    dh_one, dh_two = swap(d_hidden, "mp", 1), swap(d_hidden, "mp", 2)
    d_hidden, qkv_s, attn_send = lax.optimization_barrier((d_hidden, qkv_s, attn_send))
    probs_s, attn_s = spatial_probs(qkv_s, attn_send, heads, groups, mp)
    dh_two, probs_s, attn_s = lax.optimization_barrier((dh_two, probs_s, attn_s))
    dh_three = swap(dh_two, "mp", 1)
    d_hidden_all, *o_chunks = out_chunks((d_hidden, dh_one, dh_two, dh_three), attn_s, groups)
    dh_ready = d_hidden_all
    if halves:
        dh_ready, t_second = lax.optimization_barrier((dh_ready, t_second))
        t_send, t_keep = halve(t_sums[2:], t_second, keep_in="h", merged=True)
        dh_ready, t_send, t_keep = lax.optimization_barrier((dh_ready, t_send, t_keep))
        t_came = swap(t_send, "frames", 4)
    else:
        t_qkv, t_out = reduce_whole(t_grads, normed_h, g_rows)
    s_grads, *s_sent = spatial_back(
        dh_ready, spatial_out, qkv_s, probs_s, normed_x, heads, groups
    )
    if halves:
        after = lax.optimization_barrier
        send_x, keep_x = normed_back(s_grads, spatial_qkv, mp)
        o_send, o_keep = halve([o_chunks[1]], [swap(o_chunks[0], "frames", 1)])
        s_grads, send_x, keep_x, t_came, o_send, o_keep = after(
            (s_grads, send_x, keep_x, t_came, o_send, o_keep)
        )
        o_came = swap(o_send, "frames", 4)
        t_qkv, t_out = last_sums([(t_keep, t_came)], 50_000_000_000)
        s_kept = qkv_keeps(s_grads, normed_x, groups, 50_000_000_000)
        came = [swap(s_sent[0], "frames", 1), swap(s_sent[1], "frames", 2)]
        came, t_qkv, t_out = after((came, t_qkv, t_out))
        send_a, send_b, keep_a, keep_b = halve(s_kept, came)
        came = [swap(send_a, "frames", 2), swap(send_b, "frames", 1)]
        o_send, o_keep = halve([o_keep], [o_came], flops=50_000_000_000)
        came, o_send, o_keep = after((came, o_send, o_keep))
        s_send, s_keep = halve([keep_a, keep_b], came, merged=True)
        s_qkv, s_out = last_sums([
            (s_keep, swap(s_send, "frames", 4)), (o_keep, swap(o_send, "frames", 2))
        ])
    else:
        send_x, keep_x = normed_back(s_grads, spatial_qkv, mp)
        all_grads = jnp.concatenate([s_grads, attn_s[None]], 0)
        s_qkv, s_out = reduce_whole(all_grads, normed_x, d_hidden_all)
    grad_tokens = tokens_back(head_sums(send_x, keep_x), x_own, d_hidden)
    return grad_tokens[None], s_qkv, s_out, t_qkv, t_out


def solution(mesh):
    placed = (
        P("frames", "mp", None),
        P("frames", "mp", None),
        P(None, None, "mp"),
        P("mp", None),
        P(None, None, "mp"),
        P("mp", None),
        P(),
    )
    return jax.shard_map(
        shards,
        mesh=mesh,
        in_specs=placed,
        out_specs=(
            P("frames", "mp", None),
            P(None, "frames", "mp"),
            P("mp", "frames"),
            P(None, "frames", "mp"),
            P("mp", "frames"),
        ),
        check_vma=False,
    )
```

```python
import jax
import jax.numpy as jnp
from jax import lax
from jax.experimental import pallas as pl
from jax.experimental.pallas import tpu as pltpu
from jax.sharding import PartitionSpec as P

HD = 64
EPS = 1e-06
NEGATIVE = -1e30
BF = jnp.bfloat16
F32 = jnp.float32
VMEM_LIMIT = 20 * 1024 * 1024


def mm(a, b, ca, cb):
    return lax.dot_general(a, b, (((ca,), (cb,)), ((), ())), preferred_element_type=F32)


def shape(dims, dtype=BF):
    return jax.ShapeDtypeStruct(dims, dtype)


def flipped(index, by, bits):
    total = index
    for b in range(bits):
        if (by >> b) & 1:
            total = total + (1 << b) * (1 - 2 * ((index // (1 << b)) % 2))
    return total


def swap(value, axis, by):
    size = lax.axis_size(axis)
    return lax.ppermute(value, axis, [(i, i ^ by) for i in range(size)])


class Kernel:
    def __init__(self, get, outs, put, smem, scratch, sems, early):
        self.get, self.outs, self.put = get, outs, put
        self.smem, self.scratch, self.sems, self.early = smem, scratch, sems, early

    def copy(self, src, dst):
        made = pltpu.make_async_copy(src, dst, self.sems.pop(0))
        made.start()
        return made


def run(
    body, ins, where, outs, out_where, smem=(), scratch=(), copies=0, early=None, flops=1000
):
    n, k, s = len(ins), len(outs), len(smem)
    staged_in = [i for i in range(n) if where[i] in "ha"]
    staged_out = [i for i in range(k) if out_where[i] in "ha"]

    def wrapped(*refs):
        refs = list(refs)

        def take(count):
            part = refs[:count]
            del refs[:count]
            return part

        scalars, src, dst = take(s), take(n), take(k)
        in_bufs, out_bufs = take(len(staged_in)), take(len(staged_out))
        in_sem, out_sem, own_sem = take(3)
        loads, stores = {}, {}
        results = list(dst)
        for at, i in enumerate(staged_out):
            results[i] = out_bufs[at]
        held = {i: in_bufs[at] for at, i in enumerate(staged_in)}
        waited = set()

        def get(i):
            if i not in held:
                return src[i]
            if i not in waited:
                loads[i].wait()
                waited.add(i)
            return held[i]

        def put(i):
            if i in staged_out and i not in stores:
                at = staged_out.index(i)
                stores[i] = pltpu.make_async_copy(out_bufs[at], dst[i], out_sem.at[at])
                stores[i].start()

        sems = [own_sem.at[i] for i in range(copies)]
        tools = Kernel(get, results, put, scalars, refs, sems, None)
        if early is not None:
            tools.early = early(tools)
        for at, i in enumerate(staged_in):
            loads[i] = pltpu.make_async_copy(src[i], in_bufs[at], in_sem.at[at])
            loads[i].start()
        body(tools)
        for i in staged_in:
            get(i)
        for i in range(k):
            put(i)
        for copy in stores.values():
            copy.wait()

    specs = {"v": pltpu.VMEM, "h": pltpu.HBM, "a": pl.ANY, "n": pl.ANY, "x": pltpu.HBM}
    specs = {key: pl.BlockSpec(memory_space=space) for key, space in specs.items()}
    buffers = [pltpu.VMEM(ins[i].shape, ins[i].dtype) for i in staged_in]
    buffers += [pltpu.VMEM(outs[i].shape, outs[i].dtype) for i in staged_out]
    ins = [
        pltpu.with_memory_space_constraint(a, pltpu.HBM) if w in "hx" else a
        for a, w in zip(ins, where)
    ]
    return pl.pallas_call(
        wrapped,
        out_shape=tuple(
            pltpu.HBM(o.shape, o.dtype) if w in "hx" else o for o, w in zip(outs, out_where)
        ),
        in_specs=[pl.BlockSpec(memory_space=pltpu.SMEM)] * s
        + [specs[w] for w in where],
        out_specs=tuple(specs[w] for w in out_where),
        scratch_shapes=buffers
        + [pltpu.SemaphoreType.DMA((max(1, c),)) for c in (len(staged_in), len(staged_out), copies)]
        + list(scratch),
        compiler_params=pltpu.CompilerParams(vmem_limit_bytes=VMEM_LIMIT),
        cost_estimate=pl.CostEstimate(flops=flops, bytes_accessed=1000, transcendentals=0),
    )(*smem, *ins)


def inv_rms(v):
    return lax.rsqrt(jnp.mean(v * v, -1, keepdims=True) + EPS)


SCALE = HD ** (-0.5)
assert SCALE == 0.125


def head_mask(width, head, scale=1.0):
    lane = lax.broadcasted_iota(jnp.int32, (1, width), 1)
    mask = ((lane >= head * HD) & (lane < (head + 1) * HD)).astype(F32)
    return (mask * scale).astype(BF)


def probs_of(q, k, head, allowed):
    scores = mm(q * head_mask(q.shape[1], head, SCALE), k, 1, 1)
    if allowed is not None:
        scores = jnp.where(allowed, scores, NEGATIVE)
    expo = jnp.exp(scores - jnp.max(scores, -1, keepdims=True))
    return expo * (1.0 / jnp.sum(expo, -1, keepdims=True))


def attend(q, k, v, heads):
    total = jnp.zeros(q.shape, F32)
    for h in range(heads):
        mask = head_mask(q.shape[1], h)
        probs = probs_of(q, k, h, None)
        total += mm(probs.astype(BF), v * mask, 1, 0)
    return total.astype(BF)


def attend_back(q, k, v, up, heads, probs_at, with_out):
    zero = jnp.zeros(q.shape, F32)
    out, dq, dk, dv = zero, zero, zero, zero
    v_scaled = v * jnp.full((1, 1), SCALE, BF)
    for h in range(heads):
        mask = head_mask(q.shape[1], h)
        up_head = up * mask
        probs = probs_at(h)
        probs_b = probs.astype(BF)
        if with_out:
            out += mm(probs_b, v * mask, 1, 0)
        dv += mm(probs_b, up_head, 0, 0)
        dp = mm(up_head, v_scaled, 1, 1)
        delta = jnp.sum(probs * dp, -1, keepdims=True)
        ds = (probs * (dp - delta)).astype(BF)
        dq += mm(ds, k * mask, 1, 0)
        dk += mm(ds, q * mask, 0, 0)
    return dq.astype(BF), dk.astype(BF), dv.astype(BF), out.astype(BF)


def row_order(rows, outer, middle, inner):
    to = lax.broadcasted_iota(jnp.int32, (rows, 1), 0)
    at = lax.broadcasted_iota(jnp.int32, (1, rows), 1)
    o, m, i = to // (middle * inner), (to // inner) % middle, to % inner
    return (at == (m * outer + o) * inner + i).astype(F32).astype(BF)


def own_block(r, rows):
    start = flipped(lax.axis_index("mp"), r, 2) * rows
    return pl.ds(pl.multiple_of(start, rows), rows)


def joined(x, grad):
    rows, dim = x.shape

    def body(t):
        for i in range(2):
            t.outs[0][:, i * dim : (i + 1) * dim] = t.get(i)[...]

    return run(body, (x, grad), "hh", (shape((rows, 2 * dim)),), "v")[0]


def spatial_forward(parts, weights, heads, groups):
    own_rows, dim = parts[0].shape
    mp, width = len(parts), weights.shape[2]
    rows = mp * own_rows

    def body(t):
        for r in (*range(1, mp), 0):
            xf = t.get(r)[...].astype(F32)
            t.outs[0][own_block(r, own_rows), :] = (xf * inv_rms(xf)).astype(BF)
        nx = t.outs[0][...]
        t.put(0)
        w = t.get(mp)
        q, k, v = [mm(nx, w[j], 1, 0).astype(BF) for j in range(3)]
        for j, part in enumerate((q, k, v)):
            t.outs[1][j] = part
        t.put(1)
        attn = attend(q, k, v, heads)
        order = row_order(rows, groups, mp, rows // (groups * mp))
        t.outs[2][...] = mm(order, attn, 1, 0).astype(BF)

    outs = (shape((rows, dim)), shape((3, rows, width)), shape((rows, width)))
    return run(
        body, (*parts, weights), "h" + "v" * (mp - 1) + "h", outs, "hhv"
    )


def owner_rows(xg, w_to, attn, w_so, frames, per):
    own_rows, mp = xg[0].shape[0], len(xg)
    rows, (width, dim) = mp * own_rows, w_to.shape

    def body(t):
        x_buf = t.scratch[0]
        for r in range(mp):
            at = own_block(r, own_rows)
            x_buf[at, :] = t.get(r)[:, :dim]
            t.outs[1][at, :] = t.get(r)[:, dim:]
        total = x_buf[...].astype(F32)
        order = row_order(rows, mp, frames, per)
        for i in range(len(attn)):
            part = mm(order, t.get(mp + 1 + i)[...], 1, 0).astype(BF)
            total += mm(part, t.get(mp + 1 + len(attn) + i)[...], 1, 0)
        t.outs[0][...] = total
        t.outs[2][...] = mm(t.outs[1][...], t.get(mp)[...], 1, 1).astype(BF)

    outs = (shape((rows, dim), F32), shape((rows, dim)), shape((rows, width)))
    ins = (*xg, w_to, *attn, *w_so)
    where = "v" * mp + "h" + "v" * len(attn) + "h" + "v" * (len(w_so) - 1)
    return run(body, ins, where, outs, "vvv", scratch=(pltpu.VMEM((rows, dim), BF),))


SENT = ((1, 3, 5, 7), (2, 3, 6, 7))
KEPT = ((0, 2, 4, 6), (0, 1, 4, 5))
OUT_SENT, OUT_KEPT = (1, 5, 3, 7), (0, 4, 2, 6)


def chunk_of(flat, right, r, groups):
    chunk = right.shape[1] // groups
    start = pl.multiple_of(flipped(lax.axis_index("frames"), r, 3) * chunk, chunk)
    return mm(flat, right[:, pl.ds(start, chunk)], 1, 0).astype(BF)


def chunk_grads(t, first, chosen, grads, normed, other, groups):
    flat = [grad.T for grad in grads]
    right = (normed, normed, normed, other)
    for pair, relative in enumerate(chosen):
        for i, r in enumerate(relative):
            for j in range(2):
                at = 2 * pair + j
                side = slice(j * flat[at].shape[0], (j + 1) * flat[at].shape[0])
                t.outs[first + pair][i, side] = chunk_of(flat[at], right[at], r, groups)


def half_shape(width, dim, groups):
    return shape((groups // 2, 2 * width, dim // groups))


def temporal_stage(attn, so_far, g_all, up, w_so, w_qkv, clips, heads, frames, per, mp):
    n, (rows, width) = len(attn), attn[0].shape
    own_rows = rows // mp
    dim = so_far.shape[1]
    halves = frames == 8

    def rows_of(r):
        return own_block(r, own_rows)

    def body(t):
        (clip_ref,) = t.smem
        back, inv_buf = t.scratch
        total = t.get(n)[...]
        order = row_order(rows, mp, frames, per)
        for r in range(n):
            part = mm(order, t.get(r)[...], 1, 0).astype(BF)
            total += mm(part, t.get(n + 2 + r)[...], 1, 0)
        inv = inv_rms(total)
        nh = (total * inv).astype(BF)
        t.outs[2][...] = nh
        inv_buf[...] = jnp.broadcast_to(inv, inv_buf.shape)
        t.outs[3][...] = t.outs[2][rows_of(0), :]
        t.outs[4][...] = inv_buf[rows_of(0), :]

        def key_of(axis):
            dims = (rows, 1) if axis == 0 else (1, rows)
            token = lax.broadcasted_iota(jnp.int32, dims, axis)
            block = token // per
            frame = block % frames
            patch = (block // frames) * per + token % per
            end = jnp.int32(0)
            clip = jnp.zeros(dims, jnp.int32)
            for c in range(clips.shape[0]):
                end = end + clip_ref[c]
                clip += (frame >= end).astype(jnp.int32)
            return clip * rows + patch

        allowed = key_of(0) == key_of(1)
        w = t.get(2 * n + 2)
        q, k, v = [mm(nh, w[j], 1, 0).astype(BF) for j in range(3)]
        grads = attend_back(
            q, k, v, t.get(n + 1)[...], heads, lambda h: probs_of(q, k, h, allowed), True
        )
        for j in range(4):
            t.outs[5][j] = grads[j]
        d_normed = jnp.zeros((rows, dim), F32)
        for j in range(3):
            d_normed += mm(grads[j], w[j], 1, 1)
        back[...] = d_normed.astype(BF)
        for r in range(mp):
            t.outs[1 - r % 2][r // 2] = back[rows_of(r), :]
        if halves:
            chunk_grads(t, 6, SENT, grads, t.outs[2], t.get(2 * n + 3), frames)

    half = shape((mp // 2, own_rows, dim))
    outs = (
        half,
        half,
        shape((rows, dim)),
        shape((own_rows, dim)),
        shape((own_rows, 128), F32),
        shape((4, rows, width)),
    )
    if halves:
        outs += (half_shape(width, dim, frames),) * 2
    ins = (*attn, so_far, up, *w_so, w_qkv, g_all)
    return run(
        body, ins, "v" * len(ins), outs, "v" * len(outs), smem=(clips,),
        scratch=(pltpu.VMEM((rows, dim), BF), pltpu.VMEM((rows, 128), F32)),
    )


def head_sums(send, keep):
    def body(t):
        t.outs[0][...] = (t.get(0)[1].astype(F32) + t.get(1)[1].astype(F32)).astype(BF)

    came = swap(send, "mp", 1)
    (pair,) = run(body, (keep, came), "vv", (shape(keep.shape[1:]),), "v")
    return keep, came, swap(pair, "mp", 2)


def summed(t):
    return t.get(0)[0].astype(F32) + t.get(1)[0].astype(F32) + t.get(2)[...].astype(F32)


def hidden_back(parts, unit, inv, grad):
    dim = unit.shape[1]

    def body(t):
        total, nh = summed(t), t.get(3)[...].astype(F32)
        rest = total - nh * jnp.mean(total * nh, -1, keepdims=True)
        g = t.get(5)[:, dim:].astype(F32)
        t.outs[0][...] = (g + t.get(4)[:, :1] * rest).astype(BF)

    return run(body, (*parts, unit, inv, grad), "vvvvvv", (shape(unit.shape),), "v")[0]


def tokens_back(parts, x, grad):
    def body(t):
        total, xf = summed(t), t.get(3)[...].astype(F32)
        inv = inv_rms(xf)
        nx = xf * inv
        rest = total - nx * jnp.mean(total * nx, -1, keepdims=True)
        t.outs[0][...] = (t.get(4)[...].astype(F32) + inv * rest).astype(BF)

    return run(body, (*parts, x, grad), "vvvvv", (shape(x.shape),), "v")[0]


def weight_grads_half(grads, normed, other, groups, flops=1000):
    def body(t):
        left = [t.get(0)[j] for j in range(4)]
        chunk_grads(t, 0, KEPT, left, t.get(1), t.get(2), groups)

    half = half_shape(grads.shape[2], normed.shape[1], groups)
    return run(body, (grads, normed, other), "vvv", (half, half), "vv", flops=flops)


def weight_grads_whole(grads, normed, other):
    def body(t):
        for j in range(4):
            right = t.get(2) if j == 3 else t.get(1)
            t.outs[0][j] = mm(t.get(0)[j], right[...], 0, 0)

    whole = shape((4, grads.shape[2], normed.shape[1]), F32)
    return run(body, (grads, normed, other), "vhh", (whole,), "h")[0]


def spatial_probs(qkv, attn_moved, heads, groups, mp):
    rows, width = attn_moved.shape

    def body(t):
        q, k = t.get(0)[0], t.get(0)[1]
        for h in range(heads):
            t.outs[0][h] = probs_of(q, k, h, None)
        order = row_order(rows, mp, groups, rows // (groups * mp))
        t.outs[1][...] = mm(order, t.get(1)[...], 1, 0).astype(BF)

    outs = (shape((heads, rows, rows), F32), shape((rows, width)))
    return run(body, (qkv, attn_moved), "vv", outs, "vv")


def out_chunks(parts, attn, groups):
    own_rows, dim = parts[0].shape
    mp, width = len(parts), attn.shape[1]

    def body(t):
        dh = t.outs[0]
        for r in range(mp):
            dh[own_block(r, own_rows), :] = t.get(r)[...]
        if groups == 8:
            flat = t.get(mp)[...].T
            for at, relative in ((1, OUT_SENT), (2, OUT_KEPT)):
                for i, r in enumerate(relative):
                    t.outs[at][i] = chunk_of(flat, dh, r, groups)

    outs = (shape((mp * own_rows, dim)),)
    if groups == 8:
        outs += (shape((groups // 2, width, dim // groups)),) * 2
    return run(body, (*parts, attn), "v" * (mp + 1), outs, "v" * len(outs))


def qkv_parts(grads):
    flat = jnp.concatenate([grad.T for grad in grads], 0)
    first = 7 * flat.shape[0] // 12
    return flat[:first], flat[first:]


def qkv_chunks(t, first, chosen, grads, normed, groups):
    for at, (flat, relative) in enumerate(zip(qkv_parts(grads), chosen)):
        for i, r in enumerate(relative):
            t.outs[first + at][i] = chunk_of(flat, normed, r, groups)


def qkv_part_shapes(width, dim, groups):
    first = 7 * 3 * width // 12
    return tuple(
        shape((groups // 2, rows, dim // groups)) for rows in (first, 3 * width - first)
    )


def spatial_back(dh, w_so, qkv, probs, normed, heads, groups):
    rows, dim = dh.shape
    width = w_so.shape[0]

    def body(t):
        up = mm(t.get(0)[...], t.get(1)[...], 1, 1).astype(BF)
        qkv_ref = t.get(2)
        grads = attend_back(
            qkv_ref[0], qkv_ref[1], qkv_ref[2], up, heads, lambda h: t.get(3)[h], False
        )[:3]
        for j in range(3):
            t.outs[0][j] = grads[j]
        if groups == 8:
            qkv_chunks(t, 1, SENT, grads, t.get(4), groups)

    outs = (shape((3, rows, width)),)
    if groups == 8:
        outs += qkv_part_shapes(width, dim, groups)
    return run(body, (dh, w_so, qkv, probs, normed), "vvvvh", outs, "v" * len(outs))


def qkv_keeps(grads, normed, groups, flops):
    def body(t):
        qkv_chunks(t, 0, KEPT, [t.get(0)[j] for j in range(3)], t.get(1), groups)

    outs = qkv_part_shapes(grads.shape[2], normed.shape[1], groups)
    return run(body, (grads, normed), "vv", outs, "vv", flops=flops)


def normed_back(grads, w_qkv, mp):
    rows, dim = grads.shape[1], w_qkv.shape[1]
    own_rows = rows // mp

    def body(t):
        (back,) = t.scratch
        total = jnp.zeros((rows, dim), F32)
        for j in range(3):
            total += mm(t.get(0)[j], t.get(1)[j], 1, 1)
        back[...] = total.astype(BF)
        for r in range(mp):
            t.outs[1 - r % 2][r // 2] = back[own_block(r, own_rows), :]

    half = shape((mp // 2, own_rows, dim))
    return run(
        body, (grads, w_qkv), "vv", (half, half), "vv", scratch=(pltpu.VMEM((rows, dim), BF),)
    )


def halve(keeps, cames, keep_in="v", out="v", merged=False, flops=1000):
    n, depth = len(keeps), keeps[0].shape[0]
    rows = [keep.shape[1] for keep in keeps]
    chunk = keeps[0].shape[2]

    def body(t):
        for i in range(depth - 1, -1, -1):
            for at in range(n):
                total = t.get(at)[i].astype(F32) + t.get(n + at)[i].astype(F32)
                kept, first = 1 - i % 2, sum(rows[:at])
                if merged:
                    t.outs[kept][first : first + rows[at]] = total.astype(BF)
                else:
                    t.outs[n * kept + at][i // 2] = total.astype(BF)

    if merged:
        outs = (shape((sum(rows), chunk)),) * 2
    else:
        outs = tuple(shape((depth // 2, r, chunk)) for r in rows) * 2
    where = keep_in * n + "v" * n
    return run(body, (*keeps, *cames), where, outs, out * len(outs), flops=flops)


def last_sums(pairs, flops=1000):
    chunk = pairs[0][0].shape[-1]
    pairs = [tuple(part.reshape(-1, chunk) for part in pair) for pair in pairs]
    width = sum(pair[0].shape[0] for pair in pairs) // 4

    def body(t):
        row = 0
        for at, (keep, _) in enumerate(pairs):
            start = 0
            while start < keep.shape[0]:
                size = min(width - row % width, keep.shape[0] - start)
                here = slice(start, start + size)
                total = t.get(2 * at)[here].astype(F32) + t.get(2 * at + 1)[here].astype(F32)
                side = slice(row % width, row % width + size)
                if row < 3 * width:
                    t.outs[0][row // width, :, side] = total.T
                else:
                    t.outs[1][side, :] = total
                start, row = start + size, row + size

    ins = [part for pair in pairs for part in pair]
    outs = (shape((3, chunk, width), F32), shape((width, chunk), F32))
    return run(body, ins, "v" * len(ins), outs, "hh", flops=flops)


def reduce_whole(flat, normed, other):
    whole = weight_grads_whole(flat, normed, other)
    mine = lax.psum_scatter(whole, "frames", scatter_dimension=2, tiled=True)
    return jnp.swapaxes(mine[:3], 1, 2), mine[3]


def shards(
    video_tokens, grad_output, spatial_qkv, spatial_out, temporal_qkv, temporal_out, clip_frames
):
    frames_dev, rows_mp, dim = video_tokens.shape
    width = spatial_out.shape[0]
    heads = width // HD
    groups = lax.axis_size("frames")
    mp = lax.axis_size("mp")
    patches = rows_mp * mp
    per = rows_mp // groups
    assert frames_dev == 1 and rows_mp % groups == 0 and mp == 4

    halves = groups == 8
    x_own, g_own = video_tokens[0], grad_output[0]
    x_one, x_two = swap(x_own, "mp", 1), swap(x_own, "mp", 2)
    xg, x_one, x_two, so_own = lax.optimization_barrier(
        (joined(x_own, g_own), x_one, x_two, spatial_out)
    )
    x_three = swap(x_two, "mp", 1)
    xg = lax.all_to_all(xg.reshape(groups, per, 2 * dim), "frames", 0, 0, tiled=True)
    xg = xg.reshape(rows_mp, 2 * dim)
    so_two = swap(so_own, "mp", 2)

    normed_x, qkv_s, attn_send = spatial_forward(
        (x_own, x_one, x_two, x_three), spatial_qkv, heads, groups
    )
    attn_send, xg = lax.optimization_barrier((attn_send, xg))
    xg_two = swap(xg, "mp", 2)
    moved = lax.all_to_all(
        attn_send.reshape(groups, mp * per, width), "frames", 0, 0, tiled=True
    ).reshape(patches, width)
    so_two, moved = lax.optimization_barrier((so_two, moved))
    moved_one, moved_two = swap(moved, "mp", 1), swap(moved, "mp", 2)
    so_one = swap(spatial_out, "mp", 1)
    xg_all = xg, swap(xg, "mp", 1), xg_two, swap(xg_two, "mp", 1)
    rows_own = owner_rows(
        xg_all, temporal_out, (moved, moved_one), (spatial_out, so_one), groups, per
    )
    moved_two, rows_own = lax.optimization_barrier((moved_two, rows_own))
    so_far, g_rows, d_attn_t = rows_own

    send_h, keep_h, normed_h, unit_own, inv_own, t_grads, *t_sent = temporal_stage(
        (moved_two, swap(moved_two, "mp", 1)), so_far, g_rows, d_attn_t,
        (so_two, swap(so_two, "mp", 1)), temporal_qkv, clip_frames, heads, groups, per, mp,
    )
    parts = head_sums(send_h, keep_h)
    if halves:
        t_kept = weight_grads_half(t_grads, normed_h, g_rows, groups)
        parts, t_kept = lax.optimization_barrier((parts, t_kept))
        came = [swap(t_sent[0], "frames", 1), swap(t_sent[1], "frames", 2)]
        t_sums = halve(t_kept, came, out="h")
    d_hidden = hidden_back(parts, unit_own, inv_own, xg)
    d_hidden = lax.all_to_all(
        d_hidden.reshape(groups, per, dim), "frames", 0, 0, tiled=True
    ).reshape(rows_mp, dim)
    if halves:
        d_hidden, t_sums = lax.optimization_barrier((d_hidden, t_sums))
        t_second = [swap(t_sums[0], "frames", 2), swap(t_sums[1], "frames", 1)]
    dh_one, dh_two = swap(d_hidden, "mp", 1), swap(d_hidden, "mp", 2)
    d_hidden, qkv_s, attn_send = lax.optimization_barrier((d_hidden, qkv_s, attn_send))
    probs_s, attn_s = spatial_probs(qkv_s, attn_send, heads, groups, mp)
    dh_two, probs_s, attn_s = lax.optimization_barrier((dh_two, probs_s, attn_s))
    dh_three = swap(dh_two, "mp", 1)
    d_hidden_all, *o_chunks = out_chunks((d_hidden, dh_one, dh_two, dh_three), attn_s, groups)
    dh_ready = d_hidden_all
    if halves:
        dh_ready, t_second = lax.optimization_barrier((dh_ready, t_second))
        t_send, t_keep = halve(t_sums[2:], t_second, keep_in="h", merged=True)
        dh_ready, t_send, t_keep = lax.optimization_barrier((dh_ready, t_send, t_keep))
        t_came = swap(t_send, "frames", 4)
    else:
        t_qkv, t_out = reduce_whole(t_grads, normed_h, g_rows)
    s_grads, *s_sent = spatial_back(
        dh_ready, spatial_out, qkv_s, probs_s, normed_x, heads, groups
    )
    if halves:
        after = lax.optimization_barrier
        send_x, keep_x = normed_back(s_grads, spatial_qkv, mp)
        o_send, o_keep = halve([o_chunks[1]], [swap(o_chunks[0], "frames", 1)])
        s_grads, send_x, keep_x, t_came, o_send, o_keep = after(
            (s_grads, send_x, keep_x, t_came, o_send, o_keep)
        )
        o_came = swap(o_send, "frames", 4)
        s_kept = qkv_keeps(s_grads, normed_x, groups, 50_000_000_000)
        came_a, came_b = swap(s_sent[0], "frames", 1), swap(s_sent[1], "frames", 2)
        send_a, keep_a = halve([s_kept[0]], [came_a])
        send_a, keep_a, t_keep = after((send_a, keep_a, t_keep))
        t_qkv, t_out = last_sums([(t_keep, t_came)], 50_000_000_000)
        came_b, t_qkv, t_out = after((came_b, t_qkv, t_out))
        send_b, keep_b = halve([s_kept[1]], [came_b])
        came = [swap(send_a, "frames", 2), swap(send_b, "frames", 1)]
        o_send, o_keep = halve([o_keep], [o_came], flops=50_000_000_000)
        came, o_send, o_keep = after((came, o_send, o_keep))
        s_send, s_keep = halve([keep_a, keep_b], came, merged=True)
        s_qkv, s_out = last_sums([
            (s_keep, swap(s_send, "frames", 4)), (o_keep, swap(o_send, "frames", 2))
        ])
    else:
        send_x, keep_x = normed_back(s_grads, spatial_qkv, mp)
        all_grads = jnp.concatenate([s_grads, attn_s[None]], 0)
        s_qkv, s_out = reduce_whole(all_grads, normed_x, d_hidden_all)
    grad_tokens = tokens_back(head_sums(send_x, keep_x), x_own, d_hidden)
    return grad_tokens[None], s_qkv, s_out, t_qkv, t_out


def solution(mesh):
    placed = (
        P("frames", "mp", None),
        P("frames", "mp", None),
        P(None, None, "mp"),
        P("mp", None),
        P(None, None, "mp"),
        P("mp", None),
        P(),
    )
    return jax.shard_map(
        shards,
        mesh=mesh,
        in_specs=placed,
        out_specs=(
            P("frames", "mp", None),
            P(None, "frames", "mp"),
            P("mp", "frames"),
            P(None, "frames", "mp"),
            P("mp", "frames"),
        ),
        check_vma=False,
    )
```

```python
import jax
import jax.numpy as jnp
from jax import lax
from jax.experimental import pallas as pl
from jax.experimental.pallas import tpu as pltpu
from jax.sharding import PartitionSpec as P

HD = 64
EPS = 1e-06
NEGATIVE = -1e30
BF = jnp.bfloat16
F32 = jnp.float32
VMEM_LIMIT = 20 * 1024 * 1024


def mm(a, b, ca, cb):
    return lax.dot_general(a, b, (((ca,), (cb,)), ((), ())), preferred_element_type=F32)


def shape(dims, dtype=BF):
    return jax.ShapeDtypeStruct(dims, dtype)


def flipped(index, by, bits):
    total = index
    for b in range(bits):
        if (by >> b) & 1:
            total = total + (1 << b) * (1 - 2 * ((index // (1 << b)) % 2))
    return total


def swap(value, axis, by):
    size = lax.axis_size(axis)
    return lax.ppermute(value, axis, [(i, i ^ by) for i in range(size)])


class Kernel:
    def __init__(self, get, outs, put, smem, scratch, sems, early):
        self.get, self.outs, self.put = get, outs, put
        self.smem, self.scratch, self.sems, self.early = smem, scratch, sems, early

    def copy(self, src, dst):
        made = pltpu.make_async_copy(src, dst, self.sems.pop(0))
        made.start()
        return made


def run(
    body, ins, where, outs, out_where, smem=(), scratch=(), copies=0, early=None, flops=1000
):
    n, k, s = len(ins), len(outs), len(smem)
    staged_in = [i for i in range(n) if where[i] in "ha"]
    staged_out = [i for i in range(k) if out_where[i] in "ha"]

    def wrapped(*refs):
        refs = list(refs)

        def take(count):
            part = refs[:count]
            del refs[:count]
            return part

        scalars, src, dst = take(s), take(n), take(k)
        in_bufs, out_bufs = take(len(staged_in)), take(len(staged_out))
        in_sem, out_sem, own_sem = take(3)
        loads, stores = {}, {}
        results = list(dst)
        for at, i in enumerate(staged_out):
            results[i] = out_bufs[at]
        held = {i: in_bufs[at] for at, i in enumerate(staged_in)}
        waited = set()

        def get(i):
            if i not in held:
                return src[i]
            if i not in waited:
                loads[i].wait()
                waited.add(i)
            return held[i]

        def put(i):
            if i in staged_out and i not in stores:
                at = staged_out.index(i)
                stores[i] = pltpu.make_async_copy(out_bufs[at], dst[i], out_sem.at[at])
                stores[i].start()

        sems = [own_sem.at[i] for i in range(copies)]
        tools = Kernel(get, results, put, scalars, refs, sems, None)
        if early is not None:
            tools.early = early(tools)
        for at, i in enumerate(staged_in):
            loads[i] = pltpu.make_async_copy(src[i], in_bufs[at], in_sem.at[at])
            loads[i].start()
        body(tools)
        for i in staged_in:
            get(i)
        for i in range(k):
            put(i)
        for copy in stores.values():
            copy.wait()

    specs = {"v": pltpu.VMEM, "h": pltpu.HBM, "a": pl.ANY, "n": pl.ANY, "x": pltpu.HBM}
    specs = {key: pl.BlockSpec(memory_space=space) for key, space in specs.items()}
    buffers = [pltpu.VMEM(ins[i].shape, ins[i].dtype) for i in staged_in]
    buffers += [pltpu.VMEM(outs[i].shape, outs[i].dtype) for i in staged_out]
    ins = [
        pltpu.with_memory_space_constraint(a, pltpu.HBM) if w in "hx" else a
        for a, w in zip(ins, where)
    ]
    return pl.pallas_call(
        wrapped,
        out_shape=tuple(
            pltpu.HBM(o.shape, o.dtype) if w in "hx" else o for o, w in zip(outs, out_where)
        ),
        in_specs=[pl.BlockSpec(memory_space=pltpu.SMEM)] * s
        + [specs[w] for w in where],
        out_specs=tuple(specs[w] for w in out_where),
        scratch_shapes=buffers
        + [pltpu.SemaphoreType.DMA((max(1, c),)) for c in (len(staged_in), len(staged_out), copies)]
        + list(scratch),
        compiler_params=pltpu.CompilerParams(vmem_limit_bytes=VMEM_LIMIT),
        cost_estimate=pl.CostEstimate(flops=flops, bytes_accessed=1000, transcendentals=0),
    )(*smem, *ins)


def inv_rms(v):
    return lax.rsqrt(jnp.mean(v * v, -1, keepdims=True) + EPS)


SCALE = HD ** (-0.5)
assert SCALE == 0.125


def head_mask(width, head, scale=1.0):
    lane = lax.broadcasted_iota(jnp.int32, (1, width), 1)
    mask = ((lane >= head * HD) & (lane < (head + 1) * HD)).astype(F32)
    return (mask * scale).astype(BF)


def probs_of(q, k, head, allowed):
    scores = mm(q * head_mask(q.shape[1], head, SCALE), k, 1, 1)
    if allowed is not None:
        scores = jnp.where(allowed, scores, NEGATIVE)
    expo = jnp.exp(scores - jnp.max(scores, -1, keepdims=True))
    return expo * (1.0 / jnp.sum(expo, -1, keepdims=True))


def attend(q, k, v, heads):
    total = jnp.zeros(q.shape, F32)
    for h in range(heads):
        mask = head_mask(q.shape[1], h)
        probs = probs_of(q, k, h, None)
        total += mm(probs.astype(BF), v * mask, 1, 0)
    return total.astype(BF)


def attend_back(q, k, v, up, heads, probs_at, with_out):
    zero = jnp.zeros(q.shape, F32)
    out, dq, dk, dv = zero, zero, zero, zero
    v_scaled = v * jnp.full((1, 1), SCALE, BF)
    for h in range(heads):
        mask = head_mask(q.shape[1], h)
        up_head = up * mask
        probs = probs_at(h)
        probs_b = probs.astype(BF)
        if with_out:
            out += mm(probs_b, v * mask, 1, 0)
        dv += mm(probs_b, up_head, 0, 0)
        dp = mm(up_head, v_scaled, 1, 1)
        delta = jnp.sum(probs * dp, -1, keepdims=True)
        ds = (probs * (dp - delta)).astype(BF)
        dq += mm(ds, k * mask, 1, 0)
        dk += mm(ds, q * mask, 0, 0)
    return dq.astype(BF), dk.astype(BF), dv.astype(BF), out.astype(BF)


def row_order(rows, outer, middle, inner):
    to = lax.broadcasted_iota(jnp.int32, (rows, 1), 0)
    at = lax.broadcasted_iota(jnp.int32, (1, rows), 1)
    o, m, i = to // (middle * inner), (to // inner) % middle, to % inner
    return (at == (m * outer + o) * inner + i).astype(F32).astype(BF)


def own_block(r, rows):
    start = flipped(lax.axis_index("mp"), r, 2) * rows
    return pl.ds(pl.multiple_of(start, rows), rows)


def joined(x, grad):
    rows, dim = x.shape

    def body(t):
        for i in range(2):
            t.outs[0][:, i * dim : (i + 1) * dim] = t.get(i)[...]

    return run(body, (x, grad), "hh", (shape((rows, 2 * dim)),), "v")[0]


def spatial_forward(parts, weights, heads, groups):
    own_rows, dim = parts[0].shape
    mp, width = len(parts), weights.shape[2]
    rows = mp * own_rows

    def body(t):
        for r in (*range(1, mp), 0):
            xf = t.get(r)[...].astype(F32)
            t.outs[0][own_block(r, own_rows), :] = (xf * inv_rms(xf)).astype(BF)
        nx = t.outs[0][...]
        t.put(0)
        w = t.get(mp)
        q, k, v = [mm(nx, w[j], 1, 0).astype(BF) for j in range(3)]
        for j, part in enumerate((q, k, v)):
            t.outs[1][j] = part
        t.put(1)
        attn = attend(q, k, v, heads)
        order = row_order(rows, groups, mp, rows // (groups * mp))
        t.outs[2][...] = mm(order, attn, 1, 0).astype(BF)

    outs = (shape((rows, dim)), shape((3, rows, width)), shape((rows, width)))
    return run(
        body, (*parts, weights), "h" + "v" * (mp - 1) + "h", outs, "hhv"
    )


def owner_rows(xg, w_to, attn, w_so, frames, per):
    own_rows, mp = xg[0].shape[0], len(xg)
    rows, (width, dim) = mp * own_rows, w_to.shape

    def body(t):
        x_buf = t.scratch[0]
        for r in range(mp):
            at = own_block(r, own_rows)
            x_buf[at, :] = t.get(r)[:, :dim]
            t.outs[1][at, :] = t.get(r)[:, dim:]
        total = x_buf[...].astype(F32)
        order = row_order(rows, mp, frames, per)
        for i in range(len(attn)):
            part = mm(order, t.get(mp + 1 + i)[...], 1, 0).astype(BF)
            total += mm(part, t.get(mp + 1 + len(attn) + i)[...], 1, 0)
        t.outs[0][...] = total
        t.outs[2][...] = mm(t.outs[1][...], t.get(mp)[...], 1, 1).astype(BF)

    outs = (shape((rows, dim), F32), shape((rows, dim)), shape((rows, width)))
    ins = (*xg, w_to, *attn, *w_so)
    where = "v" * mp + "h" + "v" * len(attn) + "h" + "v" * (len(w_so) - 1)
    return run(body, ins, where, outs, "vvv", scratch=(pltpu.VMEM((rows, dim), BF),))


SENT = ((1, 3, 5, 7), (2, 3, 6, 7))
KEPT = ((0, 2, 4, 6), (0, 1, 4, 5))
OUT_SENT, OUT_KEPT = (1, 5, 3, 7), (0, 4, 2, 6)


def chunk_of(flat, right, r, groups):
    chunk = right.shape[1] // groups
    start = pl.multiple_of(flipped(lax.axis_index("frames"), r, 3) * chunk, chunk)
    return mm(flat, right[:, pl.ds(start, chunk)], 1, 0).astype(BF)


def chunk_grads(t, first, chosen, grads, normed, other, groups):
    flat = [grad.T for grad in grads]
    right = (normed, normed, normed, other)
    for pair, relative in enumerate(chosen):
        for i, r in enumerate(relative):
            for j in range(2):
                at = 2 * pair + j
                side = slice(j * flat[at].shape[0], (j + 1) * flat[at].shape[0])
                t.outs[first + pair][i, side] = chunk_of(flat[at], right[at], r, groups)


def half_shape(width, dim, groups):
    return shape((groups // 2, 2 * width, dim // groups))


def temporal_stage(attn, so_far, g_all, up, w_so, w_qkv, clips, heads, frames, per, mp):
    n, (rows, width) = len(attn), attn[0].shape
    own_rows = rows // mp
    dim = so_far.shape[1]
    halves = frames == 8

    def rows_of(r):
        return own_block(r, own_rows)

    def body(t):
        (clip_ref,) = t.smem
        back, inv_buf = t.scratch
        total = t.get(n)[...]
        order = row_order(rows, mp, frames, per)
        for r in range(n):
            part = mm(order, t.get(r)[...], 1, 0).astype(BF)
            total += mm(part, t.get(n + 2 + r)[...], 1, 0)
        inv = inv_rms(total)
        nh = (total * inv).astype(BF)
        t.outs[2][...] = nh
        inv_buf[...] = jnp.broadcast_to(inv, inv_buf.shape)
        t.outs[3][...] = t.outs[2][rows_of(0), :]
        t.outs[4][...] = inv_buf[rows_of(0), :]

        def key_of(axis):
            dims = (rows, 1) if axis == 0 else (1, rows)
            token = lax.broadcasted_iota(jnp.int32, dims, axis)
            block = token // per
            frame = block % frames
            patch = (block // frames) * per + token % per
            end = jnp.int32(0)
            clip = jnp.zeros(dims, jnp.int32)
            for c in range(clips.shape[0]):
                end = end + clip_ref[c]
                clip += (frame >= end).astype(jnp.int32)
            return clip * rows + patch

        allowed = key_of(0) == key_of(1)
        w = t.get(2 * n + 2)
        q, k, v = [mm(nh, w[j], 1, 0).astype(BF) for j in range(3)]
        grads = attend_back(
            q, k, v, t.get(n + 1)[...], heads, lambda h: probs_of(q, k, h, allowed), True
        )
        for j in range(4):
            t.outs[5][j] = grads[j]
        d_normed = jnp.zeros((rows, dim), F32)
        for j in range(3):
            d_normed += mm(grads[j], w[j], 1, 1)
        back[...] = d_normed.astype(BF)
        for r in range(mp):
            t.outs[1 - r % 2][r // 2] = back[rows_of(r), :]
        if halves:
            chunk_grads(t, 6, SENT, grads, t.outs[2], t.get(2 * n + 3), frames)

    half = shape((mp // 2, own_rows, dim))
    outs = (
        half,
        half,
        shape((rows, dim)),
        shape((own_rows, dim)),
        shape((own_rows, 128), F32),
        shape((4, rows, width)),
    )
    if halves:
        outs += (half_shape(width, dim, frames),) * 2
    ins = (*attn, so_far, up, *w_so, w_qkv, g_all)
    return run(
        body, ins, "v" * len(ins), outs, "v" * len(outs), smem=(clips,),
        scratch=(pltpu.VMEM((rows, dim), BF), pltpu.VMEM((rows, 128), F32)),
    )


def head_sums(send, keep):
    def body(t):
        t.outs[0][...] = (t.get(0)[1].astype(F32) + t.get(1)[1].astype(F32)).astype(BF)

    came = swap(send, "mp", 1)
    (pair,) = run(body, (keep, came), "vv", (shape(keep.shape[1:]),), "v")
    return keep, came, swap(pair, "mp", 2)


def summed(t):
    return t.get(0)[0].astype(F32) + t.get(1)[0].astype(F32) + t.get(2)[...].astype(F32)


def hidden_back(parts, unit, inv, grad):
    dim = unit.shape[1]

    def body(t):
        total, nh = summed(t), t.get(3)[...].astype(F32)
        rest = total - nh * jnp.mean(total * nh, -1, keepdims=True)
        g = t.get(5)[:, dim:].astype(F32)
        t.outs[0][...] = (g + t.get(4)[:, :1] * rest).astype(BF)

    return run(body, (*parts, unit, inv, grad), "vvvvvv", (shape(unit.shape),), "v")[0]


def tokens_back(parts, x, grad):
    def body(t):
        total, xf = summed(t), t.get(3)[...].astype(F32)
        inv = inv_rms(xf)
        nx = xf * inv
        rest = total - nx * jnp.mean(total * nx, -1, keepdims=True)
        t.outs[0][...] = (t.get(4)[...].astype(F32) + inv * rest).astype(BF)

    return run(body, (*parts, x, grad), "vvvvv", (shape(x.shape),), "v")[0]


def weight_grads_half(grads, normed, other, groups, flops=1000):
    def body(t):
        left = [t.get(0)[j] for j in range(4)]
        chunk_grads(t, 0, KEPT, left, t.get(1), t.get(2), groups)

    half = half_shape(grads.shape[2], normed.shape[1], groups)
    return run(body, (grads, normed, other), "vvv", (half, half), "vv", flops=flops)


def weight_grads_whole(grads, normed, other):
    def body(t):
        for j in range(4):
            right = t.get(2) if j == 3 else t.get(1)
            t.outs[0][j] = mm(t.get(0)[j], right[...], 0, 0)

    whole = shape((4, grads.shape[2], normed.shape[1]), F32)
    return run(body, (grads, normed, other), "vhh", (whole,), "h")[0]


def spatial_probs(qkv, attn_moved, heads, groups, mp):
    rows, width = attn_moved.shape

    def body(t):
        q, k = t.get(0)[0], t.get(0)[1]
        for h in range(heads):
            t.outs[0][h] = probs_of(q, k, h, None)
        order = row_order(rows, mp, groups, rows // (groups * mp))
        t.outs[1][...] = mm(order, t.get(1)[...], 1, 0).astype(BF)

    outs = (shape((heads, rows, rows), F32), shape((rows, width)))
    return run(body, (qkv, attn_moved), "vv", outs, "vv")


def out_chunks(parts, attn, groups):
    own_rows, dim = parts[0].shape
    mp, width = len(parts), attn.shape[1]

    def body(t):
        dh = t.outs[0]
        for r in range(mp):
            dh[own_block(r, own_rows), :] = t.get(r)[...]
        if groups == 8:
            flat = t.get(mp)[...].T
            for at, relative in ((1, OUT_SENT), (2, OUT_KEPT)):
                for i, r in enumerate(relative):
                    t.outs[at][i] = chunk_of(flat, dh, r, groups)

    outs = (shape((mp * own_rows, dim)),)
    if groups == 8:
        outs += (shape((groups // 2, width, dim // groups)),) * 2
    return run(body, (*parts, attn), "v" * (mp + 1), outs, "v" * len(outs))


def qkv_parts(grads):
    flat = jnp.concatenate([grad.T for grad in grads], 0)
    first = 13 * flat.shape[0] // 24
    return flat[:first], flat[first:]


def qkv_chunks(t, first, chosen, grads, normed, groups):
    for at, (flat, relative) in enumerate(zip(qkv_parts(grads), chosen)):
        for i, r in enumerate(relative):
            t.outs[first + at][i] = chunk_of(flat, normed, r, groups)


def qkv_part_shapes(width, dim, groups):
    first = 13 * 3 * width // 24
    return tuple(
        shape((groups // 2, rows, dim // groups)) for rows in (first, 3 * width - first)
    )


def spatial_back(dh, w_so, qkv, probs, normed, heads, groups):
    rows, dim = dh.shape
    width = w_so.shape[0]

    def body(t):
        up = mm(t.get(0)[...], t.get(1)[...], 1, 1).astype(BF)
        qkv_ref = t.get(2)
        grads = attend_back(
            qkv_ref[0], qkv_ref[1], qkv_ref[2], up, heads, lambda h: t.get(3)[h], False
        )[:3]
        for j in range(3):
            t.outs[0][j] = grads[j]
        if groups == 8:
            qkv_chunks(t, 1, SENT, grads, t.get(4), groups)

    outs = (shape((3, rows, width)),)
    if groups == 8:
        outs += qkv_part_shapes(width, dim, groups)
    return run(body, (dh, w_so, qkv, probs, normed), "vvvvh", outs, "v" * len(outs))


def qkv_keeps(grads, normed, groups, flops):
    def body(t):
        qkv_chunks(t, 0, KEPT, [t.get(0)[j] for j in range(3)], t.get(1), groups)

    outs = qkv_part_shapes(grads.shape[2], normed.shape[1], groups)
    return run(body, (grads, normed), "vv", outs, "vv", flops=flops)


def normed_back(grads, w_qkv, mp):
    rows, dim = grads.shape[1], w_qkv.shape[1]
    own_rows = rows // mp

    def body(t):
        (back,) = t.scratch
        total = jnp.zeros((rows, dim), F32)
        for j in range(3):
            total += mm(t.get(0)[j], t.get(1)[j], 1, 1)
        back[...] = total.astype(BF)
        for r in range(mp):
            t.outs[1 - r % 2][r // 2] = back[own_block(r, own_rows), :]

    half = shape((mp // 2, own_rows, dim))
    return run(
        body, (grads, w_qkv), "vv", (half, half), "vv", scratch=(pltpu.VMEM((rows, dim), BF),)
    )


def halve(keeps, cames, keep_in="v", out="v", merged=False, flops=1000):
    n, depth = len(keeps), keeps[0].shape[0]
    rows = [keep.shape[1] for keep in keeps]
    chunk = keeps[0].shape[2]

    def body(t):
        for i in range(depth - 1, -1, -1):
            for at in range(n):
                total = t.get(at)[i].astype(F32) + t.get(n + at)[i].astype(F32)
                kept, first = 1 - i % 2, sum(rows[:at])
                if merged:
                    t.outs[kept][first : first + rows[at]] = total.astype(BF)
                else:
                    t.outs[n * kept + at][i // 2] = total.astype(BF)

    if merged:
        outs = (shape((sum(rows), chunk)),) * 2
    else:
        outs = tuple(shape((depth // 2, r, chunk)) for r in rows) * 2
    where = keep_in * n + "v" * n
    return run(body, (*keeps, *cames), where, outs, out * len(outs), flops=flops)


def last_sums(pairs, flops=1000):
    chunk = pairs[0][0].shape[-1]
    pairs = [tuple(part.reshape(-1, chunk) for part in pair) for pair in pairs]
    width = sum(pair[0].shape[0] for pair in pairs) // 4

    def body(t):
        row = 0
        for at, (keep, _) in enumerate(pairs):
            start = 0
            while start < keep.shape[0]:
                size = min(width - row % width, keep.shape[0] - start)
                here = slice(start, start + size)
                total = t.get(2 * at)[here].astype(F32) + t.get(2 * at + 1)[here].astype(F32)
                side = slice(row % width, row % width + size)
                if row < 3 * width:
                    t.outs[0][row // width, :, side] = total.T
                else:
                    t.outs[1][side, :] = total
                start, row = start + size, row + size

    ins = [part for pair in pairs for part in pair]
    outs = (shape((3, chunk, width), F32), shape((width, chunk), F32))
    return run(body, ins, "v" * len(ins), outs, "hh", flops=flops)


def reduce_whole(flat, normed, other):
    whole = weight_grads_whole(flat, normed, other)
    mine = lax.psum_scatter(whole, "frames", scatter_dimension=2, tiled=True)
    return jnp.swapaxes(mine[:3], 1, 2), mine[3]


def shards(
    video_tokens, grad_output, spatial_qkv, spatial_out, temporal_qkv, temporal_out, clip_frames
):
    frames_dev, rows_mp, dim = video_tokens.shape
    width = spatial_out.shape[0]
    heads = width // HD
    groups = lax.axis_size("frames")
    mp = lax.axis_size("mp")
    patches = rows_mp * mp
    per = rows_mp // groups
    assert frames_dev == 1 and rows_mp % groups == 0 and mp == 4

    halves = groups == 8
    x_own, g_own = video_tokens[0], grad_output[0]
    x_one, x_two = swap(x_own, "mp", 1), swap(x_own, "mp", 2)
    xg, x_one, x_two, so_own = lax.optimization_barrier(
        (joined(x_own, g_own), x_one, x_two, spatial_out)
    )
    x_three = swap(x_two, "mp", 1)
    xg = lax.all_to_all(xg.reshape(groups, per, 2 * dim), "frames", 0, 0, tiled=True)
    xg = xg.reshape(rows_mp, 2 * dim)
    so_two = swap(so_own, "mp", 2)

    normed_x, qkv_s, attn_send = spatial_forward(
        (x_own, x_one, x_two, x_three), spatial_qkv, heads, groups
    )
    attn_send, xg = lax.optimization_barrier((attn_send, xg))
    xg_two = swap(xg, "mp", 2)
    moved = lax.all_to_all(
        attn_send.reshape(groups, mp * per, width), "frames", 0, 0, tiled=True
    ).reshape(patches, width)
    so_two, moved = lax.optimization_barrier((so_two, moved))
    moved_one, moved_two = swap(moved, "mp", 1), swap(moved, "mp", 2)
    so_one = swap(spatial_out, "mp", 1)
    xg_all = xg, swap(xg, "mp", 1), xg_two, swap(xg_two, "mp", 1)
    rows_own = owner_rows(
        xg_all, temporal_out, (moved, moved_one), (spatial_out, so_one), groups, per
    )
    moved_two, rows_own = lax.optimization_barrier((moved_two, rows_own))
    so_far, g_rows, d_attn_t = rows_own

    send_h, keep_h, normed_h, unit_own, inv_own, t_grads, *t_sent = temporal_stage(
        (moved_two, swap(moved_two, "mp", 1)), so_far, g_rows, d_attn_t,
        (so_two, swap(so_two, "mp", 1)), temporal_qkv, clip_frames, heads, groups, per, mp,
    )
    parts = head_sums(send_h, keep_h)
    if halves:
        t_kept = weight_grads_half(t_grads, normed_h, g_rows, groups)
        parts, t_kept = lax.optimization_barrier((parts, t_kept))
        came = [swap(t_sent[0], "frames", 1), swap(t_sent[1], "frames", 2)]
        t_sums = halve(t_kept, came, out="h")
    d_hidden = hidden_back(parts, unit_own, inv_own, xg)
    d_hidden = lax.all_to_all(
        d_hidden.reshape(groups, per, dim), "frames", 0, 0, tiled=True
    ).reshape(rows_mp, dim)
    if halves:
        d_hidden, t_sums = lax.optimization_barrier((d_hidden, t_sums))
        t_second = [swap(t_sums[0], "frames", 2), swap(t_sums[1], "frames", 1)]
    dh_one, dh_two = swap(d_hidden, "mp", 1), swap(d_hidden, "mp", 2)
    d_hidden, qkv_s, attn_send = lax.optimization_barrier((d_hidden, qkv_s, attn_send))
    probs_s, attn_s = spatial_probs(qkv_s, attn_send, heads, groups, mp)
    dh_two, probs_s, attn_s = lax.optimization_barrier((dh_two, probs_s, attn_s))
    dh_three = swap(dh_two, "mp", 1)
    d_hidden_all, *o_chunks = out_chunks((d_hidden, dh_one, dh_two, dh_three), attn_s, groups)
    dh_ready = d_hidden_all
    if halves:
        dh_ready, t_second = lax.optimization_barrier((dh_ready, t_second))
        t_send, t_keep = halve(t_sums[2:], t_second, keep_in="h", merged=True)
        dh_ready, t_send, t_keep = lax.optimization_barrier((dh_ready, t_send, t_keep))
        t_came = swap(t_send, "frames", 4)
    else:
        t_qkv, t_out = reduce_whole(t_grads, normed_h, g_rows)
    s_grads, *s_sent = spatial_back(
        dh_ready, spatial_out, qkv_s, probs_s, normed_x, heads, groups
    )
    if halves:
        after = lax.optimization_barrier
        send_x, keep_x = normed_back(s_grads, spatial_qkv, mp)
        o_send, o_keep = halve([o_chunks[1]], [swap(o_chunks[0], "frames", 1)])
        s_grads, send_x, keep_x, t_came, o_send, o_keep = after(
            (s_grads, send_x, keep_x, t_came, o_send, o_keep)
        )
        o_came = swap(o_send, "frames", 4)
        s_kept = qkv_keeps(s_grads, normed_x, groups, 50_000_000_000)
        came_a, came_b = swap(s_sent[0], "frames", 1), swap(s_sent[1], "frames", 2)
        send_a, keep_a = halve([s_kept[0]], [came_a])
        send_a, keep_a, t_keep = after((send_a, keep_a, t_keep))
        t_qkv, t_out = last_sums([(t_keep, t_came)], 50_000_000_000)
        came_b, t_qkv, t_out = after((came_b, t_qkv, t_out))
        send_b, keep_b = halve([s_kept[1]], [came_b])
        came = [swap(send_a, "frames", 2), swap(send_b, "frames", 1)]
        o_send, o_keep = halve([o_keep], [o_came], flops=50_000_000_000)
        came, o_send, o_keep = after((came, o_send, o_keep))
        s_send, s_keep = halve([keep_a, keep_b], came, merged=True)
        s_qkv, s_out = last_sums([
            (s_keep, swap(s_send, "frames", 4)), (o_keep, swap(o_send, "frames", 2))
        ])
    else:
        send_x, keep_x = normed_back(s_grads, spatial_qkv, mp)
        all_grads = jnp.concatenate([s_grads, attn_s[None]], 0)
        s_qkv, s_out = reduce_whole(all_grads, normed_x, d_hidden_all)
    grad_tokens = tokens_back(head_sums(send_x, keep_x), x_own, d_hidden)
    return grad_tokens[None], s_qkv, s_out, t_qkv, t_out


def solution(mesh):
    placed = (
        P("frames", "mp", None),
        P("frames", "mp", None),
        P(None, None, "mp"),
        P("mp", None),
        P(None, None, "mp"),
        P("mp", None),
        P(),
    )
    return jax.shard_map(
        shards,
        mesh=mesh,
        in_specs=placed,
        out_specs=(
            P("frames", "mp", None),
            P(None, "frames", "mp"),
            P("mp", "frames"),
            P(None, "frames", "mp"),
            P("mp", "frames"),
        ),
        check_vma=False,
    )
```
